32 devices in a mesh: dp: 8 (over y, x, core), band: 4 (over z).
Axes of the slice: x: 2, y: 2, z: 4, core: 2. Of those that a mesh axis runs over, the one named last changes fastest.
Arguments:
- tokens: bfloat16 [24, 580, 768], P('dp', 'band'), may hold values from -6 to 6
- cotangent: bfloat16 [24, 580, 768], P('dp', 'band'), may hold values from -6 to 6
- lengths: int32 [24], P('dp'), may hold values from 257 to 577, as said below
- slot_of_block: int32 [864], replicated, may hold values from 0 to 863, as said below
- master: float32 [864, 128, 128], P('dp')
- statistics: float32 [864, 2, 128, 128], P('dp')
- inverse_roots: float32 [864, 2, 128, 128], P('dp')
- gain_values: float32 [4, 768], replicated, may hold values from 0.5 to 1.5
- gain_moments: float32 [4, 768], replicated, may hold values from 7.0627216e-08 to 1.1300355e-06
Outputs:
- layer_output: bfloat16 [24, 580, 768], P('dp', 'band')
- input_grad: bfloat16 [24, 580, 768], P('dp', 'band')
- weight_grads: float32 [864, 128, 128], P('dp')
- grad_norm: float32 [], replicated
- new_statistics: float32 [864, 2, 128, 128], P('dp')
- new_master: float32 [864, 128, 128], P('dp')
- master_copy: bfloat16 [864, 128, 128], P('dp')
- gain_grads: float32 [4, 768], replicated
- new_moments: float32 [4, 768], replicated
- new_gains: float32 [4, 768], replicated
The draws below stay inside these ranges and needn't reach their ends.
Inputs may be any that keep to these rules, and one draw needn't show every extreme that they name: `lengths`: each image holds 257 or 577 tokens; each aligned run of 3 images holds one of 577 or more. `slot_of_block`: distinct slots; slots 0 and 863 are always used.
All inputs are finite; a program needn't handle non-finite values.
Results may differ from the reference program's by a relative error of at most 0.02.
Values may be sent and summed in bfloat16 or wider, within the bound.
No kernel may reach another device: no remote copies, remote signals or barrier semaphores. Data moves between devices by JAX's collectives and lax.ppermute only.
A program may use at most 384 MiB of HBM per device.

```python
import math
import jax
import jax.numpy as jnp
from jax import lax

D = 768
HEADS = 12
HEAD_DIM = 64
FF = 2048
LAYERS = 2
IMG_DEV = 3
SEQ = 580
SHORT = 257
LONG = 577
BLOCK = 128
IMAGES = 24
BLOCKS = 864
SLOTS_ALL = 864
PARAMS = 14158848


def slot_table(key):
    first_key, second_key = jax.random.split(jax.random.fold_in(key, 11))
    middle_ids = jax.random.permutation(first_key, jnp.arange(1, SLOTS_ALL - 1, dtype=jnp.int32))
    end_slots = jnp.array([0, SLOTS_ALL - 1], dtype=jnp.int32)
    chosen_ids = jnp.concatenate([end_slots, middle_ids])[:BLOCKS]
    return chosen_ids[jax.random.permutation(second_key, BLOCKS)]


def build_tiles(diag_key, off_tiles, low_end, high_end, magnitude):
    diagonal = jnp.exp(jax.random.uniform(diag_key, (SLOTS_ALL, 2, BLOCK), minval=math.log(low_end), maxval=math.log(high_end)))
    mirrored = (off_tiles + jnp.swapaxes(off_tiles, 2, 3)) * (0.8 / math.sqrt(2.0 * BLOCK))
    identity_mask = jnp.eye(BLOCK, dtype=jnp.float32)
    return magnitude * (diagonal[..., None] * identity_mask + mirrored * (1.0 - identity_mask))


def draw_lengths(key, part):
    key = jax.random.fold_in(key, 1)
    coin_key, pick_key = jax.random.split(key)
    coin_flips = jax.random.randint(coin_key, (IMAGES,), 0, 2)
    chosen_rows = jax.random.randint(pick_key, (IMAGES // IMG_DEV,), 0, IMG_DEV)
    forced = jnp.arange(IMAGES // IMG_DEV) * IMG_DEV + chosen_rows
    coin_flips = coin_flips.at[forced].set(1)
    return jnp.where(coin_flips == 1, LONG, SHORT).astype(jnp.int32)


def draw_slot_of_block(key, part):
    return slot_table(key)


def draw_master(key, part):
    slot_ids = slot_table(key)
    key = jax.random.fold_in(key, 2)
    owner_block = jnp.zeros((SLOTS_ALL,), jnp.int32).at[slot_ids].set(jnp.arange(BLOCKS, dtype=jnp.int32))
    per_layer = BLOCKS // LAYERS
    within = owner_block % per_layer
    qkv_count = D // BLOCK * (3 * D // BLOCK)
    out_count = D // BLOCK * (D // BLOCK)
    gate_count = D // BLOCK * (2 * FF // BLOCK)
    tile_scale = jnp.where(within < qkv_count, D ** (-0.5), jnp.where(within < qkv_count + out_count, 4.0 * D ** (-0.5), jnp.where(within < qkv_count + out_count + gate_count, D ** (-0.5), FF ** (-0.5))))
    random_tiles = jax.random.normal(key, (SLOTS_ALL, BLOCK, BLOCK))
    return random_tiles * tile_scale[:, None, None]


def draw_statistics(key, part):
    key = jax.random.fold_in(key, 3)
    diag_key, off_key = jax.random.split(key)
    off_tiles = jax.random.truncated_normal(off_key, -4.0, 4.0, (SLOTS_ALL, 2, BLOCK, BLOCK))
    return build_tiles(diag_key, off_tiles, 1.0, 4.0, BLOCK / PARAMS)


def draw_inverse_roots(key, part):
    key = jax.random.fold_in(key, 4)
    diag_key, off_key = jax.random.split(key)
    off_tiles = jax.random.truncated_normal(off_key, -4.0, 4.0, (SLOTS_ALL, 2, BLOCK, BLOCK))
    return build_tiles(diag_key, off_tiles, 0.7, 1.4, (BLOCK / PARAMS) ** (-0.25))


def levels(rng, extent, shards, smallest, high):
    level = 1.0
    for dim, shards_of in shards:
        heights = jax.random.uniform(jax.random.fold_in(jax.random.fold_in(rng, 6), dim), (shards_of,), jnp.float32, smallest / len(shards), high / len(shards))
        level = level * jnp.repeat(jnp.exp(heights), extent[dim] // shards_of).reshape((-1,) + (1,) * (len(extent) - 1 - dim))
    return level


def normal_values(rng, shape, spread, most, cuts=(), kind=jnp.bfloat16):
    values = jax.random.normal(rng, shape, jnp.float32) * spread
    if len(cuts) > 0:
        values = levels(rng, shape, cuts, -0.22, 0.18) * values
    return jnp.clip(values, min=-most, max=most).astype(kind)


def setup_inputs(seed: int = 0) -> dict:
    splits = jax.random.split(jax.random.key(seed), 10)
    return {
        "tokens": normal_values(splits[0], (IMAGES, SEQ, D), 1.0, 6.0, ((0, 8), (1, 4))),
        "cotangent": normal_values(splits[1], (IMAGES, SEQ, D), 1.0, 6.0, ((0, 8), (1, 4))),
        "lengths": draw_lengths(jax.random.fold_in(splits[9], 71), 0),
        "slot_of_block": draw_slot_of_block(jax.random.fold_in(splits[9], 71), 0),
        "master": draw_master(jax.random.fold_in(splits[9], 71), 0),
        "statistics": draw_statistics(jax.random.fold_in(splits[9], 71), 0),
        "inverse_roots": draw_inverse_roots(jax.random.fold_in(splits[9], 71), 0),
        "gain_values": jnp.clip(1.0 + 0.1 * jax.random.normal(splits[7], (2 * LAYERS, D), jnp.float32), 0.5, 1.5),
        "gain_moments": jnp.clip(jnp.exp(jax.random.uniform(splits[8], (2 * LAYERS, D), jnp.float32, math.log(7.062721607553613e-08), math.log(1.130035457208578e-06))), 7.062721607553613e-08, 1.130035457208578e-06),
    }


epsilon = 1e-05
rope_base = 10000.0
decay_rate = 0.5
step_rate = 0.4
gain_rate = 0.2
clip_limit = 1.0
masked_score = -1e+30
highest = lax.Precision.HIGHEST

@jax.custom_vjp
def low(v):
    return lax.optimization_barrier(v.astype(jnp.bfloat16)).astype(jnp.float32)

@jax.custom_vjp
def low_back(v):
    return v

def low_keep(v):
    return (low(v), None)

def low_pass(kept, grad):
    return (grad,)

def back_keep(v):
    return (v, None)

def back_low(kept, grad):
    return (low(grad),)
low.defvjp(low_keep, low_pass)
low_back.defvjp(back_keep, back_low)

def matrix_shapes():
    return [(D, 3 * D), (D, D), (D, 2 * FF), (FF, D)]

def assemble(blocks):
    layers_out = []
    offset = 0
    for layer_index in range(LAYERS):
        matrices = []
        for rows_all, cols_all in matrix_shapes():
            block_count = rows_all // BLOCK * (cols_all // BLOCK)
            block_view = blocks[offset:offset + block_count].reshape(rows_all // BLOCK, cols_all // BLOCK, BLOCK, BLOCK)
            matrices.append(block_view.transpose(0, 2, 1, 3).reshape(rows_all, cols_all))
            offset = offset + block_count
        layers_out.append(matrices)
    return layers_out

def disassemble(layers_in):
    tiled_parts = []
    for matrices in layers_in:
        for matrix in matrices:
            rows_all, cols_all = matrix.shape
            tiled = matrix.reshape(rows_all // BLOCK, BLOCK, cols_all // BLOCK, BLOCK).transpose(0, 2, 1, 3)
            tiled_parts.append(tiled.reshape(-1, BLOCK, BLOCK))
    return jnp.concatenate(tiled_parts, 0)

def rope_tables(positions):
    half_dim = HEAD_DIM // 2
    frequency = rope_base ** (-(jnp.arange(half_dim, dtype=jnp.float32) * 2.0 / HEAD_DIM))
    angles = positions.astype(jnp.float32)[:, None] * frequency[None, :]
    return (jnp.cos(angles), jnp.sin(angles))

def rotate(values, cosine_table, sine_table):
    half_dim = HEAD_DIM // 2
    first_half = values[..., :half_dim]
    second_half = values[..., half_dim:]
    cosine = cosine_table[:, None, :]
    sine_part = sine_table[:, None, :]
    return jnp.concatenate([first_half * cosine - second_half * sine_part, second_half * cosine + first_half * sine_part], -1)

def rms_scale(hidden, gain):
    return hidden * lax.rsqrt(lax.optimization_barrier(jnp.mean(hidden * hidden, -1, keepdims=True)) + epsilon) * gain

def gated(gate_up):
    return jax.nn.silu(gate_up[..., :FF]) * gate_up[..., FF:]

def shampoo_stats(statistics, grad_tiles):
    left_new = jnp.einsum('sij,skj->sik', grad_tiles, grad_tiles, precision=highest)
    right_new = jnp.einsum('sji,sjk->sik', grad_tiles, grad_tiles, precision=highest)
    return decay_rate * statistics + (1.0 - decay_rate) * jnp.stack([left_new, right_new], 1)

def precondition(root_pair, grad_tiles):
    left_applied = jnp.einsum('sij,sjk->sik', root_pair[:, 0], grad_tiles, precision=highest)
    return jnp.einsum('sij,sjk->sik', left_applied, root_pair[:, 1], precision=highest)

def attend(queries, key_rows, value_rows, query_pos, lengths_in):
    scores = low_back(jnp.einsum('gqhe,gkhe->ghqk', queries, key_rows, precision=highest) * HEAD_DIM ** (-0.5))
    key_pos = jnp.arange(key_rows.shape[1])
    allowed = (key_pos[None, None, None, :] <= query_pos[None, None, :, None]) & (key_pos[None, None, None, :] < lengths_in[:, None, None, None])
    scores = jnp.where(allowed, scores, masked_score)
    row_top = lax.optimization_barrier(jnp.max(scores, -1, keepdims=True))
    exp_scores = jnp.where(allowed, jnp.exp(scores - row_top), 0.0)
    probabilities = low(exp_scores / lax.optimization_barrier(jnp.sum(exp_scores, -1, keepdims=True)))
    return jnp.einsum('ghqk,gkhe->gqhe', probabilities, value_rows, precision=highest)

def layer(hidden, weights, gain_pair, lengths_in, cosine_table, sine_table):
    w_qkv, w_out, w_gate_up, w_down = weights
    groups, seq_len, model_width = hidden.shape
    normed = low(rms_scale(hidden, gain_pair[0]))
    projected = low_back(jnp.einsum('gsd,de->gse', normed, w_qkv, precision=highest))
    shaped = projected.reshape(groups, seq_len, 3, HEADS, HEAD_DIM)
    queries = low(rotate(shaped[:, :, 0], cosine_table, sine_table))
    key_rows = low(rotate(shaped[:, :, 1], cosine_table, sine_table))
    value_rows = low(shaped[:, :, 2])
    mixed_heads = attend(queries, key_rows, value_rows, jnp.arange(seq_len), lengths_in)
    mixed_heads = low(low_back(mixed_heads)).reshape(groups, seq_len, model_width)
    hidden = hidden + low_back(jnp.einsum('gsd,de->gse', mixed_heads, w_out, precision=highest))
    normed_two = low(rms_scale(hidden, gain_pair[1]))
    gate_up = low_back(jnp.einsum('gsd,de->gse', normed_two, w_gate_up, precision=highest))
    activated = low(gated(gate_up))
    return hidden + low_back(jnp.einsum('gsf,fd->gsd', activated, w_down, precision=highest))

def reference(tokens, cotangent, lengths, slot_of_block, master, statistics, inverse_roots, gain_values, gain_moments):
    weights = assemble(low(master[slot_of_block]))
    cosine_table, sine_table = rope_tables(jnp.arange(SEQ))
    group_count = IMAGES // IMG_DEV
    token_groups = tokens.reshape(group_count, IMG_DEV, SEQ, D)
    back_groups = cotangent.reshape(group_count, IMG_DEV, SEQ, D)
    length_groups = lengths.reshape(group_count, IMG_DEV)

    def group_step(totals, group_data):
        group_tokens, group_back, group_lengths = group_data

        def local_forward(weights_in, gains_in, hidden):
            for layer_index in range(LAYERS):
                hidden = layer(hidden, weights_in[layer_index], gains_in[2 * layer_index:2 * layer_index + 2], group_lengths, cosine_table, sine_table)
            return hidden
        outputs, pullback = jax.vjp(local_forward, weights, gain_values, group_tokens.astype(jnp.float32))
        valid = (jnp.arange(SEQ)[None, :] < group_lengths[:, None]).astype(jnp.float32)
        weight_back, gain_back, input_back = pullback(group_back.astype(jnp.float32) * valid[:, :, None])
        totals = jax.tree.map(jnp.add, totals, (weight_back, gain_back))
        return (totals, (outputs.astype(jnp.bfloat16), input_back.astype(jnp.bfloat16)))
    zero_tree = jax.tree.map(jnp.zeros_like, (weights, gain_values))
    (weight_grad, gain_raw), (layer_rows, input_rows) = lax.scan(group_step, zero_tree, (token_groups, back_groups, length_groups))
    tile_grads = disassemble(weight_grad)
    squares = jnp.sum(tile_grads * tile_grads) + jnp.sum(gain_raw * gain_raw)
    grad_norm = jnp.sqrt(squares)
    factor = jnp.minimum(1.0, clip_limit / grad_norm)
    weight_grads = jnp.zeros((SLOTS_ALL, BLOCK, BLOCK), jnp.float32).at[slot_of_block].set(tile_grads * factor)
    new_statistics = shampoo_stats(statistics, weight_grads)
    new_master = master - step_rate * precondition(inverse_roots, weight_grads)
    gain_grads = gain_raw * factor
    new_moments = decay_rate * gain_moments + (1.0 - decay_rate) * gain_grads * gain_grads
    new_gains = gain_values - gain_rate * gain_grads / (jnp.sqrt(new_moments) + epsilon)
    return (layer_rows.reshape(IMAGES, SEQ, D), input_rows.reshape(IMAGES, SEQ, D), weight_grads, grad_norm, new_statistics, new_master, new_master.astype(jnp.bfloat16), gain_grads, new_moments, new_gains)
```

```python
import functools

import jax
import jax.numpy as jnp
from jax import lax
from jax.experimental import pallas as pl
from jax.experimental.pallas import tpu as pltpu
from jax.sharding import PartitionSpec as P

D = 768
HEADS = 12
HEAD_DIM = 64
FF = 2048
LAYERS = 2
BLOCK = 128
PAIR = 2 * HEAD_DIM

epsilon = 1e-05
rope_base = 10000.0
decay_rate = 0.5
step_rate = 0.4
gain_rate = 0.2
clip_limit = 1.0
masked_score = -1e30
VMEM_BYTES = 62 * 2**20

f32 = jnp.float32
bf16 = jnp.bfloat16

GRIDS = [
    (D // BLOCK, 3 * D // BLOCK),
    (D // BLOCK, D // BLOCK),
    (D // BLOCK, 2 * FF // BLOCK),
    (FF // BLOCK, D // BLOCK),
]
COUNTS = [r * c for r, c in GRIDS]
OFFSETS = [sum(COUNTS[:i]) for i in range(4)]
PER_LAYER = sum(COUNTS)
FF_STEP = 512


def round_up(n, m):
    return -(-n // m) * m


def nn(a, b):
    return lax.dot_general(a, b, (((1,), (0,)), ((), ())), preferred_element_type=f32)


def nt(a, b):
    return lax.dot_general(a, b, (((1,), (1,)), ((), ())), preferred_element_type=f32)


def tn(a, b):
    return lax.dot_general(a, b, (((0,), (0,)), ((), ())), preferred_element_type=f32)


def query_blocks(rows, step=256):
    return [(s, min(s + step, rows)) for s in range(0, rows, step)]


def swap_halves(t):
    lane = lax.broadcasted_iota(jnp.int32, t.shape, 1)
    half = HEAD_DIM // 2
    return jnp.where(lane % HEAD_DIM < half, pltpu.roll(t, PAIR - half, 1), pltpu.roll(t, half, 1))


def rms(m):
    return lax.rsqrt(jnp.mean(m * m, -1, keepdims=True) + epsilon)


def rms_back(u, m, g):
    r = rms(m)
    t = u * g
    dot = jnp.mean(t * m, -1, keepdims=True)
    return r * t - m * (r * r * r * dot), jnp.sum(u * m * r, 0, keepdims=True)


def forward_kernel(
    slots, length, x_ref, g_ref, cos_ref, sin_ref, w_hbm,
    xn_ref, normed_ref, q_ref, k_ref, v_ref, st_ref, mixed_ref, mid_ref, n2_ref, gu_ref,
    wqkv_o, wout_o, wgu_o, wd_o,
    wqkv, wout, wgu, wd, bias, sem_in, sem_out,
):
    rows = x_ref.shape[0]
    key_rows = q_ref.shape[0]
    held = (wqkv, wout, wgu, wd)
    for m in range(4):
        tile_rows, tile_cols = GRIDS[m]

        @pl.loop(0, tile_rows)
        def _(i, m=m, tile_cols=tile_cols):
            for j in range(tile_cols):
                slot = slots[OFFSETS[m] + i * tile_cols + j]
                pltpu.make_async_copy(
                    w_hbm.at[slot],
                    held[m].at[pl.ds(pl.multiple_of(i * BLOCK, BLOCK), BLOCK), pl.ds(j * BLOCK, BLOCK)],
                    sem_in.at[m],
                ).start()

    def arrive(m):
        pltpu.make_async_copy(held[m], held[m], sem_in.at[m]).wait()

    outs = (wqkv_o, wout_o, wgu_o, wd_o)

    def leave(m):
        return pltpu.make_async_copy(held[m], outs[m], sem_out.at[m])

    query = lax.broadcasted_iota(jnp.int32, bias.shape, 0)
    key = lax.broadcasted_iota(jnp.int32, bias.shape, 1)
    bias[...] = jnp.where((key <= query) & (key < length[0]), 0.0, masked_score)
    x = x_ref[...]
    normed_ref[...] = (x * rms(x) * g_ref[0:1, :]).astype(bf16)
    tail = key_rows - rows
    for ref in (q_ref, k_ref, v_ref):
        ref[rows:, :] = jnp.zeros((tail, D), bf16)
    arrive(0)
    leave(0).start()

    @pl.loop(0, 2)
    def _(part):
        acc = nn(normed_ref[...], wqkv[:, pl.ds(pl.multiple_of(part * D, D), D)])
        scale = jnp.where(part == 0, HEAD_DIM ** (-0.5), 1.0)
        for p in range(HEADS // 2):
            t = acc[:, p * PAIR : (p + 1) * PAIR]
            rot = ((t * cos_ref[...] + swap_halves(t) * sin_ref[...]) * scale).astype(bf16)

            @pl.when(part == 0)
            def _(p=p, rot=rot):
                q_ref[0:rows, p * PAIR : (p + 1) * PAIR] = rot

            @pl.when(part == 1)
            def _(p=p, rot=rot):
                k_ref[0:rows, p * PAIR : (p + 1) * PAIR] = rot

    v_ref[0:rows, :] = nn(normed_ref[...], wqkv[:, 2 * D :]).astype(bf16)
    st_ref[...] = jnp.zeros(st_ref.shape, f32)

    @pl.loop(0, HEADS // 2)
    def _(p):
        cols = pl.ds(pl.multiple_of(p * PAIR, PAIR), PAIR)
        kp = k_ref[:, cols]
        vp = v_ref[:, cols]
        low = lax.broadcasted_iota(jnp.int32, kp.shape, 1) < HEAD_DIM
        keys = (jnp.where(low, kp, 0), jnp.where(low, 0, kp))
        values = (jnp.where(low, vp, 1), jnp.where(low, 1, vp))
        for q0, q1 in query_blocks(rows):
            kend = min(round_up(q1, BLOCK), key_rows)
            qp = q_ref[q0:q1, cols]
            mask = bias[q0:q1, :kend]
            parts = []
            tops = []
            for h in range(2):
                s = nt(qp, keys[h][:kend]) + mask
                top = jnp.max(s, -1, keepdims=True)
                e = jnp.exp(s - top).astype(bf16)
                parts.append(nn(e, values[h][:kend]))
                tops.append(top)
            lane = lax.broadcasted_iota(jnp.int32, parts[0].shape, 1)
            low_q = lane < HEAD_DIM
            total = pltpu.roll(jnp.where(low_q, parts[1], parts[0]), HEAD_DIM, 1)
            mixed_ref[q0:q1, cols] = (jnp.where(low_q, parts[0], parts[1]) / total).astype(bf16)
            log_total = jnp.log(total)
            other = pltpu.roll(log_total, HEAD_DIM, 1)
            first = tops[0] + jnp.where(low_q, log_total, other)
            second = tops[1] + jnp.where(low_q, other, log_total)
            old = st_ref[q0:q1, :]
            st_ref[q0:q1, :] = jnp.where(
                lane == 2 * p, first, jnp.where(lane == 2 * p + 1, second, old)
            )

    arrive(1)
    leave(1).start()
    middle = x_ref[...] + nn(mixed_ref[...], wout[...])
    mid_ref[...] = middle
    n2_ref[...] = (middle * rms(middle) * g_ref[1:2, :]).astype(bf16)
    arrive(2)
    leave(2).start()
    arrive(3)
    leave(3).start()
    xn_ref[...] = mid_ref[...]

    @pl.loop(0, FF // FF_STEP)
    def _(t):
        at = pl.multiple_of(t * FF_STEP, FF_STEP)
        gate = nn(n2_ref[...], wgu[:, pl.ds(at, FF_STEP)])
        up = nn(n2_ref[...], wgu[:, pl.ds(FF + at, FF_STEP)])
        act = (gate / (1.0 + jnp.exp(-gate)) * up).astype(bf16)
        gu_ref[:, pl.ds(at, FF_STEP)] = gate.astype(bf16)
        gu_ref[:, pl.ds(FF + at, FF_STEP)] = up.astype(bf16)
        xn_ref[...] += nn(act, wd[pl.ds(at, FF_STEP), :])

    for m in range(4):
        leave(m).wait()


def backward_kernel(
    slots, spare, length, back_ref, g_ref, cos_ref, sin_ref,
    x_ref, normed_ref, q_ref, k_ref, v_ref, st_ref, mixed_ref, mid_ref, n2_ref, gu_ref,
    wqkv_i, wout_i, wgu_i, wd_i, *rest,
):
    (
        dx_ref, gain_ref, tiles_out,
        wqkv, wout, wgu, wd, gqkv, gout, ggu, gd, zero, bias, turned, sums, big, mixed_back, dproj,
        sem_in, sem_out, sem_zero,
    ) = rest[-21:]
    rows = x_ref.shape[0]
    key_rows = q_ref.shape[0]
    held = (wqkv, wout, wgu, wd)
    given = (wqkv_i, wout_i, wgu_i, wd_i)

    def arrive(m):
        return pltpu.make_async_copy(given[m], held[m], sem_in.at[m])

    for m in (3, 2, 1, 0):
        arrive(m).start()
    grads = (gqkv, gout, ggu, gd)

    def send(m, i0, i1, j0, count_j):
        @pl.loop(i0, i1)
        def _(i):
            for jj in range(count_j):
                j = j0 + jj
                slot = slots[OFFSETS[m] + i * GRIDS[m][1] + j]
                pltpu.make_async_copy(
                    grads[m].at[
                        pl.ds(pl.multiple_of(i * BLOCK, BLOCK), BLOCK),
                        pl.ds(pl.multiple_of(j * BLOCK, BLOCK), BLOCK),
                    ],
                    tiles_out.at[slot],
                    sem_out.at[m],
                ).start()

    spares = spare.shape[0] - 1
    if spares > 0:
        zero[...] = jnp.zeros(zero.shape, bf16)

        @pl.loop(0, spares)
        def _(i):
            pltpu.make_async_copy(zero, tiles_out.at[spare[i]], sem_zero).start()

    key = lax.broadcasted_iota(jnp.int32, bias.shape, 0)
    query = lax.broadcasted_iota(jnp.int32, bias.shape, 1)
    bias[...] = jnp.where((key <= query) & (key < length[0]), 0.0, masked_score)
    levels = st_ref[...].T
    for h in range(HEADS):
        turned[h] = levels[h : h + 1, :]
    big[...] = jnp.zeros(big.shape, f32)
    back_b = back_ref[...].astype(bf16)
    arrive(3).wait()
    arrive(2).wait()

    @pl.loop(0, FF // FF_STEP)
    def _(t):
        at = pl.multiple_of(t * FF_STEP, FF_STEP)
        here = pl.ds(at, FF_STEP)
        there = pl.ds(FF + at, FF_STEP)
        back_ffn = back_ref[...].astype(bf16)
        d_act = nt(back_ffn, wd[here, :])
        gate = gu_ref[:, here].astype(f32)
        up = gu_ref[:, there].astype(f32)
        sig = 1.0 / (1.0 + jnp.exp(-gate))
        silu = gate * sig
        act = (silu * up).astype(bf16)
        d_gate = (d_act * up * (sig * (1.0 + gate * (1.0 - sig)))).astype(bf16)
        d_up = (d_act * silu).astype(bf16)
        gd[here, :] = tn(act, back_ffn).astype(bf16)
        ggu[:, here] = tn(n2_ref[...], d_gate).astype(bf16)
        ggu[:, there] = tn(n2_ref[...], d_up).astype(bf16)
        per = FF_STEP // BLOCK
        send(3, t * per, (t + 1) * per, 0, D // BLOCK)
        send(2, 0, D // BLOCK, t * per, per)
        send(2, 0, D // BLOCK, FF // BLOCK + t * per, per)
        big[...] += nt(d_gate, wgu[:, here]) + nt(d_up, wgu[:, there])

    step, gain_two = rms_back(big[...], mid_ref[...], g_ref[1:2, :])
    gain_ref[1:2, :] = gain_two
    dx_ref[...] = back_ref[...] + step
    arrive(1).wait()
    back_attn = dx_ref[...].astype(bf16)
    gout[...] = tn(mixed_ref[...], back_attn).astype(bf16)
    send(1, 0, D // BLOCK, 0, D // BLOCK)
    mixed_back[0:rows, :] = nt(back_attn, wout[...]).astype(bf16)
    mixed_back[rows:, :] = jnp.zeros((key_rows - rows, D), bf16)

    @pl.loop(0, HEADS // 2)
    def _(p):
        cols = pl.ds(pl.multiple_of(p * PAIR, PAIR), PAIR)
        low = lax.broadcasted_iota(jnp.int32, (key_rows, PAIR), 1) < HEAD_DIM

        def both(t):
            return (jnp.where(low, t, 0), jnp.where(low, 0, t))

        qp = q_ref[:, cols]
        op = mixed_back[:, cols]
        keys, values, queries, backs = both(k_ref[:, cols]), both(v_ref[:, cols]), both(qp), both(op)
        sums[...] = jnp.zeros(sums.shape, f32)
        for q0, q1 in query_blocks(key_rows):
            kend = q1
            d_query = jnp.zeros((q1 - q0, PAIR), f32)
            d_key = jnp.zeros((kend, PAIR), f32)
            d_value = jnp.zeros((kend, PAIR), f32)
            for h in range(2):
                level = turned[2 * p + h, :, q0:q1]
                soft = jnp.exp(nt(keys[h][:kend], qp[q0:q1]) + bias[:kend, q0:q1] - level)
                d_prob = nt(values[h][:kend], op[q0:q1])
                row_dot = jnp.sum(soft * d_prob, 0, keepdims=True)
                d_score = (soft * (d_prob - row_dot)).astype(bf16)
                d_value += nn(soft.astype(bf16), backs[h][q0:q1])
                d_key += nn(d_score, queries[h][q0:q1])
                d_query += tn(d_score, keys[h][:kend])
            sums[0, q0:q1, :] += d_query * HEAD_DIM ** (-0.5)
            sums[1, :kend, :] += d_key
            sums[2, :kend, :] += d_value
        for part in range(2):
            t = sums[part, 0:rows, :]
            dproj[:, pl.ds(pl.multiple_of(part * D + p * PAIR, PAIR), PAIR)] = (
                t * cos_ref[...] - swap_halves(t) * sin_ref[...]
            ).astype(bf16)
        dproj[:, pl.ds(pl.multiple_of(2 * D + p * PAIR, PAIR), PAIR)] = sums[2, 0:rows, :].astype(bf16)

    arrive(0).wait()
    big[...] = jnp.zeros(big.shape, f32)

    @pl.loop(0, 3)
    def _(part):
        cols = pl.ds(pl.multiple_of(part * D, D), D)
        gqkv[:, cols] = tn(normed_ref[...], dproj[:, cols]).astype(bf16)
        send(0, 0, D // BLOCK, part * (D // BLOCK), D // BLOCK)
        big[...] += nt(dproj[:, cols], wqkv[:, cols])

    step, gain_one = rms_back(big[...], x_ref[...], g_ref[0:1, :])
    gain_ref[0:1, :] = gain_one
    dx_ref[...] += step
    for m in range(4):
        pltpu.make_async_copy(grads[m], grads[m], sem_out.at[m]).wait()
    if spares > 0:

        @pl.loop(0, spares)
        def _(i):
            pltpu.make_async_copy(zero, tiles_out.at[spare[i]], sem_zero).wait()


def weight_shapes():
    return [(r * BLOCK, c * BLOCK) for r, c in GRIDS]


def forward_layer(slots, length, x, gains, cos, sin, gathered):
    rows = x.shape[0]
    key_rows = round_up(rows, BLOCK)
    vmem = pl.BlockSpec(memory_space=pltpu.VMEM)
    smem = pl.BlockSpec(memory_space=pltpu.SMEM)
    hbm = pl.BlockSpec(memory_space=pl.ANY)
    S = jax.ShapeDtypeStruct
    out_shape = [
        S((rows, D), f32),
        S((rows, D), bf16),
        S((key_rows, D), bf16),
        S((key_rows, D), bf16),
        S((key_rows, D), bf16),
        S((key_rows, BLOCK), f32),
        S((rows, D), bf16),
        S((rows, D), f32),
        S((rows, D), bf16),
        S((rows, 2 * FF), bf16),
    ] + [S(s, bf16) for s in weight_shapes()]
    return pl.pallas_call(
        forward_kernel,
        out_shape=out_shape,
        in_specs=[smem, smem, vmem, vmem, vmem, vmem, hbm],
        out_specs=[vmem] * 10 + [hbm] * 4,
        scratch_shapes=[pltpu.VMEM(s, bf16) for s in weight_shapes()]
        + [
            pltpu.VMEM((rows, key_rows), f32),
            pltpu.SemaphoreType.DMA((4,)),
            pltpu.SemaphoreType.DMA((4,)),
        ],
        compiler_params=pltpu.CompilerParams(vmem_limit_bytes=VMEM_BYTES),
        name="forward_block",
    )(slots, length, x, gains, cos, sin, gathered)


def backward_layer(slots, spare, length, back, gains, cos, sin, x, saved, slot_count, tiles):
    rows = x.shape[0]
    key_rows = round_up(rows, BLOCK)
    vmem = pl.BlockSpec(memory_space=pltpu.VMEM)
    smem = pl.BlockSpec(memory_space=pltpu.SMEM)
    hbm = pl.BlockSpec(memory_space=pl.ANY)
    S = jax.ShapeDtypeStruct
    args = (slots, spare, length, back, gains, cos, sin, x) + tuple(saved)
    aliases = {}
    if tiles is not None:
        aliases = {len(args): 2}
        args = args + (tiles,)
    shapes = weight_shapes()
    return pl.pallas_call(
        backward_kernel,
        out_shape=[S((rows, D), f32), S((2, D), f32), S((slot_count, BLOCK, BLOCK), bf16)],
        in_specs=[smem] * 3 + [vmem] * 14 + [hbm] * (len(args) - 17),
        out_specs=[vmem, vmem, hbm],
        input_output_aliases=aliases,
        scratch_shapes=[pltpu.VMEM(s, bf16) for s in shapes]
        + [pltpu.VMEM(s, bf16) for s in shapes]
        + [
            pltpu.VMEM((BLOCK, BLOCK), bf16),
            pltpu.VMEM((key_rows, key_rows), f32),
            pltpu.VMEM((HEADS, 1, key_rows), f32),
            pltpu.VMEM((3, key_rows, PAIR), f32),
            pltpu.VMEM((rows, D), f32),
            pltpu.VMEM((key_rows, D), bf16),
            pltpu.VMEM((rows, 3 * D), bf16),
            pltpu.SemaphoreType.DMA((4,)),
            pltpu.SemaphoreType.DMA((4,)),
            pltpu.SemaphoreType.DMA,
        ],
        compiler_params=pltpu.CompilerParams(vmem_limit_bytes=VMEM_BYTES),
        name="backward_block",
    )(*args)


def optimizer_kernel(factor, g_ref, m_ref, s_ref, r_ref, wg_ref, ns_ref, nm_ref, nc_ref):
    f = factor[0]
    for i in range(g_ref.shape[0]):
        gb = g_ref[i]
        wg_ref[i] = gb.astype(f32) * f
        half = (1.0 - decay_rate) * f * f
        ns_ref[i, 0] = decay_rate * s_ref[i, 0] + half * nt(gb, gb)
        ns_ref[i, 1] = decay_rate * s_ref[i, 1] + half * tn(gb, gb)
        left = nn(r_ref[i, 0].astype(bf16), (gb.astype(f32) * f).astype(bf16)).astype(bf16)
        new = m_ref[i] - step_rate * nn(left, r_ref[i, 1].astype(bf16))
        nm_ref[i] = new
        nc_ref[i] = new.astype(bf16)


def optimizer(factor, owned, master, statistics, inverse_roots):
    count = owned.shape[0]
    per = max(n for n in range(1, 13) if count % n == 0)
    S = jax.ShapeDtypeStruct
    one = pl.BlockSpec((per, BLOCK, BLOCK), lambda i: (i, 0, 0))
    two = pl.BlockSpec((per, 2, BLOCK, BLOCK), lambda i: (i, 0, 0, 0))
    return pl.pallas_call(
        optimizer_kernel,
        grid=(count // per,),
        out_shape=[
            S(master.shape, f32),
            S(statistics.shape, f32),
            S(master.shape, f32),
            S(master.shape, bf16),
        ],
        in_specs=[pl.BlockSpec(memory_space=pltpu.SMEM), one, one, two, two],
        out_specs=[one, two, one, one],
        compiler_params=pltpu.CompilerParams(vmem_limit_bytes=VMEM_BYTES),
        name="optimizer",
    )(factor, owned, master, statistics, inverse_roots)


def to_images(local, bands, band):
    images, band_rows = local.shape[0], local.shape[-2]
    padded = jnp.concatenate([local, jnp.zeros((bands - images,) + local.shape[1:], local.dtype)], 0)
    whole = jnp.zeros((bands,) + local.shape[1:], local.dtype)
    for shift in range(bands):
        block = lax.dynamic_index_in_dim(padded, (band + shift) % bands, 0, keepdims=False)
        if shift > 0:
            pairs = [(b, (b + shift) % bands) for b in range(bands) if (b + shift) % bands < images]
            block = lax.ppermute(block, "band", pairs)
        whole = lax.dynamic_update_index_in_dim(whole, block, (band - shift) % bands, 0)
    return whole


def to_bands(whole, images, bands, band):
    local = jnp.zeros(whole.shape, whole.dtype)
    for shift in range(bands):
        block = lax.dynamic_index_in_dim(whole, (band + shift) % bands, 0, keepdims=False)
        if shift > 0:
            pairs = [(b, (b + shift) % bands) for b in range(images)]
            block = lax.ppermute(block, "band", pairs)
        local = lax.dynamic_update_index_in_dim(local, block, (band - shift) % bands, 0)
    return local[:images]


def rope_tables(rows):
    half = HEAD_DIM // 2
    frequency = rope_base ** (-(jnp.arange(half, dtype=f32) * 2.0 / HEAD_DIM))
    angles = jnp.arange(rows, dtype=jnp.int32).astype(f32)[:, None] * frequency[None, :]
    cosine, sine = jnp.cos(angles), jnp.sin(angles)
    return jnp.tile(cosine, (1, 4)), jnp.tile(jnp.concatenate([-sine, sine], 1), (1, 2))


def shards(
    tokens,
    cotangent,
    lengths,
    slot_of_block,
    master,
    statistics,
    inverse_roots,
    gain_values,
    gain_moments,
):
    images, band_rows, _ = tokens.shape
    band = lax.axis_index("band")
    bands = lax.axis_size("band")
    seq = band_rows * bands
    rows = round_up(seq, 16)
    gathered = lax.all_gather(master.astype(bf16), "dp", axis=0, tiled=True)
    slot_count = gathered.shape[0]

    arrived = to_images(jnp.stack([tokens, cotangent], 1), bands, band)
    token_rows = jnp.pad(arrived[:, 0].reshape(seq, D), ((0, rows - seq), (0, 0)))
    back_rows = jnp.pad(arrived[:, 1].reshape(seq, D), ((0, rows - seq), (0, 0)))
    length = lengths[jnp.minimum(band, images - 1)]
    valid = (jnp.arange(rows, dtype=jnp.int32) < length).astype(f32)
    length = length.reshape(1)
    cos, sin = rope_tables(rows)

    spare_count = slot_count - slot_of_block.shape[0]
    spare = jnp.zeros((1,), jnp.int32)
    if spare_count > 0:
        used = jnp.zeros((slot_count,), jnp.int32).at[slot_of_block].set(1)
        spare = jnp.concatenate([jnp.argsort(used)[:spare_count].astype(jnp.int32), spare])

    hidden = token_rows.astype(f32)
    inputs, saves = [], []
    for layer in range(LAYERS):
        slots = slot_of_block[layer * PER_LAYER : (layer + 1) * PER_LAYER]
        gains = gain_values[2 * layer : 2 * layer + 2]
        inputs.append(hidden)
        hidden, *saved = forward_layer(slots, length, hidden, gains, cos, sin, gathered)
        saves.append(saved)
    layer_output = to_bands(
        hidden[:seq].astype(bf16).reshape(bands, band_rows, D), images, bands, band
    )

    back = back_rows.astype(f32) * valid[:, None]
    tiles = None
    gain_parts = [None] * LAYERS
    for layer in range(LAYERS - 1, -1, -1):
        slots = slot_of_block[layer * PER_LAYER : (layer + 1) * PER_LAYER]
        gains = gain_values[2 * layer : 2 * layer + 2]
        back, gain_parts[layer], tiles = backward_layer(
            slots, spare if layer == LAYERS - 1 else spare[-1:], length, back, gains, cos, sin,
            inputs[layer], saves[layer], slot_count, tiles,
        )
    input_grad = to_bands(back[:seq].astype(bf16).reshape(bands, band_rows, D), images, bands, band)

    owned = lax.psum_scatter(tiles, "dp", scatter_dimension=0, tiled=True)
    owned = lax.psum(owned, "band")
    gain_total = lax.psum(jnp.concatenate(gain_parts, 0), ("dp", "band"))
    owned_f = owned.astype(f32)
    owned_squares = lax.psum(jnp.sum(owned_f * owned_f), "dp")
    grad_norm = jnp.sqrt(owned_squares + jnp.sum(gain_total * gain_total))
    factor = jnp.minimum(1.0, clip_limit / grad_norm)
    weight_grads, new_statistics, new_master, master_copy = optimizer(
        factor.reshape(1), owned, master, statistics, inverse_roots
    )
    gain_grads = gain_total * factor
    new_moments = decay_rate * gain_moments + (1.0 - decay_rate) * gain_grads * gain_grads
    new_gains = gain_values - gain_rate * gain_grads / (jnp.sqrt(new_moments) + epsilon)
    return (
        layer_output,
        input_grad,
        weight_grads,
        grad_norm,
        new_statistics,
        new_master,
        master_copy,
        gain_grads,
        new_moments,
        new_gains,
    )


def solution(mesh):
    return jax.shard_map(
        shards,
        mesh=mesh,
        in_specs=(
            P("dp", "band", None),
            P("dp", "band", None),
            P("dp"),
            P(),
            P("dp", None, None),
            P("dp", None, None, None),
            P("dp", None, None, None),
            P(),
            P(),
        ),
        out_specs=(
            P("dp", "band", None),
            P("dp", "band", None),
            P("dp", None, None),
            P(),
            P("dp", None, None, None),
            P("dp", None, None),
            P("dp", None, None),
            P(),
            P(),
            P(),
        ),
        check_vma=False,
    )
```

```python
import functools

import jax
import jax.numpy as jnp
from jax import lax
from jax.experimental import pallas as pl
from jax.experimental.pallas import tpu as pltpu
from jax.sharding import PartitionSpec as P

D = 768
HEADS = 12
HEAD_DIM = 64
FF = 2048
LAYERS = 2
BLOCK = 128
PAIR = 2 * HEAD_DIM

epsilon = 1e-05
rope_base = 10000.0
decay_rate = 0.5
step_rate = 0.4
gain_rate = 0.2
clip_limit = 1.0
masked_score = -1e30
VMEM_BYTES = 62 * 2**20

f32 = jnp.float32
bf16 = jnp.bfloat16

GRIDS = [
    (D // BLOCK, 3 * D // BLOCK),
    (D // BLOCK, D // BLOCK),
    (D // BLOCK, 2 * FF // BLOCK),
    (FF // BLOCK, D // BLOCK),
]
COUNTS = [r * c for r, c in GRIDS]
OFFSETS = [sum(COUNTS[:i]) for i in range(4)]
PER_LAYER = sum(COUNTS)
FF_STEP = 512


def round_up(n, m):
    return -(-n // m) * m


def nn(a, b):
    return lax.dot_general(a, b, (((1,), (0,)), ((), ())), preferred_element_type=f32)


def nt(a, b):
    return lax.dot_general(a, b, (((1,), (1,)), ((), ())), preferred_element_type=f32)


def tn(a, b):
    return lax.dot_general(a, b, (((0,), (0,)), ((), ())), preferred_element_type=f32)


def query_blocks(rows, step=256):
    return [(s, min(s + step, rows)) for s in range(0, rows, step)]


def swap_halves(t):
    lane = lax.broadcasted_iota(jnp.int32, t.shape, 1)
    half = HEAD_DIM // 2
    return jnp.where(lane % HEAD_DIM < half, pltpu.roll(t, PAIR - half, 1), pltpu.roll(t, half, 1))


def rms(m):
    return lax.rsqrt(jnp.mean(m * m, -1, keepdims=True) + epsilon)


def rms_back(u, m, g):
    r = rms(m)
    t = u * g
    dot = jnp.mean(t * m, -1, keepdims=True)
    return r * t - m * (r * r * r * dot), jnp.sum(u * m * r, 0, keepdims=True)


def forward_kernel(
    slots, length, x_ref, g_ref, cos_ref, sin_ref, w_hbm,
    xn_ref, normed_ref, q_ref, k_ref, v_ref, st_ref, mixed_ref, mid_ref, n2_ref, gu_ref,
    wqkv_o, wout_o, wgu_o, wd_o,
    wqkv, wout, wgu, wd, bias, sem_in, sem_out,
):
    rows = x_ref.shape[0]
    key_rows = q_ref.shape[0]
    held = (wqkv, wout, wgu, wd)
    for m in range(4):
        tile_rows, tile_cols = GRIDS[m]

        @pl.loop(0, tile_rows)
        def _(i, m=m, tile_cols=tile_cols):
            for j in range(tile_cols):
                slot = slots[OFFSETS[m] + i * tile_cols + j]
                pltpu.make_async_copy(
                    w_hbm.at[slot],
                    held[m].at[pl.ds(pl.multiple_of(i * BLOCK, BLOCK), BLOCK), pl.ds(j * BLOCK, BLOCK)],
                    sem_in.at[m],
                ).start()

    def arrive(m):
        pltpu.make_async_copy(held[m], held[m], sem_in.at[m]).wait()

    outs = (wqkv_o, wout_o, wgu_o, wd_o)

    def leave(m):
        return pltpu.make_async_copy(held[m], outs[m], sem_out.at[m])

    query = lax.broadcasted_iota(jnp.int32, bias.shape, 0)
    key = lax.broadcasted_iota(jnp.int32, bias.shape, 1)
    bias[...] = jnp.where((key <= query) & (key < length[0]), 0.0, masked_score)
    x = x_ref[...]
    normed_ref[...] = (x * rms(x) * g_ref[0:1, :]).astype(bf16)
    tail = key_rows - rows
    for ref in (q_ref, k_ref, v_ref):
        ref[rows:, :] = jnp.zeros((tail, D), bf16)
    arrive(0)
    leave(0).start()

    @pl.loop(0, 2)
    def _(part):
        acc = nn(normed_ref[...], wqkv[:, pl.ds(pl.multiple_of(part * D, D), D)])
        scale = jnp.where(part == 0, HEAD_DIM ** (-0.5), 1.0)
        for p in range(HEADS // 2):
            t = acc[:, p * PAIR : (p + 1) * PAIR]
            rot = ((t * cos_ref[...] + swap_halves(t) * sin_ref[...]) * scale).astype(bf16)

            @pl.when(part == 0)
            def _(p=p, rot=rot):
                q_ref[0:rows, p * PAIR : (p + 1) * PAIR] = rot

            @pl.when(part == 1)
            def _(p=p, rot=rot):
                k_ref[0:rows, p * PAIR : (p + 1) * PAIR] = rot

    v_ref[0:rows, :] = nn(normed_ref[...], wqkv[:, 2 * D :]).astype(bf16)
    st_ref[...] = jnp.zeros(st_ref.shape, f32)

    @pl.loop(0, HEADS // 2)
    def _(p):
        cols = pl.ds(pl.multiple_of(p * PAIR, PAIR), PAIR)
        kp = k_ref[:, cols]
        vp = v_ref[:, cols]
        low = lax.broadcasted_iota(jnp.int32, kp.shape, 1) < HEAD_DIM
        keys = (jnp.where(low, kp, 0), jnp.where(low, 0, kp))
        values = (jnp.where(low, vp, 1), jnp.where(low, 1, vp))
        for q0, q1 in query_blocks(rows):
            kend = min(round_up(q1, BLOCK), key_rows)
            qp = q_ref[q0:q1, cols]
            mask = bias[q0:q1, :kend]
            parts = []
            tops = []
            for h in range(2):
                s = nt(qp, keys[h][:kend]) + mask
                top = jnp.max(s, -1, keepdims=True)
                e = jnp.exp(s - top).astype(bf16)
                parts.append(nn(e, values[h][:kend]))
                tops.append(top)
            lane = lax.broadcasted_iota(jnp.int32, parts[0].shape, 1)
            low_q = lane < HEAD_DIM
            total = pltpu.roll(jnp.where(low_q, parts[1], parts[0]), HEAD_DIM, 1)
            mixed_ref[q0:q1, cols] = (jnp.where(low_q, parts[0], parts[1]) / total).astype(bf16)
            log_total = jnp.log(total)
            other = pltpu.roll(log_total, HEAD_DIM, 1)
            first = tops[0] + jnp.where(low_q, log_total, other)
            second = tops[1] + jnp.where(low_q, other, log_total)
            old = st_ref[q0:q1, :]
            st_ref[q0:q1, :] = jnp.where(
                lane == 2 * p, first, jnp.where(lane == 2 * p + 1, second, old)
            )

    arrive(1)
    leave(1).start()
    middle = x_ref[...] + nn(mixed_ref[...], wout[...])
    mid_ref[...] = middle
    n2_ref[...] = (middle * rms(middle) * g_ref[1:2, :]).astype(bf16)
    arrive(2)
    leave(2).start()
    arrive(3)
    leave(3).start()
    xn_ref[...] = mid_ref[...]

    @pl.loop(0, FF // FF_STEP)
    def _(t):
        at = pl.multiple_of(t * FF_STEP, FF_STEP)
        gate = nn(n2_ref[...], wgu[:, pl.ds(at, FF_STEP)])
        up = nn(n2_ref[...], wgu[:, pl.ds(FF + at, FF_STEP)])
        act = (gate / (1.0 + jnp.exp(-gate)) * up).astype(bf16)
        gu_ref[:, pl.ds(at, FF_STEP)] = gate.astype(bf16)
        gu_ref[:, pl.ds(FF + at, FF_STEP)] = up.astype(bf16)
        xn_ref[...] += nn(act, wd[pl.ds(at, FF_STEP), :])

    for m in range(4):
        leave(m).wait()


def backward_kernel(
    slots, spare, length, back_ref, g_ref, cos_ref, sin_ref,
    x_ref, normed_ref, q_ref, k_ref, v_ref, st_ref, mixed_ref, mid_ref, n2_ref, gu_ref,
    wqkv_i, wout_i, wgu_i, wd_i, *rest,
):
    (
        dx_ref, gain_ref, tiles_out,
        wqkv, wout, wgu, wd, gqkv, gout, ggu, gd, zero, bias, turned, sums, big, mixed_back, dproj,
        sem_in, sem_out, sem_zero,
    ) = rest[-21:]
    rows = x_ref.shape[0]
    key_rows = q_ref.shape[0]
    held = (wqkv, wout, wgu, wd)
    given = (wqkv_i, wout_i, wgu_i, wd_i)

    def arrive(m):
        return pltpu.make_async_copy(given[m], held[m], sem_in.at[m])

    for m in (3, 2, 1, 0):
        arrive(m).start()
    grads = (gqkv, gout, ggu, gd)

    def send(m, i0, i1, j0, count_j):
        @pl.loop(i0, i1)
        def _(i):
            for jj in range(count_j):
                j = j0 + jj
                slot = slots[OFFSETS[m] + i * GRIDS[m][1] + j]
                pltpu.make_async_copy(
                    grads[m].at[
                        pl.ds(pl.multiple_of(i * BLOCK, BLOCK), BLOCK),
                        pl.ds(pl.multiple_of(j * BLOCK, BLOCK), BLOCK),
                    ],
                    tiles_out.at[slot],
                    sem_out.at[m],
                ).start()

    spares = spare.shape[0] - 1
    if spares > 0:
        zero[...] = jnp.zeros(zero.shape, bf16)

        @pl.loop(0, spares)
        def _(i):
            pltpu.make_async_copy(zero, tiles_out.at[spare[i]], sem_zero).start()

    key = lax.broadcasted_iota(jnp.int32, bias.shape, 0)
    query = lax.broadcasted_iota(jnp.int32, bias.shape, 1)
    bias[...] = jnp.where((key <= query) & (key < length[0]), 0.0, masked_score)
    levels = st_ref[...].T
    for h in range(HEADS):
        turned[h] = levels[h : h + 1, :]
    big[...] = jnp.zeros(big.shape, f32)
    back_b = back_ref[...].astype(bf16)
    arrive(3).wait()
    arrive(2).wait()

    @pl.loop(0, FF // FF_STEP)
    def _(t):
        at = pl.multiple_of(t * FF_STEP, FF_STEP)
        here = pl.ds(at, FF_STEP)
        there = pl.ds(FF + at, FF_STEP)
        back_ffn = back_ref[...].astype(bf16)
        d_act = nt(back_ffn, wd[here, :])
        gate = gu_ref[:, here].astype(f32)
        up = gu_ref[:, there].astype(f32)
        sig = 1.0 / (1.0 + jnp.exp(-gate))
        silu = gate * sig
        act = (silu * up).astype(bf16)
        d_gate = (d_act * up * (sig * (1.0 + gate * (1.0 - sig)))).astype(bf16)
        d_up = (d_act * silu).astype(bf16)
        gd[here, :] = tn(act, back_ffn).astype(bf16)
        ggu[:, here] = tn(n2_ref[...], d_gate).astype(bf16)
        ggu[:, there] = tn(n2_ref[...], d_up).astype(bf16)
        per = FF_STEP // BLOCK
        send(3, t * per, (t + 1) * per, 0, D // BLOCK)
        send(2, 0, D // BLOCK, t * per, per)
        send(2, 0, D // BLOCK, FF // BLOCK + t * per, per)
        big[...] += nt(d_gate, wgu[:, here]) + nt(d_up, wgu[:, there])

    step, gain_two = rms_back(big[...], mid_ref[...], g_ref[1:2, :])
    gain_ref[1:2, :] = gain_two
    dx_ref[...] = back_ref[...] + step
    arrive(1).wait()
    back_attn = dx_ref[...].astype(bf16)
    gout[...] = tn(mixed_ref[...], back_attn).astype(bf16)
    send(1, 0, D // BLOCK, 0, D // BLOCK)
    mixed_back[0:rows, :] = nt(back_attn, wout[...]).astype(bf16)
    mixed_back[rows:, :] = jnp.zeros((key_rows - rows, D), bf16)

    @pl.loop(0, HEADS // 2)
    def _(p):
        cols = pl.ds(pl.multiple_of(p * PAIR, PAIR), PAIR)
        low = lax.broadcasted_iota(jnp.int32, (key_rows, PAIR), 1) < HEAD_DIM

        def both(t):
            return (jnp.where(low, t, 0), jnp.where(low, 0, t))

        qp = q_ref[:, cols]
        op = mixed_back[:, cols]
        keys, values, queries, backs = both(k_ref[:, cols]), both(v_ref[:, cols]), both(qp), both(op)
        sums[...] = jnp.zeros(sums.shape, f32)
        for q0, q1 in query_blocks(key_rows):
            kend = q1
            d_query = jnp.zeros((q1 - q0, PAIR), f32)
            d_key = jnp.zeros((kend, PAIR), f32)
            d_value = jnp.zeros((kend, PAIR), f32)
            for h in range(2):
                level = turned[2 * p + h, :, q0:q1]
                soft = jnp.exp(nt(keys[h][:kend], qp[q0:q1]) + bias[:kend, q0:q1] - level)
                d_prob = nt(values[h][:kend], op[q0:q1])
                row_dot = jnp.sum(soft * d_prob, 0, keepdims=True)
                d_score = (soft * (d_prob - row_dot)).astype(bf16)
                d_value += nn(soft.astype(bf16), backs[h][q0:q1])
                d_key += nn(d_score, queries[h][q0:q1])
                d_query += tn(d_score, keys[h][:kend])
            sums[0, q0:q1, :] += d_query * HEAD_DIM ** (-0.5)
            sums[1, :kend, :] += d_key
            sums[2, :kend, :] += d_value
        for part in range(2):
            t = sums[part, 0:rows, :]
            dproj[:, pl.ds(pl.multiple_of(part * D + p * PAIR, PAIR), PAIR)] = (
                t * cos_ref[...] - swap_halves(t) * sin_ref[...]
            ).astype(bf16)
        dproj[:, pl.ds(pl.multiple_of(2 * D + p * PAIR, PAIR), PAIR)] = sums[2, 0:rows, :].astype(bf16)

    arrive(0).wait()
    big[...] = jnp.zeros(big.shape, f32)

    @pl.loop(0, 3)
    def _(part):
        cols = pl.ds(pl.multiple_of(part * D, D), D)
        gqkv[:, cols] = tn(normed_ref[...], dproj[:, cols]).astype(bf16)
        send(0, 0, D // BLOCK, part * (D // BLOCK), D // BLOCK)
        big[...] += nt(dproj[:, cols], wqkv[:, cols])

    step, gain_one = rms_back(big[...], x_ref[...], g_ref[0:1, :])
    gain_ref[0:1, :] = gain_one
    dx_ref[...] += step
    for m in range(4):
        pltpu.make_async_copy(grads[m], grads[m], sem_out.at[m]).wait()
    if spares > 0:

        @pl.loop(0, spares)
        def _(i):
            pltpu.make_async_copy(zero, tiles_out.at[spare[i]], sem_zero).wait()


def weight_shapes():
    return [(r * BLOCK, c * BLOCK) for r, c in GRIDS]


def forward_layer(slots, length, x, gains, cos, sin, gathered):
    rows = x.shape[0]
    key_rows = round_up(rows, BLOCK)
    vmem = pl.BlockSpec(memory_space=pltpu.VMEM)
    smem = pl.BlockSpec(memory_space=pltpu.SMEM)
    hbm = pl.BlockSpec(memory_space=pl.ANY)
    S = jax.ShapeDtypeStruct
    out_shape = [
        S((rows, D), f32),
        S((rows, D), bf16),
        S((key_rows, D), bf16),
        S((key_rows, D), bf16),
        S((key_rows, D), bf16),
        S((key_rows, BLOCK), f32),
        S((rows, D), bf16),
        S((rows, D), f32),
        S((rows, D), bf16),
        S((rows, 2 * FF), bf16),
    ] + [S(s, bf16) for s in weight_shapes()]
    return pl.pallas_call(
        forward_kernel,
        out_shape=out_shape,
        in_specs=[smem, smem, vmem, vmem, vmem, vmem, hbm],
        out_specs=[vmem] * 10 + [hbm] * 4,
        scratch_shapes=[pltpu.VMEM(s, bf16) for s in weight_shapes()]
        + [
            pltpu.VMEM((rows, key_rows), f32),
            pltpu.SemaphoreType.DMA((4,)),
            pltpu.SemaphoreType.DMA((4,)),
        ],
        compiler_params=pltpu.CompilerParams(vmem_limit_bytes=VMEM_BYTES),
        name="forward_block",
    )(slots, length, x, gains, cos, sin, gathered)


def backward_layer(slots, spare, length, back, gains, cos, sin, x, saved, slot_count, tiles):
    rows = x.shape[0]
    key_rows = round_up(rows, BLOCK)
    vmem = pl.BlockSpec(memory_space=pltpu.VMEM)
    smem = pl.BlockSpec(memory_space=pltpu.SMEM)
    hbm = pl.BlockSpec(memory_space=pl.ANY)
    S = jax.ShapeDtypeStruct
    args = (slots, spare, length, back, gains, cos, sin, x) + tuple(saved)
    aliases = {}
    if tiles is not None:
        aliases = {len(args): 2}
        args = args + (tiles,)
    shapes = weight_shapes()
    return pl.pallas_call(
        backward_kernel,
        out_shape=[S((rows, D), f32), S((2, D), f32), S((slot_count, BLOCK, BLOCK), bf16)],
        in_specs=[smem] * 3 + [vmem] * 14 + [hbm] * (len(args) - 17),
        out_specs=[vmem, vmem, hbm],
        input_output_aliases=aliases,
        scratch_shapes=[pltpu.VMEM(s, bf16) for s in shapes]
        + [pltpu.VMEM(s, bf16) for s in shapes]
        + [
            pltpu.VMEM((BLOCK, BLOCK), bf16),
            pltpu.VMEM((key_rows, key_rows), f32),
            pltpu.VMEM((HEADS, 1, key_rows), f32),
            pltpu.VMEM((3, key_rows, PAIR), f32),
            pltpu.VMEM((rows, D), f32),
            pltpu.VMEM((key_rows, D), bf16),
            pltpu.VMEM((rows, 3 * D), bf16),
            pltpu.SemaphoreType.DMA((4,)),
            pltpu.SemaphoreType.DMA((4,)),
            pltpu.SemaphoreType.DMA,
        ],
        compiler_params=pltpu.CompilerParams(vmem_limit_bytes=VMEM_BYTES),
        name="backward_block",
    )(*args)


def optimizer_kernel(factor, g_ref, m_ref, s_ref, r_ref, wg_ref, ns_ref, nm_ref, nc_ref):
    f = factor[0]
    for i in range(g_ref.shape[0]):
        gb = g_ref[i]
        wg_ref[i] = gb.astype(f32) * f
        half = (1.0 - decay_rate) * f * f
        ns_ref[i, 0] = decay_rate * s_ref[i, 0] + half * nt(gb, gb)
        ns_ref[i, 1] = decay_rate * s_ref[i, 1] + half * tn(gb, gb)
        left = nn(r_ref[i, 0].astype(bf16), (gb.astype(f32) * f).astype(bf16)).astype(bf16)
        new = m_ref[i] - step_rate * nn(left, r_ref[i, 1].astype(bf16))
        nm_ref[i] = new
        nc_ref[i] = new.astype(bf16)


def optimizer(factor, owned, master, statistics, inverse_roots):
    count = owned.shape[0]
    per = max(n for n in range(1, 13) if count % n == 0)
    S = jax.ShapeDtypeStruct
    one = pl.BlockSpec((per, BLOCK, BLOCK), lambda i: (i, 0, 0))
    two = pl.BlockSpec((per, 2, BLOCK, BLOCK), lambda i: (i, 0, 0, 0))
    return pl.pallas_call(
        optimizer_kernel,
        grid=(count // per,),
        out_shape=[
            S(master.shape, f32),
            S(statistics.shape, f32),
            S(master.shape, f32),
            S(master.shape, bf16),
        ],
        in_specs=[pl.BlockSpec(memory_space=pltpu.SMEM), one, one, two, two],
        out_specs=[one, two, one, one],
        compiler_params=pltpu.CompilerParams(vmem_limit_bytes=VMEM_BYTES),
        name="optimizer",
    )(factor, owned, master, statistics, inverse_roots)


def to_images(local, bands, band):
    images, band_rows = local.shape[0], local.shape[-2]
    padded = jnp.concatenate([local, jnp.zeros((bands - images,) + local.shape[1:], local.dtype)], 0)
    whole = jnp.zeros((bands,) + local.shape[1:], local.dtype)
    for shift in range(bands):
        block = lax.dynamic_index_in_dim(padded, (band + shift) % bands, 0, keepdims=False)
        if shift > 0:
            pairs = [(b, (b + shift) % bands) for b in range(bands) if (b + shift) % bands < images]
            block = lax.ppermute(block, "band", pairs)
        whole = lax.dynamic_update_index_in_dim(whole, block, (band - shift) % bands, 0)
    return whole


def to_bands(whole, images, bands, band):
    local = jnp.zeros(whole.shape, whole.dtype)
    for shift in range(bands):
        block = lax.dynamic_index_in_dim(whole, (band + shift) % bands, 0, keepdims=False)
        if shift > 0:
            pairs = [(b, (b + shift) % bands) for b in range(images)]
            block = lax.ppermute(block, "band", pairs)
        local = lax.dynamic_update_index_in_dim(local, block, (band - shift) % bands, 0)
    return local[:images]


def add(a, b):
    return (a.astype(f32) + b.astype(f32)).astype(bf16)


def chunk_sizes(per_owner):
    parts = [per_owner * p // 108 for p in (24, 32, 28, 16)]
    return parts + [per_owner - sum(parts)]


def relative_places(slots, per_owner, me):
    owner, rank = slots // per_owner, slots % per_owner
    relative = owner ^ me
    relative = (relative % 2) * 4 + (relative // 2 % 2) * 2 + relative // 4
    place = jnp.zeros_like(slots)
    start = 0
    for size in chunk_sizes(per_owner):
        inside = (rank >= start) & (rank < start + size)
        place = jnp.where(inside, start * 8 + relative * size + rank - start, place)
        start += size
    return place


def reduce_to_owners(tiles, band):
    core = [(i, i ^ 1) for i in range(8)]
    x_pairs = [(i, i ^ 2) for i in range(8)]
    y_pairs = [(i, i ^ 4) for i in range(8)]
    sizes = chunk_sizes(tiles.shape[0] // 8)
    chunks, start = [], 0
    for size in sizes:
        chunks.append(tiles[start * 8 : (start + size) * 8].reshape(2, 2, 2, size, BLOCK, BLOCK))
        start += size
    from_core = [lax.ppermute(chunk[1], "dp", core) for chunk in chunks]
    gate, outs = None, []
    for chunk, received in zip(chunks, from_core):
        both = add(chunk[0], received)
        half = both.shape[2] // 2
        one, two = both[:, :, :half], both[:, :, half:]
        send_x, send_y = one[1], two[:, 1]
        if gate is not None:
            send_x, send_y, _ = lax.optimization_barrier((send_x, send_y, gate))
        one = add(one[0], lax.ppermute(send_x, "dp", x_pairs))
        two = add(two[:, 0], lax.ppermute(send_y, "dp", y_pairs))
        from_y = lax.ppermute(one[1], "dp", y_pairs)
        from_x = lax.ppermute(two[1], "dp", x_pairs)
        gate = (from_y, from_x)
        plane = jnp.concatenate([add(one[0], from_y), add(two[0], from_x)], 0)
        up = lax.ppermute(plane, "band", [(0, 1)])
        down = lax.ppermute(plane, "band", [(2, 1)])
        total = (plane.astype(f32) + up.astype(f32) + down.astype(f32)).astype(bf16)
        to_first = lax.ppermute(total, "band", [(1, 0)])
        to_third = lax.ppermute(total, "band", [(1, 2)])
        to_last = lax.ppermute(to_third, "band", [(2, 3)])
        total = jnp.where(band == 0, to_first, total)
        total = jnp.where(band == 2, to_third, total)
        outs.append(jnp.where(band == 3, to_last, total))
    return jnp.concatenate(outs, 0)


def rope_tables(rows):
    half = HEAD_DIM // 2
    frequency = rope_base ** (-(jnp.arange(half, dtype=f32) * 2.0 / HEAD_DIM))
    angles = jnp.arange(rows, dtype=jnp.int32).astype(f32)[:, None] * frequency[None, :]
    cosine, sine = jnp.cos(angles), jnp.sin(angles)
    return jnp.tile(cosine, (1, 4)), jnp.tile(jnp.concatenate([-sine, sine], 1), (1, 2))


def shards(
    tokens,
    cotangent,
    lengths,
    slot_of_block,
    master,
    statistics,
    inverse_roots,
    gain_values,
    gain_moments,
):
    images, band_rows, _ = tokens.shape
    band = lax.axis_index("band")
    bands = lax.axis_size("band")
    seq = band_rows * bands
    rows = round_up(seq, 16)
    gathered = lax.all_gather(master.astype(bf16), "dp", axis=0, tiled=True)
    slot_count = gathered.shape[0]

    arrived = to_images(jnp.stack([tokens, cotangent], 1), bands, band)
    token_rows = jnp.pad(arrived[:, 0].reshape(seq, D), ((0, rows - seq), (0, 0)))
    back_rows = jnp.pad(arrived[:, 1].reshape(seq, D), ((0, rows - seq), (0, 0)))
    length = lengths[jnp.minimum(band, images - 1)]
    valid = (jnp.arange(rows, dtype=jnp.int32) < length).astype(f32)
    length = length.reshape(1)
    cos, sin = rope_tables(rows)

    spare_count = slot_count - slot_of_block.shape[0]
    spare = jnp.zeros((1,), jnp.int32)
    if spare_count > 0:
        used = jnp.zeros((slot_count,), jnp.int32).at[slot_of_block].set(1)
        spare = jnp.concatenate([jnp.argsort(used)[:spare_count].astype(jnp.int32), spare])

    hidden = token_rows.astype(f32)
    inputs, saves = [], []
    for layer in range(LAYERS):
        slots = slot_of_block[layer * PER_LAYER : (layer + 1) * PER_LAYER]
        gains = gain_values[2 * layer : 2 * layer + 2]
        inputs.append(hidden)
        hidden, *saved = forward_layer(slots, length, hidden, gains, cos, sin, gathered)
        saves.append(saved)
    layer_output = to_bands(
        hidden[:seq].astype(bf16).reshape(bands, band_rows, D), images, bands, band
    )

    back = back_rows.astype(f32) * valid[:, None]
    by_permutes = lax.axis_size("dp") == 8 and bands == 4 and images == 3
    places = slot_of_block
    if by_permutes:
        places = relative_places(places, master.shape[0], lax.axis_index("dp"))
        spare = relative_places(spare, master.shape[0], lax.axis_index("dp"))
    tiles = None
    gain_parts = [None] * LAYERS
    for layer in range(LAYERS - 1, -1, -1):
        slots = places[layer * PER_LAYER : (layer + 1) * PER_LAYER]
        gains = gain_values[2 * layer : 2 * layer + 2]
        back, gain_parts[layer], tiles = backward_layer(
            slots, spare if layer == LAYERS - 1 else spare[-1:], length, back, gains, cos, sin,
            inputs[layer], saves[layer], slot_count, tiles,
        )
    input_grad = to_bands(back[:seq].astype(bf16).reshape(bands, band_rows, D), images, bands, band)

    if by_permutes:
        owned = reduce_to_owners(tiles, band)
    else:
        owned = lax.psum_scatter(tiles, "dp", scatter_dimension=0, tiled=True)
        owned = lax.psum(owned, "band")
    gain_total = lax.psum(jnp.concatenate(gain_parts, 0), ("dp", "band"))
    owned_f = owned.astype(f32)
    owned_squares = lax.psum(jnp.sum(owned_f * owned_f), "dp")
    grad_norm = jnp.sqrt(owned_squares + jnp.sum(gain_total * gain_total))
    factor = jnp.minimum(1.0, clip_limit / grad_norm)
    weight_grads, new_statistics, new_master, master_copy = optimizer(
        factor.reshape(1), owned, master, statistics, inverse_roots
    )
    gain_grads = gain_total * factor
    new_moments = decay_rate * gain_moments + (1.0 - decay_rate) * gain_grads * gain_grads
    new_gains = gain_values - gain_rate * gain_grads / (jnp.sqrt(new_moments) + epsilon)
    return (
        layer_output,
        input_grad,
        weight_grads,
        grad_norm,
        new_statistics,
        new_master,
        master_copy,
        gain_grads,
        new_moments,
        new_gains,
    )


def solution(mesh):
    return jax.shard_map(
        shards,
        mesh=mesh,
        in_specs=(
            P("dp", "band", None),
            P("dp", "band", None),
            P("dp"),
            P(),
            P("dp", None, None),
            P("dp", None, None, None),
            P("dp", None, None, None),
            P(),
            P(),
        ),
        out_specs=(
            P("dp", "band", None),
            P("dp", "band", None),
            P("dp", None, None),
            P(),
            P("dp", None, None, None),
            P("dp", None, None),
            P("dp", None, None),
            P(),
            P(),
            P(),
        ),
        check_vma=False,
    )
```

```python
import functools

import jax
import jax.numpy as jnp
from jax import lax
from jax.experimental import pallas as pl
from jax.experimental.pallas import tpu as pltpu
from jax.sharding import PartitionSpec as P

D = 768
HEADS = 12
HEAD_DIM = 64
FF = 2048
LAYERS = 2
BLOCK = 128
PAIR = 2 * HEAD_DIM

epsilon = 1e-05
rope_base = 10000.0
decay_rate = 0.5
step_rate = 0.4
gain_rate = 0.2
clip_limit = 1.0
masked_score = -1e30
VMEM_BYTES = 62 * 2**20

f32 = jnp.float32
bf16 = jnp.bfloat16

GRIDS = [
    (D // BLOCK, 3 * D // BLOCK),
    (D // BLOCK, D // BLOCK),
    (D // BLOCK, 2 * FF // BLOCK),
    (FF // BLOCK, D // BLOCK),
]
COUNTS = [r * c for r, c in GRIDS]
OFFSETS = [sum(COUNTS[:i]) for i in range(4)]
PER_LAYER = sum(COUNTS)
FF_STEP = 512


def round_up(n, m):
    return -(-n // m) * m


def nn(a, b):
    return lax.dot_general(a, b, (((1,), (0,)), ((), ())), preferred_element_type=f32)


def nt(a, b):
    return lax.dot_general(a, b, (((1,), (1,)), ((), ())), preferred_element_type=f32)


def tn(a, b):
    return lax.dot_general(a, b, (((0,), (0,)), ((), ())), preferred_element_type=f32)


def query_blocks(rows, step=256):
    return [(s, min(s + step, rows)) for s in range(0, rows, step)]


def swap_halves(t):
    lane = lax.broadcasted_iota(jnp.int32, t.shape, 1)
    half = HEAD_DIM // 2
    return jnp.where(lane % HEAD_DIM < half, pltpu.roll(t, PAIR - half, 1), pltpu.roll(t, half, 1))


def rms(m):
    return lax.rsqrt(jnp.mean(m * m, -1, keepdims=True) + epsilon)


def rms_back(u, m, g):
    r = rms(m)
    t = u * g
    dot = jnp.mean(t * m, -1, keepdims=True)
    return r * t - m * (r * r * r * dot), jnp.sum(u * m * r, 0, keepdims=True)


def copies(pairs, sem):
    return [pltpu.make_async_copy(src, dst, sem.at[i]) for i, (src, dst) in enumerate(pairs)]


def forward_kernel(
    slots, length, x_ref, g_ref, cos_ref, sin_ref, w_hbm,
    xn_ref, normed_o, q_o, k_o, v_o, st_o, mixed_o, mid_o, n2_o, gu_o, wqkv_o, wout_o, wgu_o, wd_o,
    normed_ref, q_ref, k_ref, v_ref, st_ref, mixed_ref, mid_ref, n2_ref, gu_ref,
    wqkv, wout, wgu, wd, bias, sem_in, sem_out,
):
    rows = x_ref.shape[0]
    key_rows = q_ref.shape[0]
    held = (wqkv, wout, wgu, wd)
    for m in range(4):
        tile_rows, tile_cols = GRIDS[m]

        @pl.loop(0, tile_rows)
        def _(i, m=m, tile_cols=tile_cols):
            for j in range(tile_cols):
                slot = slots[OFFSETS[m] + i * tile_cols + j]
                pltpu.make_async_copy(
                    w_hbm.at[slot],
                    held[m].at[pl.ds(pl.multiple_of(i * BLOCK, BLOCK), BLOCK), pl.ds(j * BLOCK, BLOCK)],
                    sem_in.at[m],
                ).start()

    def arrive(m):
        pltpu.make_async_copy(held[m], held[m], sem_in.at[m]).wait()

    saves = copies(
        [
            (normed_ref, normed_o), (q_ref, q_o), (k_ref, k_o), (v_ref, v_o), (st_ref, st_o),
            (mixed_ref, mixed_o), (mid_ref, mid_o), (n2_ref, n2_o), (gu_ref, gu_o),
            (wqkv, wqkv_o), (wout, wout_o), (wgu, wgu_o), (wd, wd_o),
        ],
        sem_out,
    )
    query = lax.broadcasted_iota(jnp.int32, bias.shape, 0)
    key = lax.broadcasted_iota(jnp.int32, bias.shape, 1)
    bias[...] = jnp.where((key <= query) & (key < length[0]), 0.0, masked_score)
    x = x_ref[...]
    normed_ref[...] = (x * rms(x) * g_ref[0:1, :]).astype(bf16)
    saves[0].start()
    tail = key_rows - rows
    for ref in (q_ref, k_ref, v_ref):
        ref[rows:, :] = jnp.zeros((tail, D), bf16)
    arrive(0)
    saves[9].start()

    @pl.loop(0, 2)
    def _(part):
        acc = nn(normed_ref[...], wqkv[:, pl.ds(pl.multiple_of(part * D, D), D)])
        scale = jnp.where(part == 0, HEAD_DIM ** (-0.5), 1.0)
        for p in range(HEADS // 2):
            t = acc[:, p * PAIR : (p + 1) * PAIR]
            rot = ((t * cos_ref[...] + swap_halves(t) * sin_ref[...]) * scale).astype(bf16)

            @pl.when(part == 0)
            def _(p=p, rot=rot):
                q_ref[0:rows, p * PAIR : (p + 1) * PAIR] = rot

            @pl.when(part == 1)
            def _(p=p, rot=rot):
                k_ref[0:rows, p * PAIR : (p + 1) * PAIR] = rot

    v_ref[0:rows, :] = nn(normed_ref[...], wqkv[:, 2 * D :]).astype(bf16)
    for i in (1, 2, 3):
        saves[i].start()
    st_ref[...] = jnp.zeros(st_ref.shape, f32)

    @pl.loop(0, HEADS // 2)
    def _(p):
        cols = pl.ds(pl.multiple_of(p * PAIR, PAIR), PAIR)
        kp = k_ref[:, cols]
        vp = v_ref[:, cols]
        low = lax.broadcasted_iota(jnp.int32, kp.shape, 1) < HEAD_DIM
        keys = (jnp.where(low, kp, 0), jnp.where(low, 0, kp))
        values = (jnp.where(low, vp, 1), jnp.where(low, 1, vp))
        for q0, q1 in query_blocks(rows):
            kend = min(round_up(q1, BLOCK), key_rows)
            qp = q_ref[q0:q1, cols]
            mask = bias[q0:q1, :kend]
            parts = []
            tops = []
            for h in range(2):
                s = nt(qp, keys[h][:kend]) + mask
                top = jnp.max(s, -1, keepdims=True)
                e = jnp.exp(s - top).astype(bf16)
                parts.append(nn(e, values[h][:kend]))
                tops.append(top)
            lane = lax.broadcasted_iota(jnp.int32, parts[0].shape, 1)
            low_q = lane < HEAD_DIM
            total = pltpu.roll(jnp.where(low_q, parts[1], parts[0]), HEAD_DIM, 1)
            mixed_ref[q0:q1, cols] = (jnp.where(low_q, parts[0], parts[1]) / total).astype(bf16)
            log_total = jnp.log(total)
            other = pltpu.roll(log_total, HEAD_DIM, 1)
            first = tops[0] + jnp.where(low_q, log_total, other)
            second = tops[1] + jnp.where(low_q, other, log_total)
            old = st_ref[q0:q1, :]
            st_ref[q0:q1, :] = jnp.where(
                lane == 2 * p, first, jnp.where(lane == 2 * p + 1, second, old)
            )

    saves[4].start()
    saves[5].start()
    arrive(1)
    saves[10].start()
    middle = x_ref[...] + nn(mixed_ref[...], wout[...])
    mid_ref[...] = middle
    saves[6].start()
    n2_ref[...] = (middle * rms(middle) * g_ref[1:2, :]).astype(bf16)
    saves[7].start()
    arrive(2)
    saves[11].start()
    arrive(3)
    saves[12].start()
    xn_ref[...] = mid_ref[...]

    @pl.loop(0, FF // FF_STEP)
    def _(t):
        at = pl.multiple_of(t * FF_STEP, FF_STEP)
        gate = nn(n2_ref[...], wgu[:, pl.ds(at, FF_STEP)])
        up = nn(n2_ref[...], wgu[:, pl.ds(FF + at, FF_STEP)])
        act = (gate / (1.0 + jnp.exp(-gate)) * up).astype(bf16)
        gu_ref[:, pl.ds(at, FF_STEP)] = gate.astype(bf16)
        gu_ref[:, pl.ds(FF + at, FF_STEP)] = up.astype(bf16)
        xn_ref[...] += nn(act, wd[pl.ds(at, FF_STEP), :])

    saves[8].start()
    for save in saves:
        save.wait()


def put_tiles(places, m, grad, zones, outs, sem, i0, i1, j0, count_j):
    @pl.loop(i0, i1)
    def _(i):
        for jj in range(count_j):
            j = j0 + jj
            place = places[OFFSETS[m] + i * GRIDS[m][1] + j]
            tile = grad.at[
                pl.ds(pl.multiple_of(i * BLOCK, BLOCK), BLOCK),
                pl.ds(pl.multiple_of(j * BLOCK, BLOCK), BLOCK),
            ]
            start = 0
            for size, out in zip(zones, outs):
                if len(zones) == 1:
                    pltpu.make_async_copy(tile, out.at[place], sem).start()
                else:

                    @pl.when((place >= start) & (place < start + size))
                    def _(tile=tile, out=out, place=place, start=start):
                        pltpu.make_async_copy(tile, out.at[place - start], sem).start()

                start += size


def back_ffn_kernel(
    zones, begun, places, spare, back_ref, g_ref, mid_i, n2_i, gu_i, wgu_i, wd_i, *rest
):
    rest = rest[begun:]
    mid_ref_out, gain_ref = rest[:2]
    outs = rest[2 : 2 + len(zones)]
    mid_ref, n2_ref, gu_ref, wgu, wd, ggu, gd, big, zero, sem_in, sem_out, sem_zero = rest[2 + len(zones) :]
    loads = copies([(wd_i, wd), (gu_i, gu_ref), (n2_i, n2_ref), (wgu_i, wgu), (mid_i, mid_ref)], sem_in)
    for load in loads:
        load.start()
    spares = spare.shape[0] - 1
    if spares > 0:
        zero[...] = jnp.zeros(zero.shape, bf16)

        @pl.loop(0, spares)
        def _(i):
            pltpu.make_async_copy(zero, outs[0].at[spare[i]], sem_zero).start()

    big[...] = jnp.zeros(big.shape, f32)
    for load in loads[:4]:
        load.wait()
    put = functools.partial(put_tiles, places)

    @pl.loop(0, FF // FF_STEP)
    def _(t):
        at = pl.multiple_of(t * FF_STEP, FF_STEP)
        here = pl.ds(at, FF_STEP)
        there = pl.ds(FF + at, FF_STEP)
        back_ffn = back_ref[...].astype(bf16)
        d_act = nt(back_ffn, wd[here, :])
        gate = gu_ref[:, here].astype(f32)
        up = gu_ref[:, there].astype(f32)
        sig = 1.0 / (1.0 + jnp.exp(-gate))
        silu = gate * sig
        act = (silu * up).astype(bf16)
        d_gate = (d_act * up * (sig * (1.0 + gate * (1.0 - sig)))).astype(bf16)
        d_up = (d_act * silu).astype(bf16)
        gd[here, :] = tn(act, back_ffn).astype(bf16)
        ggu[:, here] = tn(n2_ref[...], d_gate).astype(bf16)
        ggu[:, there] = tn(n2_ref[...], d_up).astype(bf16)
        per = FF_STEP // BLOCK
        put(3, gd, zones, outs, sem_out.at[1], t * per, (t + 1) * per, 0, D // BLOCK)
        put(2, ggu, zones, outs, sem_out.at[0], 0, D // BLOCK, t * per, per)
        put(2, ggu, zones, outs, sem_out.at[0], 0, D // BLOCK, FF // BLOCK + t * per, per)
        big[...] += nt(d_gate, wgu[:, here]) + nt(d_up, wgu[:, there])

    loads[4].wait()
    step, gain = rms_back(big[...], mid_ref[...], g_ref[...])
    gain_ref[...] = gain
    mid_ref_out[...] = back_ref[...] + step
    pltpu.make_async_copy(ggu, ggu, sem_out.at[0]).wait()
    pltpu.make_async_copy(gd, gd, sem_out.at[1]).wait()
    if spares > 0:

        @pl.loop(0, spares)
        def _(i):
            pltpu.make_async_copy(zero, outs[0].at[spare[i]], sem_zero).wait()


def back_attention_kernel(
    zones, begun, places, length, back_ref, cos_ref, sin_ref,
    q_i, k_i, v_i, st_i, mixed_i, wout_i, *rest
):
    rest = rest[begun:]
    dproj = rest[0]
    outs = rest[1 : 1 + len(zones)]
    (
        q_ref, k_ref, v_ref, st_ref, mixed_ref, wout,
        gout, bias, turned, sums, mixed_back, sem_in, sem_out,
    ) = rest[1 + len(zones) :]
    rows = back_ref.shape[0]
    key_rows = q_ref.shape[0]
    loads = copies(
        [
            (wout_i, wout), (mixed_i, mixed_ref), (q_i, q_ref), (k_i, k_ref), (v_i, v_ref),
            (st_i, st_ref),
        ],
        sem_in,
    )
    for load in loads:
        load.start()
    put = functools.partial(put_tiles, places)
    key = lax.broadcasted_iota(jnp.int32, bias.shape, 0)
    query = lax.broadcasted_iota(jnp.int32, bias.shape, 1)
    bias[...] = jnp.where((key <= query) & (key < length[0]), 0.0, masked_score)
    back_attn = back_ref[...].astype(bf16)
    loads[0].wait()
    mixed_back[0:rows, :] = nt(back_attn, wout[...]).astype(bf16)
    mixed_back[rows:, :] = jnp.zeros((key_rows - rows, D), bf16)
    loads[1].wait()
    gout[...] = tn(mixed_ref[...], back_attn).astype(bf16)
    put(1, gout, zones, outs, sem_out, 0, D // BLOCK, 0, D // BLOCK)
    for load in loads[2:]:
        load.wait()
    levels = st_ref[...].T
    for h in range(HEADS):
        turned[h] = levels[h : h + 1, :]

    @pl.loop(0, HEADS // 2)
    def _(p):
        cols = pl.ds(pl.multiple_of(p * PAIR, PAIR), PAIR)
        low = lax.broadcasted_iota(jnp.int32, (key_rows, PAIR), 1) < HEAD_DIM

        def both(t):
            return (jnp.where(low, t, 0), jnp.where(low, 0, t))

        qp = q_ref[:, cols]
        op = mixed_back[:, cols]
        keys, values, queries, backs = both(k_ref[:, cols]), both(v_ref[:, cols]), both(qp), both(op)
        sums[...] = jnp.zeros(sums.shape, f32)
        for q0, q1 in query_blocks(key_rows):
            kend = q1
            d_query = jnp.zeros((q1 - q0, PAIR), f32)
            d_key = jnp.zeros((kend, PAIR), f32)
            d_value = jnp.zeros((kend, PAIR), f32)
            for h in range(2):
                level = turned[2 * p + h, :, q0:q1]
                soft = jnp.exp(nt(keys[h][:kend], qp[q0:q1]) + bias[:kend, q0:q1] - level)
                d_prob = nt(values[h][:kend], op[q0:q1])
                row_dot = jnp.sum(soft * d_prob, 0, keepdims=True)
                d_score = (soft * (d_prob - row_dot)).astype(bf16)
                d_value += nn(soft.astype(bf16), backs[h][q0:q1])
                d_key += nn(d_score, queries[h][q0:q1])
                d_query += tn(d_score, keys[h][:kend])
            sums[0, q0:q1, :] += d_query * HEAD_DIM ** (-0.5)
            sums[1, :kend, :] += d_key
            sums[2, :kend, :] += d_value
        for part in range(2):
            t = sums[part, 0:rows, :]
            dproj[:, pl.ds(pl.multiple_of(part * D + p * PAIR, PAIR), PAIR)] = (
                t * cos_ref[...] - swap_halves(t) * sin_ref[...]
            ).astype(bf16)
        dproj[:, pl.ds(pl.multiple_of(2 * D + p * PAIR, PAIR), PAIR)] = sums[2, 0:rows, :].astype(bf16)

    pltpu.make_async_copy(gout, gout, sem_out).wait()


def back_qkv_kernel(zones, begun, places, back_ref, g_ref, dproj, x_i, normed_i, wqkv_i, *rest):
    rest = rest[begun:]
    dx_ref, gain_ref = rest[:2]
    outs = rest[2 : 2 + len(zones)]
    x_ref, normed_ref, wqkv, gqkv, big, sem_in, sem_out = rest[2 + len(zones) :]
    loads = copies([(normed_i, normed_ref), (wqkv_i, wqkv), (x_i, x_ref)], sem_in)
    for load in loads:
        load.start()
    big[...] = jnp.zeros(big.shape, f32)
    loads[0].wait()
    loads[1].wait()

    @pl.loop(0, 3)
    def _(part):
        cols = pl.ds(pl.multiple_of(part * D, D), D)
        gqkv[:, cols] = tn(normed_ref[...], dproj[:, cols]).astype(bf16)
        put_tiles(
            places, 0, gqkv, zones, outs, sem_out, 0, D // BLOCK, part * (D // BLOCK), D // BLOCK
        )
        big[...] += nt(dproj[:, cols], wqkv[:, cols])

    loads[2].wait()
    step, gain = rms_back(big[...], x_ref[...], g_ref[...])
    gain_ref[...] = gain
    dx_ref[...] = back_ref[...] + step
    pltpu.make_async_copy(gqkv, gqkv, sem_out).wait()


def weight_shapes():
    return [(r * BLOCK, c * BLOCK) for r, c in GRIDS]


VMEM = pl.BlockSpec(memory_space=pltpu.VMEM)
SMEM = pl.BlockSpec(memory_space=pltpu.SMEM)
HBM = pl.BlockSpec(memory_space=pl.ANY)


def like(struct):
    return pltpu.VMEM(struct.shape, struct.dtype)


def cost(flops, bytes_accessed):
    return pl.CostEstimate(flops=flops, bytes_accessed=bytes_accessed, transcendentals=0)


def forward_layer(slots, length, x, gains, cos, sin, gathered):
    rows = x.shape[0]
    key_rows = round_up(rows, BLOCK)
    S = jax.ShapeDtypeStruct
    saved = [
        S((rows, D), bf16),
        S((key_rows, D), bf16),
        S((key_rows, D), bf16),
        S((key_rows, D), bf16),
        S((key_rows, BLOCK), f32),
        S((rows, D), bf16),
        S((rows, D), f32),
        S((rows, D), bf16),
        S((rows, 2 * FF), bf16),
    ] + [S(s, bf16) for s in weight_shapes()]
    return pl.pallas_call(
        forward_kernel,
        out_shape=[S((rows, D), f32)] + saved,
        in_specs=[SMEM, SMEM, VMEM, VMEM, VMEM, VMEM, HBM],
        out_specs=[VMEM] + [HBM] * 13,
        scratch_shapes=[like(s) for s in saved]
        + [
            pltpu.VMEM((rows, key_rows), f32),
            pltpu.SemaphoreType.DMA((4,)),
            pltpu.SemaphoreType.DMA((13,)),
        ],
        compiler_params=pltpu.CompilerParams(vmem_limit_bytes=VMEM_BYTES),
        cost_estimate=cost(2 * rows * PER_LAYER * BLOCK * BLOCK, 40 * 2**20),
        name="forward_block",
    )(slots, length, x, gains, cos, sin, gathered)


def tile_outputs(zones):
    return [jax.ShapeDtypeStruct((size, BLOCK, BLOCK), bf16) for size in zones]


def back_ffn(places, spare, back, gain, saved, zones, begun):
    rows = back.shape[0]
    S = jax.ShapeDtypeStruct
    args = (places, spare, back, gain) + tuple(saved)
    first = 2 + len(zones) - len(begun)
    wgu, wd = saved[3], saved[4]
    return pl.pallas_call(
        functools.partial(back_ffn_kernel, zones, len(begun)),
        out_shape=[S((rows, D), f32), S((1, D), f32)] + tile_outputs(zones),
        in_specs=[SMEM] * 2 + [VMEM] * 2 + [HBM] * (5 + len(begun)),
        out_specs=[VMEM, VMEM] + [HBM] * len(zones),
        input_output_aliases={len(args) + i: first + i for i in range(len(begun))},
        scratch_shapes=[like(s) for s in saved]
        + [like(wgu), like(wd)]
        + [
            pltpu.VMEM((rows, D), f32),
            pltpu.VMEM((BLOCK, BLOCK), bf16),
            pltpu.SemaphoreType.DMA((5,)),
            pltpu.SemaphoreType.DMA((2,)),
            pltpu.SemaphoreType.DMA,
        ],
        compiler_params=pltpu.CompilerParams(vmem_limit_bytes=VMEM_BYTES),
        cost_estimate=cost(4 * rows * (COUNTS[2] + COUNTS[3]) * BLOCK * BLOCK, 30 * 2**20),
        name="backward_feed_forward",
    )(*args, *begun)


def back_attention(places, length, back, cos, sin, saved, zones, begun):
    rows = back.shape[0]
    key_rows = round_up(rows, BLOCK)
    S = jax.ShapeDtypeStruct
    args = (places, length, back, cos, sin) + tuple(saved)
    first = 1 + len(zones) - len(begun)
    return pl.pallas_call(
        functools.partial(back_attention_kernel, zones, len(begun)),
        out_shape=[S((rows, 3 * D), bf16)] + tile_outputs(zones),
        in_specs=[SMEM] * 2 + [VMEM] * 3 + [HBM] * (6 + len(begun)),
        out_specs=[VMEM] + [HBM] * len(zones),
        input_output_aliases={len(args) + i: first + i for i in range(len(begun))},
        scratch_shapes=[like(s) for s in saved]
        + [
            like(saved[5]),
            pltpu.VMEM((key_rows, key_rows), f32),
            pltpu.VMEM((HEADS, 1, key_rows), f32),
            pltpu.VMEM((3, key_rows, PAIR), f32),
            pltpu.VMEM((key_rows, D), bf16),
            pltpu.SemaphoreType.DMA((6,)),
            pltpu.SemaphoreType.DMA,
        ],
        compiler_params=pltpu.CompilerParams(vmem_limit_bytes=VMEM_BYTES),
        cost_estimate=cost(4 * rows * COUNTS[1] * BLOCK * BLOCK + 20 * rows * rows * D, 30 * 2**20),
        name="backward_attention",
    )(*args, *begun)


def back_qkv(places, back, gain, d_projected, saved, zones, begun):
    rows = back.shape[0]
    S = jax.ShapeDtypeStruct
    args = (places, back, gain, d_projected) + tuple(saved)
    first = 2 + len(zones) - len(begun)
    return pl.pallas_call(
        functools.partial(back_qkv_kernel, zones, len(begun)),
        out_shape=[S((rows, D), f32), S((1, D), f32)] + tile_outputs(zones),
        in_specs=[SMEM] + [VMEM] * 3 + [HBM] * (3 + len(begun)),
        out_specs=[VMEM, VMEM] + [HBM] * len(zones),
        input_output_aliases={len(args) + i: first + i for i in range(len(begun))},
        scratch_shapes=[like(s) for s in saved]
        + [
            like(saved[2]),
            pltpu.VMEM((rows, D), f32),
            pltpu.SemaphoreType.DMA((3,)),
            pltpu.SemaphoreType.DMA,
        ],
        compiler_params=pltpu.CompilerParams(vmem_limit_bytes=VMEM_BYTES),
        cost_estimate=cost(4 * rows * COUNTS[0] * BLOCK * BLOCK, 20 * 2**20),
        name="backward_qkv",
    )(*args, *begun)


def optimizer_kernel(factor, rank, g_ref, m_ref, s_ref, r_ref, wg_ref, ns_ref, nm_ref, nc_ref):
    f = factor[0]
    count = m_ref.shape[0]
    for i in range(count):
        gb = g_ref[rank[pl.program_id(0) * count + i]]
        wg_ref[i] = gb.astype(f32) * f
        half = (1.0 - decay_rate) * f * f
        ns_ref[i, 0] = decay_rate * s_ref[i, 0] + half * nt(gb, gb)
        ns_ref[i, 1] = decay_rate * s_ref[i, 1] + half * tn(gb, gb)
        left = nn(r_ref[i, 0].astype(bf16), (gb.astype(f32) * f).astype(bf16)).astype(bf16)
        new = m_ref[i] - step_rate * nn(left, r_ref[i, 1].astype(bf16))
        nm_ref[i] = new
        nc_ref[i] = new.astype(bf16)


def optimizer(factor, rank, owned, master, statistics, inverse_roots):
    count = owned.shape[0]
    per = max(n for n in range(1, 13) if count % n == 0)
    S = jax.ShapeDtypeStruct
    one = pl.BlockSpec((per, BLOCK, BLOCK), lambda i: (i, 0, 0))
    two = pl.BlockSpec((per, 2, BLOCK, BLOCK), lambda i: (i, 0, 0, 0))
    return pl.pallas_call(
        optimizer_kernel,
        grid=(count // per,),
        out_shape=[
            S(master.shape, f32),
            S(statistics.shape, f32),
            S(master.shape, f32),
            S(master.shape, bf16),
        ],
        in_specs=[SMEM, SMEM, VMEM, one, two, two],
        out_specs=[one, two, one, one],
        compiler_params=pltpu.CompilerParams(vmem_limit_bytes=VMEM_BYTES),
        name="optimizer",
    )(factor, rank, owned, master, statistics, inverse_roots)


def to_images(local, bands, band):
    images, band_rows = local.shape[0], local.shape[-2]
    padded = jnp.concatenate([local, jnp.zeros((bands - images,) + local.shape[1:], local.dtype)], 0)
    whole = jnp.zeros((bands,) + local.shape[1:], local.dtype)
    for shift in range(bands):
        block = lax.dynamic_index_in_dim(padded, (band + shift) % bands, 0, keepdims=False)
        if shift > 0:
            pairs = [(b, (b + shift) % bands) for b in range(bands) if (b + shift) % bands < images]
            block = lax.ppermute(block, "band", pairs)
        whole = lax.dynamic_update_index_in_dim(whole, block, (band - shift) % bands, 0)
    return whole


def to_bands(whole, images, bands, band):
    local = jnp.zeros(whole.shape, whole.dtype)
    for shift in range(bands):
        block = lax.dynamic_index_in_dim(whole, (band + shift) % bands, 0, keepdims=False)
        if shift > 0:
            pairs = [(b, (b + shift) % bands) for b in range(images)]
            block = lax.ppermute(block, "band", pairs)
        local = lax.dynamic_update_index_in_dim(local, block, (band - shift) % bands, 0)
    return local[:images]


EARLY = 38
LATE = (30, 24, 16)


def relative_places(slot_of_block, per_owner, me):
    blocks = slot_of_block.shape[0]
    block_of_slot = jnp.zeros((blocks,), jnp.int32).at[slot_of_block].set(
        jnp.arange(blocks, dtype=jnp.int32)
    )
    by_owner = block_of_slot.reshape(-1, per_owner)
    rank = jnp.sum(by_owner[:, None, :] < by_owner[:, :, None], -1, dtype=jnp.int32)
    early = per_owner - EARLY
    clean = jnp.all(jnp.where(rank >= early, by_owner >= PER_LAYER, True))
    relative = (jnp.arange(by_owner.shape[0], dtype=jnp.int32) ^ me)[:, None]
    core, x, y = relative % 2, relative // 2 % 2, relative // 4
    place = jnp.zeros_like(rank)
    zone_sizes = (4 * EARLY, 4 * EARLY, 4 * early, 4 * early)
    chunks = [(early, EARLY, 0, 0)]
    start = 0
    for size in LATE:
        chunks.append((start, size, 2, 4 * start))
        start += size
    for start, size, zone, inside in chunks:
        half = size // 2
        at = rank - start
        spot = jnp.where(at < half, (x * 2 + y) * half + at, 4 * half + (y * 2 + x) * half + at - half)
        base = jnp.where(core == 0, sum(zone_sizes[:zone]), sum(zone_sizes[: zone + 1]))
        place = jnp.where((at >= 0) & (at < size), base + inside + spot, place)
    return place.reshape(-1)[slot_of_block], rank, clean, zone_sizes


CORE = [(i, i ^ 1) for i in range(8)]
ALONG_X = [(i, i ^ 2) for i in range(8)]
ALONG_Y = [(i, i ^ 4) for i in range(8)]


def wide(t, lo, hi):
    return t[lo:hi].astype(f32)


def plane_start(kept, received, gate=None, beside=None):
    half = kept.shape[0] // 8

    def chip(lo, hi):
        return wide(kept, lo * half, hi * half) + wide(received, lo * half, hi * half)

    send_x, send_y = chip(2, 4).astype(bf16), chip(6, 8).astype(bf16)
    if gate is not None:
        send_x, send_y, _ = lax.optimization_barrier((send_x, send_y, gate))
    if beside is not None:
        send_x, send_y, beside = lax.optimization_barrier((send_x, send_y, beside))
    going = (chip, half, lax.ppermute(send_x, "dp", ALONG_X), lax.ppermute(send_y, "dp", ALONG_Y))
    return going if beside is None else (going, beside)


def plane_turn(chip, half, from_x, from_y):
    send_y = (chip(1, 2) + wide(from_x, half, 2 * half)).astype(bf16)
    send_x = (chip(5, 6) + wide(from_y, half, 2 * half)).astype(bf16)
    return lax.ppermute(send_x, "dp", ALONG_X), lax.ppermute(send_y, "dp", ALONG_Y)


def plane_end(chip, half, from_x, from_y, later_x, later_y):
    one = chip(0, 1) + wide(from_x, 0, half) + later_y.astype(f32)
    two = chip(4, 5) + wide(from_y, 0, half) + later_x.astype(f32)
    return jnp.concatenate([one, two], 0).astype(bf16)


def sum_bands(plane, band):
    kind = plane.dtype
    up = lax.ppermute(plane, "band", [(0, 1)])
    down = lax.ppermute(plane, "band", [(2, 1)])
    total = (plane.astype(f32) + up.astype(f32) + down.astype(f32)).astype(kind)
    to_first = lax.ppermute(total, "band", [(1, 0)])
    to_third = lax.ppermute(total, "band", [(1, 2)])
    to_last = lax.ppermute(to_third, "band", [(2, 3)])
    total = jnp.where(band == 0, to_first, total)
    total = jnp.where(band == 2, to_third, total)
    return jnp.where(band == 3, to_last, total)


def rope_tables(rows):
    half = HEAD_DIM // 2
    frequency = rope_base ** (-(jnp.arange(half, dtype=f32) * 2.0 / HEAD_DIM))
    angles = jnp.arange(rows, dtype=jnp.int32).astype(f32)[:, None] * frequency[None, :]
    cosine, sine = jnp.cos(angles), jnp.sin(angles)
    return jnp.tile(cosine, (1, 4)), jnp.tile(jnp.concatenate([-sine, sine], 1), (1, 2))


def shards(
    tokens,
    cotangent,
    lengths,
    slot_of_block,
    master,
    statistics,
    inverse_roots,
    gain_values,
    gain_moments,
):
    images, band_rows, _ = tokens.shape
    band = lax.axis_index("band")
    bands = lax.axis_size("band")
    seq = band_rows * bands
    rows = round_up(seq, 16)
    gathered = lax.all_gather(master.astype(bf16), "dp", axis=0, tiled=True)
    slot_count = gathered.shape[0]

    arrived = to_images(jnp.stack([tokens, cotangent], 1), bands, band)
    token_rows = jnp.pad(arrived[:, 0].reshape(seq, D), ((0, rows - seq), (0, 0)))
    back_rows = jnp.pad(arrived[:, 1].reshape(seq, D), ((0, rows - seq), (0, 0)))
    length = lengths[jnp.minimum(band, images - 1)]
    valid = (jnp.arange(rows, dtype=jnp.int32) < length).astype(f32)
    length = length.reshape(1)
    cos, sin = rope_tables(rows)

    spare_count = slot_count - slot_of_block.shape[0]
    spare = jnp.zeros((1,), jnp.int32)
    if spare_count > 0:
        used = jnp.zeros((slot_count,), jnp.int32).at[slot_of_block].set(1)
        spare = jnp.concatenate([jnp.argsort(used)[:spare_count].astype(jnp.int32), spare])

    hidden = token_rows.astype(f32)
    inputs, saves = [], []
    for layer in range(LAYERS):
        slots = slot_of_block[layer * PER_LAYER : (layer + 1) * PER_LAYER]
        gains = gain_values[2 * layer : 2 * layer + 2]
        inputs.append(hidden)
        hidden, *saved = forward_layer(slots, length, hidden, gains, cos, sin, gathered)
        saves.append(saved)
    layer_output = to_bands(
        hidden[:seq].astype(bf16).reshape(bands, band_rows, D), images, bands, band
    )

    back = back_rows.astype(f32) * valid[:, None]
    per_owner = master.shape[0]
    me = lax.axis_index("dp")
    by_permutes = (
        lax.axis_size("dp") == 8
        and bands == 4
        and images == 3
        and slot_count == slot_of_block.shape[0]
        and per_owner == EARLY + sum(LATE)
    )
    if by_permutes:
        places, ranks, clean, sizes = relative_places(slot_of_block, per_owner, me)
        rank = lax.dynamic_index_in_dim(ranks, me, 0, keepdims=False)
        zones_top, zones_bottom = sizes, (sizes[0] + sizes[1],) + sizes[2:]
    else:
        places, rank = slot_of_block, jnp.arange(per_owner, dtype=jnp.int32)
        zones_top = zones_bottom = (slot_count,)

    def backward(layer, back, zones, tiles, ahead=lambda back: back, later=lambda back: back):
        normed, q, k, v, st, mixed, mid, n2, gu, wqkv, wout, wgu, wd = saves[layer]
        slots = places[layer * PER_LAYER : (layer + 1) * PER_LAYER]
        fill = spare if layer == LAYERS - 1 else spare[-1:]
        back, gain_two, *tiles = back_ffn(
            slots, fill, back, gain_values[2 * layer + 1 : 2 * layer + 2], (mid, n2, gu, wgu, wd),
            zones, tiles,
        )
        back = ahead(back)
        d_projected, *tiles = back_attention(
            slots, length, back, cos, sin, (q, k, v, st, mixed, wout), zones, tiles
        )
        back = later(back)
        back, gain_one, *tiles = back_qkv(
            slots, back, gain_values[2 * layer : 2 * layer + 1], d_projected,
            (inputs[layer], normed, wqkv), zones, tiles,
        )
        return back, [gain_one, gain_two], tiles

    def after(value, *done):
        return lax.optimization_barrier((value,) + done)[0]

    back, gains_top, tiles = backward(1, back, zones_top, [])
    if by_permutes:
        early_kept, early_sent, kept, sent = tiles
        early = {"output": layer_output}
        early["core"] = lax.ppermute(early_sent, "dp", CORE)

        def ahead(back):
            back, early["output"] = lax.optimization_barrier((back, early["output"]))
            early["plane"], back = plane_start(early_kept, early["core"], beside=back)
            return back

        def later(back):
            chip, half, from_x, from_y = early["plane"]
            back, from_x, from_y = lax.optimization_barrier((back, from_x, from_y))
            early["plane"] = (chip, half, from_x, from_y)
            return back

        back, gains_bottom, tiles = backward(0, back, zones_bottom, [kept, sent], ahead, later)
        layer_output = early["output"]
        early_late, kept, sent = tiles
        chunks, start = [], 0
        for size in LATE:
            chunks.append((kept[4 * start : 4 * (start + size)], sent[4 * start : 4 * (start + size)]))
            start += size
        from_core = [lax.ppermute(chunk[1], "dp", CORE) for chunk in chunks]
        turned = plane_turn(*early["plane"])
        gate = turned
        owned = [None] * len(chunks) + [sum_bands(plane_end(*early["plane"], *turned), band)]
        gain_total = sum_bands(jnp.concatenate(gains_bottom + gains_top, 0), band)
        for i, (chunk, received) in enumerate(zip(chunks, from_core)):
            going = plane_start(chunk[0], received, gate)
            gate = plane_turn(*going)
            owned[i] = sum_bands(plane_end(*going, *gate), band)
            if i == 0:
                back = after(back, going[2], going[3])

        order = jnp.argsort(places)[: sizes[0] + sizes[1]]

        def again(trip, total):
            _, late, first, second = lax.optimization_barrier(
                (trip, early_late, early_kept, early_sent)
            )
            mine = (order < PER_LAYER)[:, None, None]
            first = jnp.where(mine[: sizes[0]], late[: sizes[0]], first)
            second = jnp.where(mine[sizes[0] :], late[sizes[0] :], second)
            going = plane_start(first, lax.ppermute(second, "dp", CORE))
            return sum_bands(plane_end(*going, *plane_turn(*going)), band)

        owned[-1] = lax.fori_loop(0, jnp.where(clean, 0, 1), again, owned[-1])
        owned = jnp.concatenate(owned, 0)
    else:
        back, gains_bottom, tiles = backward(0, back, zones_bottom, tiles)
        owned = lax.psum_scatter(tiles[0], "dp", scatter_dimension=0, tiled=True)
        owned = lax.psum(owned, "band")
        gain_total = lax.psum(jnp.concatenate(gains_bottom + gains_top, 0), "band")
    input_grad = to_bands(back[:seq].astype(bf16).reshape(bands, band_rows, D), images, bands, band)

    owned_f = owned.astype(f32)
    squares = jnp.sum(owned_f * owned_f).reshape(1)
    summed = lax.psum(jnp.concatenate([gain_total.reshape(-1), squares]), "dp")
    gain_total = summed[:-1].reshape(gain_values.shape)
    owned_squares = summed[-1]
    grad_norm = jnp.sqrt(owned_squares + jnp.sum(gain_total * gain_total))
    factor = jnp.minimum(1.0, clip_limit / grad_norm)
    weight_grads, new_statistics, new_master, master_copy = optimizer(
        factor.reshape(1), rank, owned, master, statistics, inverse_roots
    )
    gain_grads = gain_total * factor
    new_moments = decay_rate * gain_moments + (1.0 - decay_rate) * gain_grads * gain_grads
    new_gains = gain_values - gain_rate * gain_grads / (jnp.sqrt(new_moments) + epsilon)
    return (
        layer_output,
        input_grad,
        weight_grads,
        grad_norm,
        new_statistics,
        new_master,
        master_copy,
        gain_grads,
        new_moments,
        new_gains,
    )


def solution(mesh):
    return jax.shard_map(
        shards,
        mesh=mesh,
        in_specs=(
            P("dp", "band", None),
            P("dp", "band", None),
            P("dp"),
            P(),
            P("dp", None, None),
            P("dp", None, None, None),
            P("dp", None, None, None),
            P(),
            P(),
        ),
        out_specs=(
            P("dp", "band", None),
            P("dp", "band", None),
            P("dp", None, None),
            P(),
            P("dp", None, None, None),
            P("dp", None, None),
            P("dp", None, None),
            P(),
            P(),
            P(),
        ),
        check_vma=False,
    )
```

```python
import functools

import jax
import jax.numpy as jnp
from jax import lax
from jax.experimental import pallas as pl
from jax.experimental.pallas import tpu as pltpu
from jax.sharding import PartitionSpec as P

D = 768
HEADS = 12
HEAD_DIM = 64
FF = 2048
LAYERS = 2
BLOCK = 128
PAIR = 2 * HEAD_DIM

epsilon = 1e-05
rope_base = 10000.0
decay_rate = 0.5
step_rate = 0.4
gain_rate = 0.2
clip_limit = 1.0
masked_score = -1e30
VMEM_BYTES = 62 * 2**20

f32 = jnp.float32
bf16 = jnp.bfloat16

GRIDS = [
    (D // BLOCK, 3 * D // BLOCK),
    (D // BLOCK, D // BLOCK),
    (D // BLOCK, 2 * FF // BLOCK),
    (FF // BLOCK, D // BLOCK),
]
COUNTS = [r * c for r, c in GRIDS]
OFFSETS = [sum(COUNTS[:i]) for i in range(4)]
PER_LAYER = sum(COUNTS)
FF_STEP = 512


def round_up(n, m):
    return -(-n // m) * m


def nn(a, b):
    return lax.dot_general(a, b, (((1,), (0,)), ((), ())), preferred_element_type=f32)


def nt(a, b):
    return lax.dot_general(a, b, (((1,), (1,)), ((), ())), preferred_element_type=f32)


def tn(a, b):
    return lax.dot_general(a, b, (((0,), (0,)), ((), ())), preferred_element_type=f32)


def query_blocks(rows, step=256):
    return [(s, min(s + step, rows)) for s in range(0, rows, step)]


def swap_halves(t):
    lane = lax.broadcasted_iota(jnp.int32, t.shape, 1)
    half = HEAD_DIM // 2
    return jnp.where(lane % HEAD_DIM < half, pltpu.roll(t, PAIR - half, 1), pltpu.roll(t, half, 1))


def rms(m):
    return lax.rsqrt(jnp.mean(m * m, -1, keepdims=True) + epsilon)


def rms_back(u, m, g):
    r = rms(m)
    t = u * g
    dot = jnp.mean(t * m, -1, keepdims=True)
    return r * t - m * (r * r * r * dot), jnp.sum(u * m * r, 0, keepdims=True)


def copies(pairs, sem):
    return [pltpu.make_async_copy(src, dst, sem.at[i]) for i, (src, dst) in enumerate(pairs)]


def forward_kernel(
    slots, length, x_ref, g_ref, cos_ref, sin_ref, w_hbm,
    xn_ref, normed_o, q_o, k_o, v_o, st_o, mixed_o, mid_o, n2_o, gu_o, wqkv_o, wout_o, wgu_o, wd_o,
    normed_ref, q_ref, k_ref, v_ref, st_ref, mixed_ref, mid_ref, n2_ref, gu_ref,
    wqkv, wout, wgu, wd, bias, sem_in, sem_out,
):
    rows = x_ref.shape[0]
    key_rows = q_ref.shape[0]
    held = (wqkv, wout, wgu, wd)
    for m in range(4):
        tile_rows, tile_cols = GRIDS[m]

        @pl.loop(0, tile_rows)
        def _(i, m=m, tile_cols=tile_cols):
            for j in range(tile_cols):
                slot = slots[OFFSETS[m] + i * tile_cols + j]
                pltpu.make_async_copy(
                    w_hbm.at[slot],
                    held[m].at[pl.ds(pl.multiple_of(i * BLOCK, BLOCK), BLOCK), pl.ds(j * BLOCK, BLOCK)],
                    sem_in.at[m],
                ).start()

    def arrive(m):
        pltpu.make_async_copy(held[m], held[m], sem_in.at[m]).wait()

    saves = copies(
        [
            (normed_ref, normed_o), (q_ref, q_o), (k_ref, k_o), (v_ref, v_o), (st_ref, st_o),
            (mixed_ref, mixed_o), (mid_ref, mid_o), (n2_ref, n2_o), (gu_ref, gu_o),
            (wqkv, wqkv_o), (wout, wout_o), (wgu, wgu_o), (wd, wd_o),
        ],
        sem_out,
    )
    query = lax.broadcasted_iota(jnp.int32, bias.shape, 0)
    key = lax.broadcasted_iota(jnp.int32, bias.shape, 1)
    bias[...] = jnp.where((key <= query) & (key < length[0]), 0.0, masked_score)
    x = x_ref[...]
    normed_ref[...] = (x * rms(x) * g_ref[0:1, :]).astype(bf16)
    saves[0].start()
    tail = key_rows - rows
    for ref in (q_ref, k_ref, v_ref):
        ref[rows:, :] = jnp.zeros((tail, D), bf16)
    arrive(0)
    saves[9].start()

    @pl.loop(0, 2)
    def _(part):
        acc = nn(normed_ref[...], wqkv[:, pl.ds(pl.multiple_of(part * D, D), D)])
        scale = jnp.where(part == 0, HEAD_DIM ** (-0.5), 1.0)
        for p in range(HEADS // 2):
            t = acc[:, p * PAIR : (p + 1) * PAIR]
            rot = ((t * cos_ref[...] + swap_halves(t) * sin_ref[...]) * scale).astype(bf16)

            @pl.when(part == 0)
            def _(p=p, rot=rot):
                q_ref[0:rows, p * PAIR : (p + 1) * PAIR] = rot

            @pl.when(part == 1)
            def _(p=p, rot=rot):
                k_ref[0:rows, p * PAIR : (p + 1) * PAIR] = rot

    v_ref[0:rows, :] = nn(normed_ref[...], wqkv[:, 2 * D :]).astype(bf16)
    for i in (1, 2, 3):
        saves[i].start()
    st_ref[...] = jnp.zeros(st_ref.shape, f32)

    @pl.loop(0, HEADS // 2)
    def _(p):
        cols = pl.ds(pl.multiple_of(p * PAIR, PAIR), PAIR)
        kp = k_ref[:, cols]
        vp = v_ref[:, cols]
        low = lax.broadcasted_iota(jnp.int32, kp.shape, 1) < HEAD_DIM
        keys = (jnp.where(low, kp, 0), jnp.where(low, 0, kp))
        values = (jnp.where(low, vp, 1), jnp.where(low, 1, vp))
        for q0, q1 in query_blocks(rows):
            kend = min(round_up(q1, BLOCK), key_rows)
            qp = q_ref[q0:q1, cols]
            mask = bias[q0:q1, :kend]
            parts = []
            tops = []
            for h in range(2):
                s = nt(qp, keys[h][:kend]) + mask
                top = jnp.max(s, -1, keepdims=True)
                e = jnp.exp(s - top).astype(bf16)
                parts.append(nn(e, values[h][:kend]))
                tops.append(top)
            lane = lax.broadcasted_iota(jnp.int32, parts[0].shape, 1)
            low_q = lane < HEAD_DIM
            total = pltpu.roll(jnp.where(low_q, parts[1], parts[0]), HEAD_DIM, 1)
            mixed_ref[q0:q1, cols] = (jnp.where(low_q, parts[0], parts[1]) / total).astype(bf16)
            log_total = jnp.log(total)
            other = pltpu.roll(log_total, HEAD_DIM, 1)
            first = tops[0] + jnp.where(low_q, log_total, other)
            second = tops[1] + jnp.where(low_q, other, log_total)
            old = st_ref[q0:q1, :]
            st_ref[q0:q1, :] = jnp.where(
                lane == 2 * p, first, jnp.where(lane == 2 * p + 1, second, old)
            )

    saves[4].start()
    saves[5].start()
    arrive(1)
    saves[10].start()
    middle = x_ref[...] + nn(mixed_ref[...], wout[...])
    mid_ref[...] = middle
    saves[6].start()
    n2_ref[...] = (middle * rms(middle) * g_ref[1:2, :]).astype(bf16)
    saves[7].start()
    arrive(2)
    saves[11].start()
    arrive(3)
    saves[12].start()
    xn_ref[...] = mid_ref[...]

    @pl.loop(0, FF // FF_STEP)
    def _(t):
        at = pl.multiple_of(t * FF_STEP, FF_STEP)
        gate = nn(n2_ref[...], wgu[:, pl.ds(at, FF_STEP)])
        up = nn(n2_ref[...], wgu[:, pl.ds(FF + at, FF_STEP)])
        act = (gate / (1.0 + jnp.exp(-gate)) * up).astype(bf16)
        gu_ref[:, pl.ds(at, FF_STEP)] = gate.astype(bf16)
        gu_ref[:, pl.ds(FF + at, FF_STEP)] = up.astype(bf16)
        xn_ref[...] += nn(act, wd[pl.ds(at, FF_STEP), :])

    saves[8].start()
    for save in saves:
        save.wait()


def put_tiles(places, m, grad, zones, outs, sem, i0, i1, j0, count_j):
    @pl.loop(i0, i1)
    def _(i):
        for jj in range(count_j):
            j = j0 + jj
            place = places[OFFSETS[m] + i * GRIDS[m][1] + j]
            tile = grad.at[
                pl.ds(pl.multiple_of(i * BLOCK, BLOCK), BLOCK),
                pl.ds(pl.multiple_of(j * BLOCK, BLOCK), BLOCK),
            ]
            start = 0
            for size, out in zip(zones, outs):
                if len(zones) == 1:
                    pltpu.make_async_copy(tile, out.at[place], sem).start()
                else:

                    @pl.when((place >= start) & (place < start + size))
                    def _(tile=tile, out=out, place=place, start=start):
                        pltpu.make_async_copy(tile, out.at[place - start], sem).start()

                start += size


def back_ffn_kernel(
    zones, begun, places, spare, back_ref, g_ref, mid_i, n2_i, gu_i, wgu_i, wd_i, *rest
):
    rest = rest[begun:]
    mid_ref_out, gain_ref = rest[:2]
    outs = rest[2 : 2 + len(zones)]
    mid_ref, n2_ref, gu_ref, wgu, wd, ggu, gd, big, zero, sem_in, sem_out, sem_zero = rest[2 + len(zones) :]
    loads = copies([(wd_i, wd), (gu_i, gu_ref), (n2_i, n2_ref), (wgu_i, wgu), (mid_i, mid_ref)], sem_in)
    for load in loads:
        load.start()
    spares = spare.shape[0] - 1
    if spares > 0:
        zero[...] = jnp.zeros(zero.shape, bf16)

        @pl.loop(0, spares)
        def _(i):
            pltpu.make_async_copy(zero, outs[0].at[spare[i]], sem_zero).start()

    big[...] = jnp.zeros(big.shape, f32)
    for load in loads[:4]:
        load.wait()
    put = functools.partial(put_tiles, places)

    @pl.loop(0, FF // FF_STEP)
    def _(t):
        at = pl.multiple_of(t * FF_STEP, FF_STEP)
        here = pl.ds(at, FF_STEP)
        there = pl.ds(FF + at, FF_STEP)
        back_ffn = back_ref[...].astype(bf16)
        d_act = nt(back_ffn, wd[here, :])
        gate = gu_ref[:, here].astype(f32)
        up = gu_ref[:, there].astype(f32)
        sig = 1.0 / (1.0 + jnp.exp(-gate))
        silu = gate * sig
        act = (silu * up).astype(bf16)
        d_gate = (d_act * up * (sig * (1.0 + gate * (1.0 - sig)))).astype(bf16)
        d_up = (d_act * silu).astype(bf16)
        gd[here, :] = tn(act, back_ffn).astype(bf16)
        ggu[:, here] = tn(n2_ref[...], d_gate).astype(bf16)
        ggu[:, there] = tn(n2_ref[...], d_up).astype(bf16)
        per = FF_STEP // BLOCK
        put(3, gd, zones, outs, sem_out.at[1], t * per, (t + 1) * per, 0, D // BLOCK)
        put(2, ggu, zones, outs, sem_out.at[0], 0, D // BLOCK, t * per, per)
        put(2, ggu, zones, outs, sem_out.at[0], 0, D // BLOCK, FF // BLOCK + t * per, per)
        big[...] += nt(d_gate, wgu[:, here]) + nt(d_up, wgu[:, there])

    loads[4].wait()
    step, gain = rms_back(big[...], mid_ref[...], g_ref[...])
    gain_ref[...] = gain
    mid_ref_out[...] = back_ref[...] + step
    pltpu.make_async_copy(ggu, ggu, sem_out.at[0]).wait()
    pltpu.make_async_copy(gd, gd, sem_out.at[1]).wait()
    if spares > 0:

        @pl.loop(0, spares)
        def _(i):
            pltpu.make_async_copy(zero, outs[0].at[spare[i]], sem_zero).wait()


def back_attention_kernel(
    zones, begun, places, length, back_ref, cos_ref, sin_ref,
    q_i, k_i, v_i, st_i, mixed_i, wout_i, *rest
):
    rest = rest[begun:]
    dproj = rest[0]
    outs = rest[1 : 1 + len(zones)]
    (
        q_ref, k_ref, v_ref, st_ref, mixed_ref, wout,
        gout, bias, turned, sums, mixed_back, sem_in, sem_out,
    ) = rest[1 + len(zones) :]
    rows = back_ref.shape[0]
    key_rows = q_ref.shape[0]
    loads = copies(
        [
            (wout_i, wout), (mixed_i, mixed_ref), (q_i, q_ref), (k_i, k_ref), (v_i, v_ref),
            (st_i, st_ref),
        ],
        sem_in,
    )
    for load in loads:
        load.start()
    put = functools.partial(put_tiles, places)
    key = lax.broadcasted_iota(jnp.int32, bias.shape, 0)
    query = lax.broadcasted_iota(jnp.int32, bias.shape, 1)
    bias[...] = jnp.where((key <= query) & (key < length[0]), 0.0, masked_score)
    back_attn = back_ref[...].astype(bf16)
    loads[0].wait()
    mixed_back[0:rows, :] = nt(back_attn, wout[...]).astype(bf16)
    mixed_back[rows:, :] = jnp.zeros((key_rows - rows, D), bf16)
    loads[1].wait()
    gout[...] = tn(mixed_ref[...], back_attn).astype(bf16)
    put(1, gout, zones, outs, sem_out, 0, D // BLOCK, 0, D // BLOCK)
    for load in loads[2:]:
        load.wait()
    levels = st_ref[...].T
    for h in range(HEADS):
        turned[h] = levels[h : h + 1, :]

    @pl.loop(0, HEADS // 2)
    def _(p):
        cols = pl.ds(pl.multiple_of(p * PAIR, PAIR), PAIR)
        low = lax.broadcasted_iota(jnp.int32, (key_rows, PAIR), 1) < HEAD_DIM

        def both(t):
            return (jnp.where(low, t, 0), jnp.where(low, 0, t))

        qp = q_ref[:, cols]
        op = mixed_back[:, cols]
        keys, values, queries, backs = both(k_ref[:, cols]), both(v_ref[:, cols]), both(qp), both(op)
        sums[...] = jnp.zeros(sums.shape, f32)
        for q0, q1 in query_blocks(key_rows):
            kend = q1
            d_query = jnp.zeros((q1 - q0, PAIR), f32)
            d_key = jnp.zeros((kend, PAIR), f32)
            d_value = jnp.zeros((kend, PAIR), f32)
            for h in range(2):
                level = turned[2 * p + h, :, q0:q1]
                soft = jnp.exp(nt(keys[h][:kend], qp[q0:q1]) + bias[:kend, q0:q1] - level)
                d_prob = nt(values[h][:kend], op[q0:q1])
                row_dot = jnp.sum(soft * d_prob, 0, keepdims=True)
                d_score = (soft * (d_prob - row_dot)).astype(bf16)
                d_value += nn(soft.astype(bf16), backs[h][q0:q1])
                d_key += nn(d_score, queries[h][q0:q1])
                d_query += tn(d_score, keys[h][:kend])
            sums[0, q0:q1, :] += d_query * HEAD_DIM ** (-0.5)
            sums[1, :kend, :] += d_key
            sums[2, :kend, :] += d_value
        for part in range(2):
            t = sums[part, 0:rows, :]
            dproj[:, pl.ds(pl.multiple_of(part * D + p * PAIR, PAIR), PAIR)] = (
                t * cos_ref[...] - swap_halves(t) * sin_ref[...]
            ).astype(bf16)
        dproj[:, pl.ds(pl.multiple_of(2 * D + p * PAIR, PAIR), PAIR)] = sums[2, 0:rows, :].astype(bf16)

    pltpu.make_async_copy(gout, gout, sem_out).wait()


def back_qkv_kernel(zones, begun, places, back_ref, g_ref, dproj, x_i, normed_i, wqkv_i, *rest):
    rest = rest[begun:]
    dx_ref, gain_ref = rest[:2]
    outs = rest[2 : 2 + len(zones)]
    x_ref, normed_ref, wqkv, gqkv, big, sem_in, sem_out = rest[2 + len(zones) :]
    loads = copies([(normed_i, normed_ref), (wqkv_i, wqkv), (x_i, x_ref)], sem_in)
    for load in loads:
        load.start()
    big[...] = jnp.zeros(big.shape, f32)
    loads[0].wait()
    loads[1].wait()

    @pl.loop(0, 3)
    def _(part):
        cols = pl.ds(pl.multiple_of(part * D, D), D)
        gqkv[:, cols] = tn(normed_ref[...], dproj[:, cols]).astype(bf16)
        put_tiles(
            places, 0, gqkv, zones, outs, sem_out, 0, D // BLOCK, part * (D // BLOCK), D // BLOCK
        )
        big[...] += nt(dproj[:, cols], wqkv[:, cols])

    loads[2].wait()
    step, gain = rms_back(big[...], x_ref[...], g_ref[...])
    gain_ref[...] = gain
    dx_ref[...] = back_ref[...] + step
    pltpu.make_async_copy(gqkv, gqkv, sem_out).wait()


def weight_shapes():
    return [(r * BLOCK, c * BLOCK) for r, c in GRIDS]


VMEM = pl.BlockSpec(memory_space=pltpu.VMEM)
SMEM = pl.BlockSpec(memory_space=pltpu.SMEM)
HBM = pl.BlockSpec(memory_space=pl.ANY)


def like(struct):
    return pltpu.VMEM(struct.shape, struct.dtype)


def cost(flops, bytes_accessed):
    return pl.CostEstimate(flops=flops, bytes_accessed=bytes_accessed, transcendentals=0)


def forward_layer(slots, length, x, gains, cos, sin, gathered):
    rows = x.shape[0]
    key_rows = round_up(rows, BLOCK)
    S = jax.ShapeDtypeStruct
    saved = [
        S((rows, D), bf16),
        S((key_rows, D), bf16),
        S((key_rows, D), bf16),
        S((key_rows, D), bf16),
        S((key_rows, BLOCK), f32),
        S((rows, D), bf16),
        S((rows, D), f32),
        S((rows, D), bf16),
        S((rows, 2 * FF), bf16),
    ] + [S(s, bf16) for s in weight_shapes()]
    return pl.pallas_call(
        forward_kernel,
        out_shape=[S((rows, D), f32)] + saved,
        in_specs=[SMEM, SMEM, VMEM, VMEM, VMEM, VMEM, HBM],
        out_specs=[VMEM] + [HBM] * 13,
        scratch_shapes=[like(s) for s in saved]
        + [
            pltpu.VMEM((rows, key_rows), f32),
            pltpu.SemaphoreType.DMA((4,)),
            pltpu.SemaphoreType.DMA((13,)),
        ],
        compiler_params=pltpu.CompilerParams(vmem_limit_bytes=VMEM_BYTES),
        cost_estimate=cost(2 * rows * PER_LAYER * BLOCK * BLOCK, 40 * 2**20),
        name="forward_block",
    )(slots, length, x, gains, cos, sin, gathered)


def tile_outputs(zones):
    return [jax.ShapeDtypeStruct((size, BLOCK, BLOCK), bf16) for size in zones]


def back_ffn(places, spare, back, gain, saved, zones, begun):
    rows = back.shape[0]
    S = jax.ShapeDtypeStruct
    args = (places, spare, back, gain) + tuple(saved)
    first = 2 + len(zones) - len(begun)
    wgu, wd = saved[3], saved[4]
    return pl.pallas_call(
        functools.partial(back_ffn_kernel, zones, len(begun)),
        out_shape=[S((rows, D), f32), S((1, D), f32)] + tile_outputs(zones),
        in_specs=[SMEM] * 2 + [VMEM] * 2 + [HBM] * (5 + len(begun)),
        out_specs=[VMEM, VMEM] + [HBM] * len(zones),
        input_output_aliases={len(args) + i: first + i for i in range(len(begun))},
        scratch_shapes=[like(s) for s in saved]
        + [like(wgu), like(wd)]
        + [
            pltpu.VMEM((rows, D), f32),
            pltpu.VMEM((BLOCK, BLOCK), bf16),
            pltpu.SemaphoreType.DMA((5,)),
            pltpu.SemaphoreType.DMA((2,)),
            pltpu.SemaphoreType.DMA,
        ],
        compiler_params=pltpu.CompilerParams(vmem_limit_bytes=VMEM_BYTES),
        cost_estimate=cost(4 * rows * (COUNTS[2] + COUNTS[3]) * BLOCK * BLOCK, 30 * 2**20),
        name="backward_feed_forward",
    )(*args, *begun)


def back_attention(places, length, back, cos, sin, saved, zones, begun):
    rows = back.shape[0]
    key_rows = round_up(rows, BLOCK)
    S = jax.ShapeDtypeStruct
    args = (places, length, back, cos, sin) + tuple(saved)
    first = 1 + len(zones) - len(begun)
    return pl.pallas_call(
        functools.partial(back_attention_kernel, zones, len(begun)),
        out_shape=[S((rows, 3 * D), bf16)] + tile_outputs(zones),
        in_specs=[SMEM] * 2 + [VMEM] * 3 + [HBM] * (6 + len(begun)),
        out_specs=[VMEM] + [HBM] * len(zones),
        input_output_aliases={len(args) + i: first + i for i in range(len(begun))},
        scratch_shapes=[like(s) for s in saved]
        + [
            like(saved[5]),
            pltpu.VMEM((key_rows, key_rows), f32),
            pltpu.VMEM((HEADS, 1, key_rows), f32),
            pltpu.VMEM((3, key_rows, PAIR), f32),
            pltpu.VMEM((key_rows, D), bf16),
            pltpu.SemaphoreType.DMA((6,)),
            pltpu.SemaphoreType.DMA,
        ],
        compiler_params=pltpu.CompilerParams(vmem_limit_bytes=VMEM_BYTES),
        cost_estimate=cost(4 * rows * COUNTS[1] * BLOCK * BLOCK + 20 * rows * rows * D, 30 * 2**20),
        name="backward_attention",
    )(*args, *begun)


def back_qkv(places, back, gain, d_projected, saved, zones, begun):
    rows = back.shape[0]
    S = jax.ShapeDtypeStruct
    args = (places, back, gain, d_projected) + tuple(saved)
    first = 2 + len(zones) - len(begun)
    return pl.pallas_call(
        functools.partial(back_qkv_kernel, zones, len(begun)),
        out_shape=[S((rows, D), f32), S((1, D), f32)] + tile_outputs(zones),
        in_specs=[SMEM] + [VMEM] * 3 + [HBM] * (3 + len(begun)),
        out_specs=[VMEM, VMEM] + [HBM] * len(zones),
        input_output_aliases={len(args) + i: first + i for i in range(len(begun))},
        scratch_shapes=[like(s) for s in saved]
        + [
            like(saved[2]),
            pltpu.VMEM((rows, D), f32),
            pltpu.SemaphoreType.DMA((3,)),
            pltpu.SemaphoreType.DMA,
        ],
        compiler_params=pltpu.CompilerParams(vmem_limit_bytes=VMEM_BYTES),
        cost_estimate=cost(4 * rows * COUNTS[0] * BLOCK * BLOCK, 20 * 2**20),
        name="backward_qkv",
    )(*args, *begun)


def optimizer_kernel(factor, rank, g_ref, m_ref, s_ref, r_ref, wg_ref, ns_ref, nm_ref, nc_ref):
    f = factor[0]
    count = m_ref.shape[0]
    for i in range(count):
        gb = g_ref[rank[pl.program_id(0) * count + i]]
        wg_ref[i] = gb.astype(f32) * f
        half = (1.0 - decay_rate) * f * f
        ns_ref[i, 0] = decay_rate * s_ref[i, 0] + half * nt(gb, gb)
        ns_ref[i, 1] = decay_rate * s_ref[i, 1] + half * tn(gb, gb)
        left = nn(r_ref[i, 0].astype(bf16), (gb.astype(f32) * f).astype(bf16)).astype(bf16)
        new = m_ref[i] - step_rate * nn(left, r_ref[i, 1].astype(bf16))
        nm_ref[i] = new
        nc_ref[i] = new.astype(bf16)


def optimizer(factor, rank, owned, master, statistics, inverse_roots):
    count = owned.shape[0]
    per = max(n for n in range(1, 13) if count % n == 0)
    S = jax.ShapeDtypeStruct
    one = pl.BlockSpec((per, BLOCK, BLOCK), lambda i: (i, 0, 0))
    two = pl.BlockSpec((per, 2, BLOCK, BLOCK), lambda i: (i, 0, 0, 0))
    return pl.pallas_call(
        optimizer_kernel,
        grid=(count // per,),
        out_shape=[
            S(master.shape, f32),
            S(statistics.shape, f32),
            S(master.shape, f32),
            S(master.shape, bf16),
        ],
        in_specs=[SMEM, SMEM, VMEM, one, two, two],
        out_specs=[one, two, one, one],
        compiler_params=pltpu.CompilerParams(vmem_limit_bytes=VMEM_BYTES),
        name="optimizer",
    )(factor, rank, owned, master, statistics, inverse_roots)


def to_images(local, bands, band):
    images, band_rows = local.shape[0], local.shape[-2]
    padded = jnp.concatenate([local, jnp.zeros((bands - images,) + local.shape[1:], local.dtype)], 0)
    whole = jnp.zeros((bands,) + local.shape[1:], local.dtype)
    for shift in range(bands):
        block = lax.dynamic_index_in_dim(padded, (band + shift) % bands, 0, keepdims=False)
        if shift > 0:
            pairs = [(b, (b + shift) % bands) for b in range(bands) if (b + shift) % bands < images]
            block = lax.ppermute(block, "band", pairs)
        whole = lax.dynamic_update_index_in_dim(whole, block, (band - shift) % bands, 0)
    return whole


def to_bands(whole, images, bands, band):
    local = jnp.zeros(whole.shape, whole.dtype)
    for shift in range(bands):
        block = lax.dynamic_index_in_dim(whole, (band + shift) % bands, 0, keepdims=False)
        if shift > 0:
            pairs = [(b, (b + shift) % bands) for b in range(images)]
            block = lax.ppermute(block, "band", pairs)
        local = lax.dynamic_update_index_in_dim(local, block, (band - shift) % bands, 0)
    return local[:images]


EARLY = 38
LATE = (30, 24, 16)


def relative_places(slot_of_block, per_owner, me):
    blocks = slot_of_block.shape[0]
    block_of_slot = jnp.zeros((blocks,), jnp.int32).at[slot_of_block].set(
        jnp.arange(blocks, dtype=jnp.int32)
    )
    by_owner = block_of_slot.reshape(-1, per_owner)
    rank = jnp.sum(by_owner[:, None, :] < by_owner[:, :, None], -1, dtype=jnp.int32)
    early = per_owner - EARLY
    clean = jnp.all(jnp.where(rank >= early, by_owner >= PER_LAYER, True))
    relative = (jnp.arange(by_owner.shape[0], dtype=jnp.int32) ^ me)[:, None]
    core, x, y = relative % 2, relative // 2 % 2, relative // 4
    place = jnp.zeros_like(rank)
    zone_sizes = (4 * EARLY, 4 * EARLY, 4 * early, 4 * early)
    chunks = [(early, EARLY, 0, 0)]
    start = 0
    for size in LATE:
        chunks.append((start, size, 2, 4 * start))
        start += size
    for start, size, zone, inside in chunks:
        half = size // 2
        at = rank - start
        spot = jnp.where(at < half, (x * 2 + y) * half + at, 4 * half + (y * 2 + x) * half + at - half)
        base = jnp.where(core == 0, sum(zone_sizes[:zone]), sum(zone_sizes[: zone + 1]))
        place = jnp.where((at >= 0) & (at < size), base + inside + spot, place)
    return place.reshape(-1)[slot_of_block], rank, clean, zone_sizes


CORE = [(i, i ^ 1) for i in range(8)]
ALONG_X = [(i, i ^ 2) for i in range(8)]
ALONG_Y = [(i, i ^ 4) for i in range(8)]


def wide(t, lo, hi):
    return t[lo:hi].astype(f32)


def plane_start(kept, received, gate=None, beside=None):
    half = kept.shape[0] // 8

    def chip(lo, hi):
        return wide(kept, lo * half, hi * half) + wide(received, lo * half, hi * half)

    send_x, send_y = chip(2, 4).astype(bf16), chip(6, 8).astype(bf16)
    if gate is not None:
        send_x, send_y, _ = lax.optimization_barrier((send_x, send_y, gate))
    if beside is not None:
        send_x, send_y, beside = lax.optimization_barrier((send_x, send_y, beside))
    going = (chip, half, lax.ppermute(send_x, "dp", ALONG_X), lax.ppermute(send_y, "dp", ALONG_Y))
    return (going, beside) if beside is not None else (going, (send_x, send_y))


def plane_turn(chip, half, from_x, from_y):
    send_y = (chip(1, 2) + wide(from_x, half, 2 * half)).astype(bf16)
    send_x = (chip(5, 6) + wide(from_y, half, 2 * half)).astype(bf16)
    turn = lax.ppermute(send_x, "dp", ALONG_X), lax.ppermute(send_y, "dp", ALONG_Y)
    return turn, (send_x, send_y)


def plane_end(chip, half, from_x, from_y, later_x, later_y):
    one = chip(0, 1) + wide(from_x, 0, half) + later_y.astype(f32)
    two = chip(4, 5) + wide(from_y, 0, half) + later_x.astype(f32)
    return jnp.concatenate([one, two], 0).astype(bf16)


def bands_meet(plane):
    return lax.ppermute(plane, "band", [(0, 1)]), lax.ppermute(plane, "band", [(2, 1)])


def bands_total(plane, up, down):
    return (plane.astype(f32) + up.astype(f32) + down.astype(f32)).astype(bf16)


def bands_part(total):
    return lax.ppermute(total, "band", [(1, 0)]), lax.ppermute(total, "band", [(1, 2)])


def bands_last(to_third):
    return lax.ppermute(to_third, "band", [(2, 3)])


def bands_choose(band, total, to_first, to_third, to_last):
    total = jnp.where(band == 0, to_first, total)
    total = jnp.where(band == 2, to_third, total)
    return jnp.where(band == 3, to_last, total)


def sum_bands(plane, band):
    total = bands_total(plane, *bands_meet(plane))
    to_first, to_third = bands_part(total)
    return bands_choose(band, total, to_first, to_third, bands_last(to_third))


def rope_tables(rows):
    half = HEAD_DIM // 2
    frequency = rope_base ** (-(jnp.arange(half, dtype=f32) * 2.0 / HEAD_DIM))
    angles = jnp.arange(rows, dtype=jnp.int32).astype(f32)[:, None] * frequency[None, :]
    cosine, sine = jnp.cos(angles), jnp.sin(angles)
    return jnp.tile(cosine, (1, 4)), jnp.tile(jnp.concatenate([-sine, sine], 1), (1, 2))


def shards(
    tokens,
    cotangent,
    lengths,
    slot_of_block,
    master,
    statistics,
    inverse_roots,
    gain_values,
    gain_moments,
):
    images, band_rows, _ = tokens.shape
    band = lax.axis_index("band")
    bands = lax.axis_size("band")
    seq = band_rows * bands
    rows = round_up(seq, 16)
    gathered = lax.all_gather(master.astype(bf16), "dp", axis=0, tiled=True)
    slot_count = gathered.shape[0]

    arrived = to_images(jnp.stack([tokens, cotangent], 1), bands, band)
    token_rows = jnp.pad(arrived[:, 0].reshape(seq, D), ((0, rows - seq), (0, 0)))
    back_rows = jnp.pad(arrived[:, 1].reshape(seq, D), ((0, rows - seq), (0, 0)))
    length = lengths[jnp.minimum(band, images - 1)]
    valid = (jnp.arange(rows, dtype=jnp.int32) < length).astype(f32)
    length = length.reshape(1)
    cos, sin = rope_tables(rows)

    spare_count = slot_count - slot_of_block.shape[0]
    spare = jnp.zeros((1,), jnp.int32)
    if spare_count > 0:
        used = jnp.zeros((slot_count,), jnp.int32).at[slot_of_block].set(1)
        spare = jnp.concatenate([jnp.argsort(used)[:spare_count].astype(jnp.int32), spare])

    hidden = token_rows.astype(f32)
    inputs, saves = [], []
    for layer in range(LAYERS):
        slots = slot_of_block[layer * PER_LAYER : (layer + 1) * PER_LAYER]
        gains = gain_values[2 * layer : 2 * layer + 2]
        inputs.append(hidden)
        hidden, *saved = forward_layer(slots, length, hidden, gains, cos, sin, gathered)
        saves.append(saved)
    layer_output = to_bands(
        hidden[:seq].astype(bf16).reshape(bands, band_rows, D), images, bands, band
    )

    back = back_rows.astype(f32) * valid[:, None]
    per_owner = master.shape[0]
    me = lax.axis_index("dp")
    by_permutes = (
        lax.axis_size("dp") == 8
        and bands == 4
        and images == 3
        and slot_count == slot_of_block.shape[0]
        and per_owner == EARLY + sum(LATE)
    )
    if by_permutes:
        places, ranks, clean, sizes = relative_places(slot_of_block, per_owner, me)
        rank = lax.dynamic_index_in_dim(ranks, me, 0, keepdims=False)
        zones_top, zones_bottom = sizes, (sizes[0] + sizes[1],) + sizes[2:]
    else:
        places, rank = slot_of_block, jnp.arange(per_owner, dtype=jnp.int32)
        zones_top = zones_bottom = (slot_count,)

    def backward(layer, back, zones, tiles, ahead=lambda back: back, later=lambda back: back):
        normed, q, k, v, st, mixed, mid, n2, gu, wqkv, wout, wgu, wd = saves[layer]
        slots = places[layer * PER_LAYER : (layer + 1) * PER_LAYER]
        fill = spare if layer == LAYERS - 1 else spare[-1:]
        back, gain_two, *tiles = back_ffn(
            slots, fill, back, gain_values[2 * layer + 1 : 2 * layer + 2], (mid, n2, gu, wgu, wd),
            zones, tiles,
        )
        back = ahead(back)
        d_projected, *tiles = back_attention(
            slots, length, back, cos, sin, (q, k, v, st, mixed, wout), zones, tiles
        )
        back = later(back)
        back, gain_one, *tiles = back_qkv(
            slots, back, gain_values[2 * layer : 2 * layer + 1], d_projected,
            (inputs[layer], normed, wqkv), zones, tiles,
        )
        return back, [gain_one, gain_two], tiles

    back, gains_top, tiles = backward(1, back, zones_top, [])
    if by_permutes:
        early_kept, early_sent, kept, sent = tiles
        early = {"output": layer_output}
        early["core"] = lax.ppermute(early_sent, "dp", CORE)

        def ahead(back):
            back, early["output"] = lax.optimization_barrier((back, early["output"]))
            early["plane"], back = plane_start(early_kept, early["core"], beside=back)
            return back

        def later(back):
            chip, half, from_x, from_y = early["plane"]
            back, from_x, from_y = lax.optimization_barrier((back, from_x, from_y))
            early["plane"] = (chip, half, from_x, from_y)
            return back

        back, gains_bottom, tiles = backward(0, back, zones_bottom, [kept, sent], ahead, later)
        layer_output = early["output"]
        early_late, kept, sent = tiles
        before = ()

        def group(*arrays):
            return lax.optimization_barrier(arrays + before)[: len(arrays)]

        from_core, chunks, start = [], [], 0
        for size in LATE:
            here = slice(4 * start, 4 * (start + size))
            from_core.append(lax.ppermute(sent[here], "dp", CORE))
            chunks.append(kept[here])
            start += size
        early_turn, _ = plane_turn(*early["plane"])
        input_grad = to_bands(
            back[:seq].astype(bf16).reshape(bands, band_rows, D), images, bands, band
        )
        gains = jnp.concatenate(gains_bottom + gains_top, 0).astype(bf16).reshape(-1, BLOCK)
        gains = jnp.pad(gains, ((0, BLOCK - gains.shape[0]), (0, 0)))[None]

        plane_sums, meets, totals, parts, lasts = {}, {}, {}, {}, {}

        def plane_done(name, going, turn, follow=None):
            nonlocal before
            if follow is None:
                later_x, later_y = group(*turn)
            else:
                later_x, later_y, received = group(*turn, from_core[follow])
            plane = plane_end(*going, later_x, later_y)
            if name == "early":
                plane = jnp.concatenate([plane, gains], 0)
            plane_sums[name] = plane
            meets[name] = bands_meet(plane)
            before = (plane,)
            if follow is not None:
                going, sends = plane_start(chunks[follow], received)
                before = (plane,) + sends
                return going

        def plane_turned(going):
            nonlocal before
            from_x, from_y = group(going[2], going[3])
            going = going[:2] + (from_x, from_y)
            turn, before = plane_turn(*going)
            return going, turn

        def met(name, *also):
            nonlocal before
            up, down, *also = group(*meets[name], *also)
            totals[name] = bands_total(plane_sums[name], up, down)
            parts[name] = bands_part(totals[name])
            before = (totals[name],)
            return also

        def parted(name):
            nonlocal before
            parts[name] = group(*parts[name])
            lasts[name] = bands_last(parts[name][1])
            before = parts[name][1:]

        going = plane_done("early", early["plane"], early_turn, 0)
        zero, turn = plane_turned(going)
        (input_grad,) = met("early", input_grad)
        going = plane_done(0, zero, turn, 1)
        parted("early")
        one, turn = plane_turned(going)
        met(0)
        going = plane_done(1, one, turn, 2)
        parted(0)
        two, turn = plane_turned(going)
        (lasts["early"],) = met(1, lasts["early"])
        plane_done(2, two, turn)
        parted(1)
        (lasts[0],) = met(2, lasts[0])
        parted(2)
        wholes = {}
        for name in ("early", 0, 1, 2):
            (last,) = group(lasts[name])
            wholes[name] = bands_choose(band, totals[name], *parts[name], last)
            before = (last,)
        gain_total = wholes["early"][EARLY].astype(f32)[: 2 * LAYERS * D // BLOCK].reshape(-1, D)
        owned = [wholes[i] for i in range(len(LATE))] + [wholes["early"][:EARLY]]

        order = jnp.argsort(places)[: sizes[0] + sizes[1]]

        def again(trip, total):
            _, late, first, second = lax.optimization_barrier(
                (trip, early_late, early_kept, early_sent)
            )
            mine = (order < PER_LAYER)[:, None, None]
            first = jnp.where(mine[: sizes[0]], late[: sizes[0]], first)
            second = jnp.where(mine[sizes[0] :], late[sizes[0] :], second)
            going, _ = plane_start(first, lax.ppermute(second, "dp", CORE))
            turn, _ = plane_turn(*going)
            return sum_bands(plane_end(*going, *turn), band)

        owned[-1] = lax.fori_loop(0, jnp.where(clean, 0, 1), again, owned[-1])
        owned = jnp.concatenate(owned, 0)
    else:
        back, gains_bottom, tiles = backward(0, back, zones_bottom, tiles)
        owned = lax.psum_scatter(tiles[0], "dp", scatter_dimension=0, tiled=True)
        owned = lax.psum(owned, "band")
        gain_total = lax.psum(jnp.concatenate(gains_bottom + gains_top, 0), "band")
        input_grad = to_bands(
            back[:seq].astype(bf16).reshape(bands, band_rows, D), images, bands, band
        )

    owned_f = owned.astype(f32)
    squares = jnp.sum(owned_f * owned_f).reshape(1)
    summed = lax.psum(jnp.concatenate([gain_total.reshape(-1), squares]), "dp")
    gain_total = summed[:-1].reshape(gain_values.shape)
    owned_squares = summed[-1]
    grad_norm = jnp.sqrt(owned_squares + jnp.sum(gain_total * gain_total))
    factor = jnp.minimum(1.0, clip_limit / grad_norm)
    weight_grads, new_statistics, new_master, master_copy = optimizer(
        factor.reshape(1), rank, owned, master, statistics, inverse_roots
    )
    gain_grads = gain_total * factor
    new_moments = decay_rate * gain_moments + (1.0 - decay_rate) * gain_grads * gain_grads
    new_gains = gain_values - gain_rate * gain_grads / (jnp.sqrt(new_moments) + epsilon)
    return (
        layer_output,
        input_grad,
        weight_grads,
        grad_norm,
        new_statistics,
        new_master,
        master_copy,
        gain_grads,
        new_moments,
        new_gains,
    )


def solution(mesh):
    return jax.shard_map(
        shards,
        mesh=mesh,
        in_specs=(
            P("dp", "band", None),
            P("dp", "band", None),
            P("dp"),
            P(),
            P("dp", None, None),
            P("dp", None, None, None),
            P("dp", None, None, None),
            P(),
            P(),
        ),
        out_specs=(
            P("dp", "band", None),
            P("dp", "band", None),
            P("dp", None, None),
            P(),
            P("dp", None, None, None),
            P("dp", None, None),
            P("dp", None, None),
            P(),
            P(),
            P(),
        ),
        check_vma=False,
    )
```

```python
import functools

import jax
import jax.numpy as jnp
from jax import lax
from jax.experimental import pallas as pl
from jax.experimental.pallas import tpu as pltpu
from jax.sharding import PartitionSpec as P

D = 768
HEADS = 12
HEAD_DIM = 64
FF = 2048
LAYERS = 2
BLOCK = 128
PAIR = 2 * HEAD_DIM

epsilon = 1e-05
rope_base = 10000.0
decay_rate = 0.5
step_rate = 0.4
gain_rate = 0.2
clip_limit = 1.0
masked_score = -1e30
VMEM_BYTES = 62 * 2**20

f32 = jnp.float32
bf16 = jnp.bfloat16

GRIDS = [
    (D // BLOCK, 3 * D // BLOCK),
    (D // BLOCK, D // BLOCK),
    (D // BLOCK, 2 * FF // BLOCK),
    (FF // BLOCK, D // BLOCK),
]
COUNTS = [r * c for r, c in GRIDS]
OFFSETS = [sum(COUNTS[:i]) for i in range(4)]
PER_LAYER = sum(COUNTS)
FF_STEP = 512


def round_up(n, m):
    return -(-n // m) * m


def nn(a, b):
    return lax.dot_general(a, b, (((1,), (0,)), ((), ())), preferred_element_type=f32)


def nt(a, b):
    return lax.dot_general(a, b, (((1,), (1,)), ((), ())), preferred_element_type=f32)


def tn(a, b):
    return lax.dot_general(a, b, (((0,), (0,)), ((), ())), preferred_element_type=f32)


def query_blocks(rows, step=256):
    return [(s, min(s + step, rows)) for s in range(0, rows, step)]


def swap_halves(t):
    lane = lax.broadcasted_iota(jnp.int32, t.shape, 1)
    half = HEAD_DIM // 2
    return jnp.where(lane % HEAD_DIM < half, pltpu.roll(t, PAIR - half, 1), pltpu.roll(t, half, 1))


def rms(m):
    return lax.rsqrt(jnp.mean(m * m, -1, keepdims=True) + epsilon)


def rms_back(u, m, g):
    r = rms(m)
    t = u * g
    dot = jnp.mean(t * m, -1, keepdims=True)
    return r * t - m * (r * r * r * dot), jnp.sum(u * m * r, 0, keepdims=True)


def copies(pairs, sem):
    return [pltpu.make_async_copy(src, dst, sem.at[i]) for i, (src, dst) in enumerate(pairs)]


def forward_kernel(
    slots, length, x_ref, g_ref, cos_ref, sin_ref, w_hbm,
    xn_ref, normed_o, q_o, k_o, v_o, st_o, mixed_o, mid_o, n2_o, gu_o, wqkv_o, wout_o, wgu_o, wd_o,
    normed_ref, q_ref, k_ref, v_ref, st_ref, mixed_ref, mid_ref, n2_ref, gu_ref,
    wqkv, wout, wgu, wd, bias, sem_in, sem_out,
):
    rows = x_ref.shape[0]
    key_rows = q_ref.shape[0]
    held = (wqkv, wout, wgu, wd)
    for m in range(4):
        tile_rows, tile_cols = GRIDS[m]

        @pl.loop(0, tile_rows)
        def _(i, m=m, tile_cols=tile_cols):
            for j in range(tile_cols):
                slot = slots[OFFSETS[m] + i * tile_cols + j]
                pltpu.make_async_copy(
                    w_hbm.at[slot],
                    held[m].at[pl.ds(pl.multiple_of(i * BLOCK, BLOCK), BLOCK), pl.ds(j * BLOCK, BLOCK)],
                    sem_in.at[m],
                ).start()

    def arrive(m):
        pltpu.make_async_copy(held[m], held[m], sem_in.at[m]).wait()

    saves = copies(
        [
            (normed_ref, normed_o), (q_ref, q_o), (k_ref, k_o), (v_ref, v_o), (st_ref, st_o),
            (mixed_ref, mixed_o), (mid_ref, mid_o), (n2_ref, n2_o), (gu_ref, gu_o),
            (wqkv, wqkv_o), (wout, wout_o), (wgu, wgu_o), (wd, wd_o),
        ],
        sem_out,
    )
    query = lax.broadcasted_iota(jnp.int32, bias.shape, 0)
    key = lax.broadcasted_iota(jnp.int32, bias.shape, 1)
    bias[...] = jnp.where((key <= query) & (key < length[0]), 0.0, masked_score)
    x = x_ref[...]
    normed_ref[...] = (x * rms(x) * g_ref[0:1, :]).astype(bf16)
    saves[0].start()
    tail = key_rows - rows
    for ref in (q_ref, k_ref, v_ref):
        ref[rows:, :] = jnp.zeros((tail, D), bf16)
    arrive(0)
    saves[9].start()

    @pl.loop(0, 2)
    def _(part):
        acc = nn(normed_ref[...], wqkv[:, pl.ds(pl.multiple_of(part * D, D), D)])
        scale = jnp.where(part == 0, HEAD_DIM ** (-0.5), 1.0)
        for p in range(HEADS // 2):
            t = acc[:, p * PAIR : (p + 1) * PAIR]
            rot = ((t * cos_ref[...] + swap_halves(t) * sin_ref[...]) * scale).astype(bf16)

            @pl.when(part == 0)
            def _(p=p, rot=rot):
                q_ref[0:rows, p * PAIR : (p + 1) * PAIR] = rot

            @pl.when(part == 1)
            def _(p=p, rot=rot):
                k_ref[0:rows, p * PAIR : (p + 1) * PAIR] = rot

    v_ref[0:rows, :] = nn(normed_ref[...], wqkv[:, 2 * D :]).astype(bf16)
    for i in (1, 2, 3):
        saves[i].start()
    st_ref[...] = jnp.zeros(st_ref.shape, f32)

    @pl.loop(0, HEADS // 2)
    def _(p):
        cols = pl.ds(pl.multiple_of(p * PAIR, PAIR), PAIR)
        kp = k_ref[:, cols]
        vp = v_ref[:, cols]
        low = lax.broadcasted_iota(jnp.int32, kp.shape, 1) < HEAD_DIM
        keys = (jnp.where(low, kp, 0), jnp.where(low, 0, kp))
        values = (jnp.where(low, vp, 1), jnp.where(low, 1, vp))
        for q0, q1 in query_blocks(rows):
            kend = min(round_up(q1, BLOCK), key_rows)
            qp = q_ref[q0:q1, cols]
            mask = bias[q0:q1, :kend]
            parts = []
            tops = []
            for h in range(2):
                s = nt(qp, keys[h][:kend]) + mask
                top = jnp.max(s, -1, keepdims=True)
                e = jnp.exp(s - top).astype(bf16)
                parts.append(nn(e, values[h][:kend]))
                tops.append(top)
            lane = lax.broadcasted_iota(jnp.int32, parts[0].shape, 1)
            low_q = lane < HEAD_DIM
            total = pltpu.roll(jnp.where(low_q, parts[1], parts[0]), HEAD_DIM, 1)
            mixed_ref[q0:q1, cols] = (jnp.where(low_q, parts[0], parts[1]) / total).astype(bf16)
            log_total = jnp.log(total)
            other = pltpu.roll(log_total, HEAD_DIM, 1)
            first = tops[0] + jnp.where(low_q, log_total, other)
            second = tops[1] + jnp.where(low_q, other, log_total)
            old = st_ref[q0:q1, :]
            st_ref[q0:q1, :] = jnp.where(
                lane == 2 * p, first, jnp.where(lane == 2 * p + 1, second, old)
            )

    saves[4].start()
    saves[5].start()
    arrive(1)
    saves[10].start()
    middle = x_ref[...] + nn(mixed_ref[...], wout[...])
    mid_ref[...] = middle
    saves[6].start()
    n2_ref[...] = (middle * rms(middle) * g_ref[1:2, :]).astype(bf16)
    saves[7].start()
    arrive(2)
    saves[11].start()
    arrive(3)
    saves[12].start()
    xn_ref[...] = mid_ref[...]

    @pl.loop(0, FF // FF_STEP)
    def _(t):
        at = pl.multiple_of(t * FF_STEP, FF_STEP)
        gate = nn(n2_ref[...], wgu[:, pl.ds(at, FF_STEP)])
        up = nn(n2_ref[...], wgu[:, pl.ds(FF + at, FF_STEP)])
        act = (gate / (1.0 + jnp.exp(-gate)) * up).astype(bf16)
        gu_ref[:, pl.ds(at, FF_STEP)] = gate.astype(bf16)
        gu_ref[:, pl.ds(FF + at, FF_STEP)] = up.astype(bf16)
        xn_ref[...] += nn(act, wd[pl.ds(at, FF_STEP), :])

    saves[8].start()
    for save in saves:
        save.wait()


def put_tiles(places, m, grad, tiles_out, sem, i0, i1, j0, count_j):
    @pl.loop(i0, i1)
    def _(i):
        for jj in range(count_j):
            j = j0 + jj
            pltpu.make_async_copy(
                grad.at[
                    pl.ds(pl.multiple_of(i * BLOCK, BLOCK), BLOCK),
                    pl.ds(pl.multiple_of(j * BLOCK, BLOCK), BLOCK),
                ],
                tiles_out.at[places[OFFSETS[m] + i * GRIDS[m][1] + j]],
                sem,
            ).start()


def back_ffn_kernel(
    begun, places, spare, back_ref, g_ref, mid_i, n2_i, gu_i, wgu_i, wd_i, *rest
):
    mid_ref_out, gain_ref, tiles_out, *rest = rest[begun:]
    mid_ref, n2_ref, gu_ref, wgu, wd, ggu, gd, big, zero, sem_in, sem_out, sem_zero = rest
    loads = copies([(wd_i, wd), (gu_i, gu_ref), (n2_i, n2_ref), (wgu_i, wgu), (mid_i, mid_ref)], sem_in)
    for load in loads:
        load.start()
    spares = spare.shape[0] - 1
    if spares > 0:
        zero[...] = jnp.zeros(zero.shape, bf16)

        @pl.loop(0, spares)
        def _(i):
            pltpu.make_async_copy(zero, tiles_out.at[spare[i]], sem_zero).start()

    big[...] = jnp.zeros(big.shape, f32)
    for load in loads[:4]:
        load.wait()
    put = functools.partial(put_tiles, places)

    @pl.loop(0, FF // FF_STEP)
    def _(t):
        at = pl.multiple_of(t * FF_STEP, FF_STEP)
        here = pl.ds(at, FF_STEP)
        there = pl.ds(FF + at, FF_STEP)
        back_ffn = back_ref[...].astype(bf16)
        d_act = nt(back_ffn, wd[here, :])
        gate = gu_ref[:, here].astype(f32)
        up = gu_ref[:, there].astype(f32)
        sig = 1.0 / (1.0 + jnp.exp(-gate))
        silu = gate * sig
        act = (silu * up).astype(bf16)
        d_gate = (d_act * up * (sig * (1.0 + gate * (1.0 - sig)))).astype(bf16)
        d_up = (d_act * silu).astype(bf16)
        gd[here, :] = tn(act, back_ffn).astype(bf16)
        ggu[:, here] = tn(n2_ref[...], d_gate).astype(bf16)
        ggu[:, there] = tn(n2_ref[...], d_up).astype(bf16)
        per = FF_STEP // BLOCK
        put(3, gd, tiles_out, sem_out.at[1], t * per, (t + 1) * per, 0, D // BLOCK)
        put(2, ggu, tiles_out, sem_out.at[0], 0, D // BLOCK, t * per, per)
        put(2, ggu, tiles_out, sem_out.at[0], 0, D // BLOCK, FF // BLOCK + t * per, per)
        big[...] += nt(d_gate, wgu[:, here]) + nt(d_up, wgu[:, there])

    loads[4].wait()
    step, gain = rms_back(big[...], mid_ref[...], g_ref[...])
    gain_ref[...] = gain
    mid_ref_out[...] = back_ref[...] + step
    pltpu.make_async_copy(ggu, ggu, sem_out.at[0]).wait()
    pltpu.make_async_copy(gd, gd, sem_out.at[1]).wait()
    if spares > 0:

        @pl.loop(0, spares)
        def _(i):
            pltpu.make_async_copy(zero, tiles_out.at[spare[i]], sem_zero).wait()


def back_attention_kernel(
    begun, places, length, back_ref, cos_ref, sin_ref,
    q_i, k_i, v_i, st_i, mixed_i, wout_i, *rest
):
    (
        dproj, tiles_out, q_ref, k_ref, v_ref, st_ref, mixed_ref, wout,
        gout, bias, turned, sums, mixed_back, sem_in, sem_out,
    ) = rest[begun:]
    rows = back_ref.shape[0]
    key_rows = q_ref.shape[0]
    loads = copies(
        [
            (wout_i, wout), (mixed_i, mixed_ref), (q_i, q_ref), (k_i, k_ref), (v_i, v_ref),
            (st_i, st_ref),
        ],
        sem_in,
    )
    for load in loads:
        load.start()
    put = functools.partial(put_tiles, places)
    key = lax.broadcasted_iota(jnp.int32, bias.shape, 0)
    query = lax.broadcasted_iota(jnp.int32, bias.shape, 1)
    bias[...] = jnp.where((key <= query) & (key < length[0]), 0.0, masked_score)
    back_attn = back_ref[...].astype(bf16)
    loads[0].wait()
    mixed_back[0:rows, :] = nt(back_attn, wout[...]).astype(bf16)
    mixed_back[rows:, :] = jnp.zeros((key_rows - rows, D), bf16)
    loads[1].wait()
    gout[...] = tn(mixed_ref[...], back_attn).astype(bf16)
    put(1, gout, tiles_out, sem_out, 0, D // BLOCK, 0, D // BLOCK)
    for load in loads[2:]:
        load.wait()
    levels = st_ref[...].T
    for h in range(HEADS):
        turned[h] = levels[h : h + 1, :]

    @pl.loop(0, HEADS // 2)
    def _(p):
        cols = pl.ds(pl.multiple_of(p * PAIR, PAIR), PAIR)
        low = lax.broadcasted_iota(jnp.int32, (key_rows, PAIR), 1) < HEAD_DIM

        def both(t):
            return (jnp.where(low, t, 0), jnp.where(low, 0, t))

        qp = q_ref[:, cols]
        op = mixed_back[:, cols]
        keys, values, queries, backs = both(k_ref[:, cols]), both(v_ref[:, cols]), both(qp), both(op)
        sums[...] = jnp.zeros(sums.shape, f32)
        for q0, q1 in query_blocks(key_rows):
            kend = q1
            d_query = jnp.zeros((q1 - q0, PAIR), f32)
            d_key = jnp.zeros((kend, PAIR), f32)
            d_value = jnp.zeros((kend, PAIR), f32)
            for h in range(2):
                level = turned[2 * p + h, :, q0:q1]
                soft = jnp.exp(nt(keys[h][:kend], qp[q0:q1]) + bias[:kend, q0:q1] - level)
                d_prob = nt(values[h][:kend], op[q0:q1])
                row_dot = jnp.sum(soft * d_prob, 0, keepdims=True)
                d_score = (soft * (d_prob - row_dot)).astype(bf16)
                d_value += nn(soft.astype(bf16), backs[h][q0:q1])
                d_key += nn(d_score, queries[h][q0:q1])
                d_query += tn(d_score, keys[h][:kend])
            sums[0, q0:q1, :] += d_query * HEAD_DIM ** (-0.5)
            sums[1, :kend, :] += d_key
            sums[2, :kend, :] += d_value
        for part in range(2):
            t = sums[part, 0:rows, :]
            dproj[:, pl.ds(pl.multiple_of(part * D + p * PAIR, PAIR), PAIR)] = (
                t * cos_ref[...] - swap_halves(t) * sin_ref[...]
            ).astype(bf16)
        dproj[:, pl.ds(pl.multiple_of(2 * D + p * PAIR, PAIR), PAIR)] = sums[2, 0:rows, :].astype(bf16)

    pltpu.make_async_copy(gout, gout, sem_out).wait()


def back_qkv_kernel(begun, places, back_ref, g_ref, dproj, x_i, normed_i, wqkv_i, *rest):
    dx_ref, gain_ref, tiles_out, *rest = rest[begun:]
    x_ref, normed_ref, wqkv, gqkv, big, sem_in, sem_out = rest
    loads = copies([(normed_i, normed_ref), (wqkv_i, wqkv), (x_i, x_ref)], sem_in)
    for load in loads:
        load.start()
    big[...] = jnp.zeros(big.shape, f32)
    loads[0].wait()
    loads[1].wait()

    @pl.loop(0, 3)
    def _(part):
        cols = pl.ds(pl.multiple_of(part * D, D), D)
        gqkv[:, cols] = tn(normed_ref[...], dproj[:, cols]).astype(bf16)
        put_tiles(places, 0, gqkv, tiles_out, sem_out, 0, D // BLOCK, part * (D // BLOCK), D // BLOCK)
        big[...] += nt(dproj[:, cols], wqkv[:, cols])

    loads[2].wait()
    step, gain = rms_back(big[...], x_ref[...], g_ref[...])
    gain_ref[...] = gain
    dx_ref[...] = back_ref[...] + step
    pltpu.make_async_copy(gqkv, gqkv, sem_out).wait()


def weight_shapes():
    return [(r * BLOCK, c * BLOCK) for r, c in GRIDS]


VMEM = pl.BlockSpec(memory_space=pltpu.VMEM)
SMEM = pl.BlockSpec(memory_space=pltpu.SMEM)
HBM = pl.BlockSpec(memory_space=pl.ANY)


def like(struct):
    return pltpu.VMEM(struct.shape, struct.dtype)


def cost(flops, bytes_accessed):
    return pl.CostEstimate(flops=flops, bytes_accessed=bytes_accessed, transcendentals=0)


def forward_layer(slots, length, x, gains, cos, sin, gathered):
    rows = x.shape[0]
    key_rows = round_up(rows, BLOCK)
    S = jax.ShapeDtypeStruct
    saved = [
        S((rows, D), bf16),
        S((key_rows, D), bf16),
        S((key_rows, D), bf16),
        S((key_rows, D), bf16),
        S((key_rows, BLOCK), f32),
        S((rows, D), bf16),
        S((rows, D), f32),
        S((rows, D), bf16),
        S((rows, 2 * FF), bf16),
    ] + [S(s, bf16) for s in weight_shapes()]
    return pl.pallas_call(
        forward_kernel,
        out_shape=[S((rows, D), f32)] + saved,
        in_specs=[SMEM, SMEM, VMEM, VMEM, VMEM, VMEM, HBM],
        out_specs=[VMEM] + [HBM] * 13,
        scratch_shapes=[like(s) for s in saved]
        + [
            pltpu.VMEM((rows, key_rows), f32),
            pltpu.SemaphoreType.DMA((4,)),
            pltpu.SemaphoreType.DMA((13,)),
        ],
        compiler_params=pltpu.CompilerParams(vmem_limit_bytes=VMEM_BYTES),
        cost_estimate=cost(2 * rows * PER_LAYER * BLOCK * BLOCK, 40 * 2**20),
        name="forward_block",
    )(slots, length, x, gains, cos, sin, gathered)


def back_ffn(places, spare, back, gain, saved, slot_count, begun):
    rows = back.shape[0]
    S = jax.ShapeDtypeStruct
    args = (places, spare, back, gain) + tuple(saved)
    wgu, wd = saved[3], saved[4]
    return pl.pallas_call(
        functools.partial(back_ffn_kernel, len(begun)),
        out_shape=[S((rows, D), f32), S((1, D), f32), S((slot_count, BLOCK, BLOCK), bf16)],
        in_specs=[SMEM] * 2 + [VMEM] * 2 + [HBM] * (5 + len(begun)),
        out_specs=[VMEM, VMEM, HBM],
        input_output_aliases={len(args): 2} if begun else {},
        scratch_shapes=[like(s) for s in saved]
        + [like(wgu), like(wd)]
        + [
            pltpu.VMEM((rows, D), f32),
            pltpu.VMEM((BLOCK, BLOCK), bf16),
            pltpu.SemaphoreType.DMA((5,)),
            pltpu.SemaphoreType.DMA((2,)),
            pltpu.SemaphoreType.DMA,
        ],
        compiler_params=pltpu.CompilerParams(vmem_limit_bytes=VMEM_BYTES),
        cost_estimate=cost(4 * rows * (COUNTS[2] + COUNTS[3]) * BLOCK * BLOCK, 30 * 2**20),
        name="backward_feed_forward",
    )(*args, *begun)


def back_attention(places, length, back, cos, sin, saved, slot_count, begun):
    rows = back.shape[0]
    key_rows = round_up(rows, BLOCK)
    S = jax.ShapeDtypeStruct
    args = (places, length, back, cos, sin) + tuple(saved)
    return pl.pallas_call(
        functools.partial(back_attention_kernel, len(begun)),
        out_shape=[S((rows, 3 * D), bf16), S((slot_count, BLOCK, BLOCK), bf16)],
        in_specs=[SMEM] * 2 + [VMEM] * 3 + [HBM] * (6 + len(begun)),
        out_specs=[VMEM, HBM],
        input_output_aliases={len(args): 1} if begun else {},
        scratch_shapes=[like(s) for s in saved]
        + [
            like(saved[5]),
            pltpu.VMEM((key_rows, key_rows), f32),
            pltpu.VMEM((HEADS, 1, key_rows), f32),
            pltpu.VMEM((3, key_rows, PAIR), f32),
            pltpu.VMEM((key_rows, D), bf16),
            pltpu.SemaphoreType.DMA((6,)),
            pltpu.SemaphoreType.DMA,
        ],
        compiler_params=pltpu.CompilerParams(vmem_limit_bytes=VMEM_BYTES),
        cost_estimate=cost(4 * rows * COUNTS[1] * BLOCK * BLOCK + 20 * rows * rows * D, 30 * 2**20),
        name="backward_attention",
    )(*args, *begun)


def back_qkv(places, back, gain, d_projected, saved, slot_count, begun):
    rows = back.shape[0]
    S = jax.ShapeDtypeStruct
    args = (places, back, gain, d_projected) + tuple(saved)
    return pl.pallas_call(
        functools.partial(back_qkv_kernel, len(begun)),
        out_shape=[S((rows, D), f32), S((1, D), f32), S((slot_count, BLOCK, BLOCK), bf16)],
        in_specs=[SMEM] + [VMEM] * 3 + [HBM] * (3 + len(begun)),
        out_specs=[VMEM, VMEM, HBM],
        input_output_aliases={len(args): 2} if begun else {},
        scratch_shapes=[like(s) for s in saved]
        + [
            like(saved[2]),
            pltpu.VMEM((rows, D), f32),
            pltpu.SemaphoreType.DMA((3,)),
            pltpu.SemaphoreType.DMA,
        ],
        compiler_params=pltpu.CompilerParams(vmem_limit_bytes=VMEM_BYTES),
        cost_estimate=cost(4 * rows * COUNTS[0] * BLOCK * BLOCK, 20 * 2**20),
        name="backward_qkv",
    )(*args, *begun)


def optimizer_kernel(factor, rank, g_ref, m_ref, s_ref, r_ref, wg_ref, ns_ref, nm_ref, nc_ref):
    f = factor[0]
    count = m_ref.shape[0]
    for i in range(count):
        gb = g_ref[rank[pl.program_id(0) * count + i]]
        wg_ref[i] = gb.astype(f32) * f
        half = (1.0 - decay_rate) * f * f
        ns_ref[i, 0] = decay_rate * s_ref[i, 0] + half * nt(gb, gb)
        ns_ref[i, 1] = decay_rate * s_ref[i, 1] + half * tn(gb, gb)
        left = nn(r_ref[i, 0].astype(bf16), (gb.astype(f32) * f).astype(bf16)).astype(bf16)
        new = m_ref[i] - step_rate * nn(left, r_ref[i, 1].astype(bf16))
        nm_ref[i] = new
        nc_ref[i] = new.astype(bf16)


def optimizer(factor, rank, owned, master, statistics, inverse_roots):
    count = owned.shape[0]
    per = max(n for n in range(1, 13) if count % n == 0)
    S = jax.ShapeDtypeStruct
    one = pl.BlockSpec((per, BLOCK, BLOCK), lambda i: (i, 0, 0))
    two = pl.BlockSpec((per, 2, BLOCK, BLOCK), lambda i: (i, 0, 0, 0))
    return pl.pallas_call(
        optimizer_kernel,
        grid=(count // per,),
        out_shape=[
            S(master.shape, f32),
            S(statistics.shape, f32),
            S(master.shape, f32),
            S(master.shape, bf16),
        ],
        in_specs=[SMEM, SMEM, VMEM, one, two, two],
        out_specs=[one, two, one, one],
        compiler_params=pltpu.CompilerParams(vmem_limit_bytes=VMEM_BYTES),
        name="optimizer",
    )(factor, rank, owned, master, statistics, inverse_roots)


def to_images(local, bands, band):
    images, band_rows = local.shape[0], local.shape[-2]
    padded = jnp.concatenate([local, jnp.zeros((bands - images,) + local.shape[1:], local.dtype)], 0)
    whole = jnp.zeros((bands,) + local.shape[1:], local.dtype)
    for shift in range(bands):
        block = lax.dynamic_index_in_dim(padded, (band + shift) % bands, 0, keepdims=False)
        if shift > 0:
            pairs = [(b, (b + shift) % bands) for b in range(bands) if (b + shift) % bands < images]
            block = lax.ppermute(block, "band", pairs)
        whole = lax.dynamic_update_index_in_dim(whole, block, (band - shift) % bands, 0)
    return whole


def send_to_bands(whole, images, bands, band):
    blocks = []
    for shift in range(bands):
        block = lax.dynamic_index_in_dim(whole, (band + shift) % bands, 0, keepdims=False)
        if shift > 0:
            pairs = [(b, (b + shift) % bands) for b in range(images)]
            block = lax.ppermute(block, "band", pairs)
        blocks.append(block)
    return tuple(blocks)


def at_bands(blocks, images, bands, band):
    local = jnp.zeros((bands,) + blocks[0].shape, blocks[0].dtype)
    for shift, block in enumerate(blocks):
        local = lax.dynamic_update_index_in_dim(local, block, (band - shift) % bands, 0)
    return local[:images]


CHUNKS = (22, 18, 20, 18, 18, 12)
FFN_FIRST = OFFSETS[2]
LEAST = (PER_LAYER + FFN_FIRST, PER_LAYER, FFN_FIRST, FFN_FIRST, 0, 0)
GAIN_CHUNK = 4
STARTS = tuple(sum(CHUNKS[:i]) for i in range(len(CHUNKS)))


def relative_places(slot_of_block, per_owner, me):
    blocks = slot_of_block.shape[0]
    block_of_slot = jnp.zeros((blocks,), jnp.int32).at[slot_of_block].set(
        jnp.arange(blocks, dtype=jnp.int32)
    )
    by_owner = block_of_slot.reshape(-1, per_owner)
    rank = jnp.sum(by_owner[:, None, :] > by_owner[:, :, None], -1, dtype=jnp.int32)
    relative = (jnp.arange(by_owner.shape[0], dtype=jnp.int32) ^ me)[:, None]
    core, x, y = relative % 2, relative // 2 % 2, relative // 4
    place = jnp.zeros_like(rank)
    clean = jnp.bool_(True)
    for start, size, least in zip(STARTS, CHUNKS, LEAST):
        half = size // 2
        at = rank - start
        here = (at >= 0) & (at < size)
        spot = jnp.where(at < half, (x * 2 + y) * half + at, 4 * half + (y * 2 + x) * half + at - half)
        place = jnp.where(here, 8 * start + core * 4 * size + spot, place)
        clean = clean & jnp.all(jnp.where(here, by_owner >= least, True))
    return place.reshape(-1)[slot_of_block], rank, clean


CORE = [(i, i ^ 1) for i in range(8)]
ALONG_X = [(i, i ^ 2) for i in range(8)]
ALONG_Y = [(i, i ^ 4) for i in range(8)]


def wide(t, lo, hi):
    return t[lo:hi].astype(f32)


def split_wide(t):
    high = lax.reduce_precision(t, 8, 7)
    both = jnp.concatenate([high, t - high], 0)
    return jnp.pad(both, ((0, BLOCK - both.shape[0]), (0, 0))).astype(bf16)[None]


def join_wide(tile, rows):
    return tile[0, :rows].astype(f32) + tile[0, rows : 2 * rows].astype(f32)


def with_tile(t, extra):
    return t if extra is None else jnp.concatenate([t, split_wide(extra)], 0)


class Chunk:
    def __init__(self, index, extra=None):
        self.index, self.extra = index, extra
        self.half = CHUNKS[index] // 2

    def begin(self, tiles):
        size, at = CHUNKS[self.index], 8 * STARTS[self.index]
        self.kept = tiles[at : at + 4 * size]
        self.sent = tiles[at + 4 * size : at + 8 * size]

    def own(self):
        return join_wide(split_wide(self.extra), self.extra.shape[0])

    def take(self, arrived):
        if self.extra is not None:
            self.extra = self.own() + join_wide(arrived[-1:], self.extra.shape[0])

    def chip(self, lo, hi):
        lo, hi = lo * self.half, hi * self.half
        return wide(self.kept, lo, hi) + wide(self.received, lo, hi)

    def to_core(self):
        return (with_tile(self.sent, self.extra),)

    def go_core(self, send):
        return (lax.ppermute(send, "dp", CORE),)

    def to_plane(self, received):
        self.received = received
        self.take(received)
        return with_tile(self.chip(2, 4).astype(bf16), self.extra), self.chip(6, 8).astype(bf16)

    def go_plane(self, send_x, send_y):
        return lax.ppermute(send_x, "dp", ALONG_X), lax.ppermute(send_y, "dp", ALONG_Y)

    def to_turn(self, from_x, from_y):
        self.from_x, self.from_y = from_x, from_y
        self.take(from_x)
        half = self.half
        send_y = (self.chip(1, 2) + wide(from_x, half, 2 * half)).astype(bf16)
        send_x = (self.chip(5, 6) + wide(from_y, half, 2 * half)).astype(bf16)
        return send_x, with_tile(send_y, self.extra)

    def to_meet(self, from_x, from_y):
        self.take(from_y)
        half = self.half
        one = self.chip(0, 1) + wide(self.from_x, 0, half) + wide(from_y, 0, half)
        two = self.chip(4, 5) + wide(self.from_y, 0, half) + wide(from_x, 0, half)
        self.plane = with_tile(jnp.concatenate([one, two], 0).astype(bf16), self.extra)
        return (self.plane,)

    def go_meet(self, plane):
        return lax.ppermute(plane, "band", [(0, 1)]), lax.ppermute(plane, "band", [(2, 1)])

    def to_part(self, up, down):
        total = self.plane.astype(f32) + up.astype(f32) + down.astype(f32)
        if self.extra is not None:
            total = total[:-1]
            rows = self.extra.shape[0]
            self.extra = self.own() + join_wide(up[-1:], rows) + join_wide(down[-1:], rows)
        self.total = with_tile(total.astype(bf16), self.extra)
        return (self.total,)

    def go_part(self, total):
        return lax.ppermute(total, "band", [(1, 0)]), lax.ppermute(total, "band", [(1, 2)])

    def to_last(self, to_first, to_third):
        self.to_first, self.to_third = to_first, to_third
        return (to_third,)

    def go_last(self, to_third):
        return (lax.ppermute(to_third, "band", [(2, 3)]),)

    def to_end(self, to_last):
        band = lax.axis_index("band")
        total = jnp.where(band == 0, self.to_first, self.total)
        total = jnp.where(band == 2, self.to_third, total)
        self.total = jnp.where(band == 3, to_last, total)
        return ()

    STEPS = ("core", "plane", "turn", "meet", "part", "last", "end")

    def step(self, name, arrived=()):
        return getattr(self, "to_" + name)(*arrived)

    def go(self, name, sends):
        way = {"turn": "plane"}.get(name, name)
        return getattr(self, "go_" + way)(*sends) if way != "end" else ()


class Sequence:
    def __init__(self):
        self.before = ()
        self.arrived = {}

    def round(self, steps, *beside):
        counts = [len(self.arrived.get(id(chunk), ())) for chunk, _ in steps]
        arrays = sum((tuple(self.arrived.get(id(chunk), ())) for chunk, _ in steps), ())
        taken = len(arrays)
        arrays = lax.optimization_barrier(arrays + self.before + beside)
        beside = arrays[len(arrays) - len(beside) :]
        new = [chunk for chunk, name in steps if name == "core"]
        for chunk in new:
            chunk.begin(*beside[:1])
        sends, at = [], 0
        for (chunk, name), count in zip(steps, counts):
            sends.append(chunk.step(name, arrays[:taken][at : at + count]))
            at += count
        flat = sum((tuple(s) for s in sends), ())
        if beside:
            kept = tuple(chunk.kept for chunk in new)
            together = lax.optimization_barrier(flat + kept + beside)
            beside = together[len(together) - len(beside) :]
            for chunk, piece in zip(new, together[len(flat) :]):
                chunk.kept = piece
            flat = together[: len(flat)]
        at = 0
        for (chunk, name), s in zip(steps, sends):
            self.arrived[id(chunk)] = chunk.go(name, flat[at : at + len(s)])
            at += len(s)
        self.before = flat
        return beside


def reduce_all(chunks, tiles):
    sequence = Sequence()
    for chunk in chunks:
        for name in Chunk.STEPS:
            (tiles,) = sequence.round([(chunk, name)], tiles)


def rope_tables(rows):
    half = HEAD_DIM // 2
    frequency = rope_base ** (-(jnp.arange(half, dtype=f32) * 2.0 / HEAD_DIM))
    angles = jnp.arange(rows, dtype=jnp.int32).astype(f32)[:, None] * frequency[None, :]
    cosine, sine = jnp.cos(angles), jnp.sin(angles)
    return jnp.tile(cosine, (1, 4)), jnp.tile(jnp.concatenate([-sine, sine], 1), (1, 2))


def shards(
    tokens,
    cotangent,
    lengths,
    slot_of_block,
    master,
    statistics,
    inverse_roots,
    gain_values,
    gain_moments,
):
    images, band_rows, _ = tokens.shape
    band = lax.axis_index("band")
    bands = lax.axis_size("band")
    seq = band_rows * bands
    rows = round_up(seq, 16)
    gathered = lax.all_gather(master.astype(bf16), "dp", axis=0, tiled=True)
    slot_count = gathered.shape[0]

    arrived = to_images(jnp.stack([tokens, cotangent], 1), bands, band)
    token_rows = jnp.pad(arrived[:, 0].reshape(seq, D), ((0, rows - seq), (0, 0)))
    back_rows = jnp.pad(arrived[:, 1].reshape(seq, D), ((0, rows - seq), (0, 0)))
    length = lengths[jnp.minimum(band, images - 1)]
    valid = (jnp.arange(rows, dtype=jnp.int32) < length).astype(f32)
    length = length.reshape(1)
    cos, sin = rope_tables(rows)

    spare_count = slot_count - slot_of_block.shape[0]
    spare = jnp.zeros((1,), jnp.int32)
    if spare_count > 0:
        used = jnp.zeros((slot_count,), jnp.int32).at[slot_of_block].set(1)
        spare = jnp.concatenate([jnp.argsort(used)[:spare_count].astype(jnp.int32), spare])

    hidden = token_rows.astype(f32)
    inputs, saves = [], []
    for layer in range(LAYERS):
        slots = slot_of_block[layer * PER_LAYER : (layer + 1) * PER_LAYER]
        gains = gain_values[2 * layer : 2 * layer + 2]
        inputs.append(hidden)
        hidden, *saved = forward_layer(slots, length, hidden, gains, cos, sin, gathered)
        saves.append(saved)

    def send_rows(t):
        return send_to_bands(t[:seq].astype(bf16).reshape(bands, band_rows, D), images, bands, band)

    output_blocks = send_rows(hidden)

    back = back_rows.astype(f32) * valid[:, None]
    per_owner = master.shape[0]
    me = lax.axis_index("dp")
    by_permutes = (
        lax.axis_size("dp") == 8
        and bands == 4
        and images == 3
        and slot_count == slot_of_block.shape[0]
        and per_owner == sum(CHUNKS)
    )
    if by_permutes:
        places, ranks, clean = relative_places(slot_of_block, per_owner, me)
        rank = lax.dynamic_index_in_dim(ranks, me, 0, keepdims=False)
    else:
        places, rank = slot_of_block, jnp.arange(per_owner, dtype=jnp.int32)

    def same(layer, part, back, tiles, *others):
        return (back, tiles) + others

    def backward(layer, back, tiles, between=same):
        normed, q, k, v, st, mixed, mid, n2, gu, wqkv, wout, wgu, wd = saves[layer]
        slots = places[layer * PER_LAYER : (layer + 1) * PER_LAYER]
        fill = spare if layer == LAYERS - 1 else spare[-1:]
        back, gain_two, *tiles = back_ffn(
            slots, fill, back, gain_values[2 * layer + 1 : 2 * layer + 2], (mid, n2, gu, wgu, wd),
            slot_count, tiles,
        )
        back, tiles = between(layer, 0, back, tiles[0])
        d_projected, *tiles = back_attention(
            slots, length, back, cos, sin, (q, k, v, st, mixed, wout), slot_count, [tiles]
        )
        back, tiles, d_projected = between(layer, 1, back, tiles[0], d_projected)
        back, gain_one, *tiles = back_qkv(
            slots, back, gain_values[2 * layer : 2 * layer + 1], d_projected,
            (inputs[layer], normed, wqkv), slot_count, [tiles],
        )
        back, tiles = between(layer, 2, back, tiles[0])
        return back, [gain_one, gain_two], [tiles]

    if by_permutes:
        sequence = Sequence()
        chunk = [Chunk(i) for i in range(len(CHUNKS))]
        rounds = [
            [(0, "core")],
            [(0, "plane")],
            [(0, "turn"), (1, "core")],
            [(0, "meet"), (1, "plane"), (2, "core"), (3, "core")],
            [(0, "part"), (1, "turn"), (2, "plane")],
        ]

        def between(layer, part, back, tiles, *others):
            nonlocal output_blocks
            after = 3 * (LAYERS - 1 - layer) + part
            if after == len(rounds):
                return (back, tiles) + others
            if after == 3:
                *output_blocks, back = lax.optimization_barrier(output_blocks + (back,))
            tiles, back, *others = sequence.round(
                [(chunk[i], name) for i, name in rounds[after]], tiles, back, *others
            )
            return (back, tiles) + tuple(others)

        back, gains_top, tiles = backward(1, back, [], between)
        back, gains_bottom, tiles = backward(0, back, tiles, between)
        gains = jnp.concatenate(gains_bottom + gains_top, 0).reshape(-1, BLOCK)
        chunk[GAIN_CHUNK].extra = gains
        for steps in (
            [(4, "core"), (1, "meet"), (0, "last")],
            [(2, "turn"), (3, "plane"), (5, "core")],
            [(2, "meet"), (4, "plane")],
            [(1, "part")],
            [(3, "turn")],
            [(0, "end"), (2, "part"), (1, "last")],
            [(3, "meet"), (5, "plane")],
            [(4, "turn")],
            [(2, "last"), (1, "end")],
            [(4, "meet"), (5, "turn")],
            [(3, "part")],
            [(5, "meet")],
            [(4, "part")],
            [(3, "last"), (2, "end")],
            [(5, "part")],
            [(4, "last"), (3, "end")],
            [(5, "last")],
            [(4, "end")],
            [(5, "end")],
        ):
            tiles = sequence.round([(chunk[i], name) for i, name in steps], *tiles)
            if steps[0] == (4, "core"):
                input_blocks = send_rows(back)
            if steps[0] == (2, "meet"):
                input_blocks = lax.optimization_barrier(input_blocks + sequence.before)
                sequence.before = sequence.before + input_blocks[:bands]
        whole = jnp.concatenate([chunk[i].total[: CHUNKS[i]] for i in range(len(CHUNKS))], 0)

        def again(trip, total):
            _, everything = lax.optimization_barrier((trip, tiles[0]))
            parts = [Chunk(i) for i in range(GAIN_CHUNK)]
            reduce_all(parts, everything)
            return jnp.concatenate([part.total for part in parts] + [total[STARTS[GAIN_CHUNK] :]], 0)

        owned = lax.fori_loop(0, jnp.where(clean, 0, 1), again, whole)
        gain_total = join_wide(chunk[GAIN_CHUNK].total[-1:], gains.shape[0]).reshape(-1, D)
    else:
        back, gains_top, tiles = backward(1, back, [])
        back, gains_bottom, tiles = backward(0, back, tiles)
        owned = lax.psum_scatter(tiles[0], "dp", scatter_dimension=0, tiled=True)
        owned = lax.psum(owned, "band")
        gain_total = lax.psum(jnp.concatenate(gains_bottom + gains_top, 0), ("dp", "band"))
        input_blocks = send_rows(back)

    layer_output = at_bands(output_blocks, images, bands, band)
    input_grad = at_bands(input_blocks[:bands], images, bands, band)
    owned_f = owned.astype(f32)
    owned_squares = lax.psum(jnp.sum(owned_f * owned_f), "dp")
    grad_norm = jnp.sqrt(owned_squares + jnp.sum(gain_total * gain_total))
    factor = jnp.minimum(1.0, clip_limit / grad_norm)
    weight_grads, new_statistics, new_master, master_copy = optimizer(
        factor.reshape(1), rank, owned, master, statistics, inverse_roots
    )
    gain_grads = gain_total * factor
    new_moments = decay_rate * gain_moments + (1.0 - decay_rate) * gain_grads * gain_grads
    new_gains = gain_values - gain_rate * gain_grads / (jnp.sqrt(new_moments) + epsilon)
    return (
        layer_output,
        input_grad,
        weight_grads,
        grad_norm,
        new_statistics,
        new_master,
        master_copy,
        gain_grads,
        new_moments,
        new_gains,
    )


def solution(mesh):
    return jax.shard_map(
        shards,
        mesh=mesh,
        in_specs=(
            P("dp", "band", None),
            P("dp", "band", None),
            P("dp"),
            P(),
            P("dp", None, None),
            P("dp", None, None, None),
            P("dp", None, None, None),
            P(),
            P(),
        ),
        out_specs=(
            P("dp", "band", None),
            P("dp", "band", None),
            P("dp", None, None),
            P(),
            P("dp", None, None, None),
            P("dp", None, None),
            P("dp", None, None),
            P(),
            P(),
            P(),
        ),
        check_vma=False,
    )
```

```python
import functools

import jax
import jax.numpy as jnp
from jax import lax
from jax.experimental import pallas as pl
from jax.experimental.pallas import tpu as pltpu
from jax.sharding import PartitionSpec as P

D = 768
HEADS = 12
HEAD_DIM = 64
FF = 2048
LAYERS = 2
BLOCK = 128
PAIR = 2 * HEAD_DIM

epsilon = 1e-05
rope_base = 10000.0
decay_rate = 0.5
step_rate = 0.4
gain_rate = 0.2
clip_limit = 1.0
masked_score = -1e30
VMEM_BYTES = 62 * 2**20

f32 = jnp.float32
bf16 = jnp.bfloat16

GRIDS = [
    (D // BLOCK, 3 * D // BLOCK),
    (D // BLOCK, D // BLOCK),
    (D // BLOCK, 2 * FF // BLOCK),
    (FF // BLOCK, D // BLOCK),
]
COUNTS = [r * c for r, c in GRIDS]
OFFSETS = [sum(COUNTS[:i]) for i in range(4)]
PER_LAYER = sum(COUNTS)
FF_STEP = 512


def round_up(n, m):
    return -(-n // m) * m


def nn(a, b):
    return lax.dot_general(a, b, (((1,), (0,)), ((), ())), preferred_element_type=f32)


def nt(a, b):
    return lax.dot_general(a, b, (((1,), (1,)), ((), ())), preferred_element_type=f32)


def tn(a, b):
    return lax.dot_general(a, b, (((0,), (0,)), ((), ())), preferred_element_type=f32)


def query_blocks(rows, step=256):
    return [(s, min(s + step, rows)) for s in range(0, rows, step)]


def swap_halves(t):
    lane = lax.broadcasted_iota(jnp.int32, t.shape, 1)
    half = HEAD_DIM // 2
    return jnp.where(lane % HEAD_DIM < half, pltpu.roll(t, PAIR - half, 1), pltpu.roll(t, half, 1))


def rms(m):
    return lax.rsqrt(jnp.mean(m * m, -1, keepdims=True) + epsilon)


def rms_back(u, m, g):
    r = rms(m)
    t = u * g
    dot = jnp.mean(t * m, -1, keepdims=True)
    return r * t - m * (r * r * r * dot), jnp.sum(u * m * r, 0, keepdims=True)


def copies(pairs, sem):
    return [pltpu.make_async_copy(src, dst, sem.at[i]) for i, (src, dst) in enumerate(pairs)]


def forward_kernel(
    slots, length, x_ref, g_ref, cos_ref, sin_ref, w_hbm,
    xn_ref, normed_o, q_o, k_o, v_o, st_o, mixed_o, mid_o, n2_o, gu_o, wqkv_o, wout_o, wgu_o, wd_o,
    normed_ref, q_ref, k_ref, v_ref, st_ref, mixed_ref, mid_ref, n2_ref, gu_ref,
    wqkv, wout, wgu, wd, bias, sem_in, sem_out,
):
    rows = x_ref.shape[0]
    key_rows = q_ref.shape[0]
    held = (wqkv, wout, wgu, wd)
    for m in range(4):
        tile_rows, tile_cols = GRIDS[m]

        @pl.loop(0, tile_rows)
        def _(i, m=m, tile_cols=tile_cols):
            for j in range(tile_cols):
                slot = slots[OFFSETS[m] + i * tile_cols + j]
                pltpu.make_async_copy(
                    w_hbm.at[slot],
                    held[m].at[pl.ds(pl.multiple_of(i * BLOCK, BLOCK), BLOCK), pl.ds(j * BLOCK, BLOCK)],
                    sem_in.at[m],
                ).start()

    def arrive(m):
        pltpu.make_async_copy(held[m], held[m], sem_in.at[m]).wait()

    saves = copies(
        [
            (normed_ref, normed_o), (q_ref, q_o), (k_ref, k_o), (v_ref, v_o), (st_ref, st_o),
            (mixed_ref, mixed_o), (mid_ref, mid_o), (n2_ref, n2_o), (gu_ref, gu_o),
            (wqkv, wqkv_o), (wout, wout_o), (wgu, wgu_o), (wd, wd_o),
        ],
        sem_out,
    )
    query = lax.broadcasted_iota(jnp.int32, bias.shape, 0)
    key = lax.broadcasted_iota(jnp.int32, bias.shape, 1)
    bias[...] = jnp.where((key <= query) & (key < length[0]), 0.0, masked_score)
    x = x_ref[...]
    normed_ref[...] = (x * rms(x) * g_ref[0:1, :]).astype(bf16)
    saves[0].start()
    tail = key_rows - rows
    for ref in (q_ref, k_ref, v_ref):
        ref[rows:, :] = jnp.zeros((tail, D), bf16)
    arrive(0)
    saves[9].start()

    @pl.loop(0, 2)
    def _(part):
        acc = nn(normed_ref[...], wqkv[:, pl.ds(pl.multiple_of(part * D, D), D)])
        scale = jnp.where(part == 0, HEAD_DIM ** (-0.5), 1.0)
        for p in range(HEADS // 2):
            t = acc[:, p * PAIR : (p + 1) * PAIR]
            rot = ((t * cos_ref[...] + swap_halves(t) * sin_ref[...]) * scale).astype(bf16)

            @pl.when(part == 0)
            def _(p=p, rot=rot):
                q_ref[0:rows, p * PAIR : (p + 1) * PAIR] = rot

            @pl.when(part == 1)
            def _(p=p, rot=rot):
                k_ref[0:rows, p * PAIR : (p + 1) * PAIR] = rot

    v_ref[0:rows, :] = nn(normed_ref[...], wqkv[:, 2 * D :]).astype(bf16)
    for i in (1, 2, 3):
        saves[i].start()
    st_ref[...] = jnp.zeros(st_ref.shape, f32)

    @pl.loop(0, HEADS // 2)
    def _(p):
        cols = pl.ds(pl.multiple_of(p * PAIR, PAIR), PAIR)
        kp = k_ref[:, cols]
        vp = v_ref[:, cols]
        low = lax.broadcasted_iota(jnp.int32, kp.shape, 1) < HEAD_DIM
        keys = (jnp.where(low, kp, 0), jnp.where(low, 0, kp))
        values = (jnp.where(low, vp, 1), jnp.where(low, 1, vp))
        for q0, q1 in query_blocks(rows):
            kend = min(round_up(q1, BLOCK), key_rows)
            qp = q_ref[q0:q1, cols]
            mask = bias[q0:q1, :kend]
            parts = []
            tops = []
            for h in range(2):
                s = nt(qp, keys[h][:kend]) + mask
                top = jnp.max(s, -1, keepdims=True)
                e = jnp.exp(s - top).astype(bf16)
                parts.append(nn(e, values[h][:kend]))
                tops.append(top)
            lane = lax.broadcasted_iota(jnp.int32, parts[0].shape, 1)
            low_q = lane < HEAD_DIM
            total = pltpu.roll(jnp.where(low_q, parts[1], parts[0]), HEAD_DIM, 1)
            mixed_ref[q0:q1, cols] = (jnp.where(low_q, parts[0], parts[1]) / total).astype(bf16)
            log_total = jnp.log(total)
            other = pltpu.roll(log_total, HEAD_DIM, 1)
            first = tops[0] + jnp.where(low_q, log_total, other)
            second = tops[1] + jnp.where(low_q, other, log_total)
            old = st_ref[q0:q1, :]
            st_ref[q0:q1, :] = jnp.where(
                lane == 2 * p, first, jnp.where(lane == 2 * p + 1, second, old)
            )

    saves[4].start()
    saves[5].start()
    arrive(1)
    saves[10].start()
    middle = x_ref[...] + nn(mixed_ref[...], wout[...])
    mid_ref[...] = middle
    saves[6].start()
    n2_ref[...] = (middle * rms(middle) * g_ref[1:2, :]).astype(bf16)
    saves[7].start()
    arrive(2)
    saves[11].start()
    arrive(3)
    saves[12].start()
    xn_ref[...] = mid_ref[...]

    @pl.loop(0, FF // FF_STEP)
    def _(t):
        at = pl.multiple_of(t * FF_STEP, FF_STEP)
        gate = nn(n2_ref[...], wgu[:, pl.ds(at, FF_STEP)])
        up = nn(n2_ref[...], wgu[:, pl.ds(FF + at, FF_STEP)])
        act = (gate / (1.0 + jnp.exp(-gate)) * up).astype(bf16)
        gu_ref[:, pl.ds(at, FF_STEP)] = gate.astype(bf16)
        gu_ref[:, pl.ds(FF + at, FF_STEP)] = up.astype(bf16)
        xn_ref[...] += nn(act, wd[pl.ds(at, FF_STEP), :])

    saves[8].start()
    for save in saves:
        save.wait()


def put_tiles(places, zones, m, grad, outs, sem, i0, i1, j0, count_j):
    @pl.loop(i0, i1)
    def _(i):
        for jj in range(count_j):
            j = j0 + jj
            place = places[OFFSETS[m] + i * GRIDS[m][1] + j]
            tile = grad.at[
                pl.ds(pl.multiple_of(i * BLOCK, BLOCK), BLOCK),
                pl.ds(pl.multiple_of(j * BLOCK, BLOCK), BLOCK),
            ]
            if len(outs) == 1:
                pltpu.make_async_copy(tile, outs[0].at[place], sem).start()
                continue
            for out, (low, high, _) in zip(outs, zones):

                @pl.when((place >= low) & (place < high))
                def _(tile=tile, out=out, place=place, low=low):
                    pltpu.make_async_copy(tile, out.at[place - low], sem).start()


def back_ffn_kernel(
    begun, zones, places, spare, back_ref, g_ref, mid_i, n2_i, gu_i, wgu_i, wd_i, *rest
):
    mid_ref_out, gain_ref, *rest = rest[begun:]
    tiles_out, rest = rest[: len(zones)], rest[len(zones) :]
    mid_ref, n2_ref, gu_ref, wgu, wd, ggu, gd, big, zero, sem_in, sem_out, sem_zero = rest
    loads = copies([(wd_i, wd), (gu_i, gu_ref), (n2_i, n2_ref), (wgu_i, wgu), (mid_i, mid_ref)], sem_in)
    for load in loads:
        load.start()
    spares = spare.shape[0] - 1
    if spares > 0:
        zero[...] = jnp.zeros(zero.shape, bf16)

        @pl.loop(0, spares)
        def _(i):
            pltpu.make_async_copy(zero, tiles_out[0].at[spare[i]], sem_zero).start()

    big[...] = jnp.zeros(big.shape, f32)
    for load in loads[:4]:
        load.wait()
    put = functools.partial(put_tiles, places, zones)

    @pl.loop(0, FF // FF_STEP)
    def _(t):
        at = pl.multiple_of(t * FF_STEP, FF_STEP)
        here = pl.ds(at, FF_STEP)
        there = pl.ds(FF + at, FF_STEP)
        back_ffn = back_ref[...].astype(bf16)
        d_act = nt(back_ffn, wd[here, :])
        gate = gu_ref[:, here].astype(f32)
        up = gu_ref[:, there].astype(f32)
        sig = 1.0 / (1.0 + jnp.exp(-gate))
        silu = gate * sig
        act = (silu * up).astype(bf16)
        d_gate = (d_act * up * (sig * (1.0 + gate * (1.0 - sig)))).astype(bf16)
        d_up = (d_act * silu).astype(bf16)
        gd[here, :] = tn(act, back_ffn).astype(bf16)
        ggu[:, here] = tn(n2_ref[...], d_gate).astype(bf16)
        ggu[:, there] = tn(n2_ref[...], d_up).astype(bf16)
        per = FF_STEP // BLOCK
        put(3, gd, tiles_out, sem_out.at[1], t * per, (t + 1) * per, 0, D // BLOCK)
        put(2, ggu, tiles_out, sem_out.at[0], 0, D // BLOCK, t * per, per)
        put(2, ggu, tiles_out, sem_out.at[0], 0, D // BLOCK, FF // BLOCK + t * per, per)
        big[...] += nt(d_gate, wgu[:, here]) + nt(d_up, wgu[:, there])

    loads[4].wait()
    step, gain = rms_back(big[...], mid_ref[...], g_ref[...])
    gain_ref[...] = gain
    mid_ref_out[...] = back_ref[...] + step
    pltpu.make_async_copy(ggu, ggu, sem_out.at[0]).wait()
    pltpu.make_async_copy(gd, gd, sem_out.at[1]).wait()
    if spares > 0:

        @pl.loop(0, spares)
        def _(i):
            pltpu.make_async_copy(zero, tiles_out[0].at[spare[i]], sem_zero).wait()


def back_attention_kernel(
    begun, zones, places, length, back_ref, cos_ref, sin_ref,
    q_i, k_i, v_i, st_i, mixed_i, wout_i, *rest
):
    dproj, *rest = rest[begun:]
    tiles_out, rest = rest[: len(zones)], rest[len(zones) :]
    (
        q_ref, k_ref, v_ref, st_ref, mixed_ref, wout,
        gout, bias, turned, sums, mixed_back, sem_in, sem_out,
    ) = rest
    rows = back_ref.shape[0]
    key_rows = q_ref.shape[0]
    loads = copies(
        [
            (wout_i, wout), (mixed_i, mixed_ref), (q_i, q_ref), (k_i, k_ref), (v_i, v_ref),
            (st_i, st_ref),
        ],
        sem_in,
    )
    for load in loads:
        load.start()
    put = functools.partial(put_tiles, places, zones)
    key = lax.broadcasted_iota(jnp.int32, bias.shape, 0)
    query = lax.broadcasted_iota(jnp.int32, bias.shape, 1)
    bias[...] = jnp.where((key <= query) & (key < length[0]), 0.0, masked_score)
    back_attn = back_ref[...].astype(bf16)
    loads[0].wait()
    mixed_back[0:rows, :] = nt(back_attn, wout[...]).astype(bf16)
    mixed_back[rows:, :] = jnp.zeros((key_rows - rows, D), bf16)
    loads[1].wait()
    gout[...] = tn(mixed_ref[...], back_attn).astype(bf16)
    put(1, gout, tiles_out, sem_out, 0, D // BLOCK, 0, D // BLOCK)
    for load in loads[2:]:
        load.wait()
    levels = st_ref[...].T
    for h in range(HEADS):
        turned[h] = levels[h : h + 1, :]

    @pl.loop(0, HEADS // 2)
    def _(p):
        cols = pl.ds(pl.multiple_of(p * PAIR, PAIR), PAIR)
        low = lax.broadcasted_iota(jnp.int32, (key_rows, PAIR), 1) < HEAD_DIM

        def both(t):
            return (jnp.where(low, t, 0), jnp.where(low, 0, t))

        qp = q_ref[:, cols]
        op = mixed_back[:, cols]
        keys, values, queries, backs = both(k_ref[:, cols]), both(v_ref[:, cols]), both(qp), both(op)
        sums[...] = jnp.zeros(sums.shape, f32)
        for q0, q1 in query_blocks(key_rows):
            kend = q1
            d_query = jnp.zeros((q1 - q0, PAIR), f32)
            d_key = jnp.zeros((kend, PAIR), f32)
            d_value = jnp.zeros((kend, PAIR), f32)
            for h in range(2):
                level = turned[2 * p + h, :, q0:q1]
                soft = jnp.exp(nt(keys[h][:kend], qp[q0:q1]) + bias[:kend, q0:q1] - level)
                d_prob = nt(values[h][:kend], op[q0:q1])
                row_dot = jnp.sum(soft * d_prob, 0, keepdims=True)
                d_score = (soft * (d_prob - row_dot)).astype(bf16)
                d_value += nn(soft.astype(bf16), backs[h][q0:q1])
                d_key += nn(d_score, queries[h][q0:q1])
                d_query += tn(d_score, keys[h][:kend])
            sums[0, q0:q1, :] += d_query * HEAD_DIM ** (-0.5)
            sums[1, :kend, :] += d_key
            sums[2, :kend, :] += d_value
        for part in range(2):
            t = sums[part, 0:rows, :]
            dproj[:, pl.ds(pl.multiple_of(part * D + p * PAIR, PAIR), PAIR)] = (
                t * cos_ref[...] - swap_halves(t) * sin_ref[...]
            ).astype(bf16)
        dproj[:, pl.ds(pl.multiple_of(2 * D + p * PAIR, PAIR), PAIR)] = sums[2, 0:rows, :].astype(bf16)

    pltpu.make_async_copy(gout, gout, sem_out).wait()


def back_qkv_kernel(begun, zones, places, back_ref, g_ref, dproj, x_i, normed_i, wqkv_i, *rest):
    dx_ref, gain_ref, *rest = rest[begun:]
    tiles_out, rest = rest[: len(zones)], rest[len(zones) :]
    x_ref, normed_ref, wqkv, gqkv, big, sem_in, sem_out = rest
    loads = copies([(normed_i, normed_ref), (wqkv_i, wqkv), (x_i, x_ref)], sem_in)
    for load in loads:
        load.start()
    big[...] = jnp.zeros(big.shape, f32)
    loads[0].wait()
    loads[1].wait()

    @pl.loop(0, 3)
    def _(part):
        cols = pl.ds(pl.multiple_of(part * D, D), D)
        gqkv[:, cols] = tn(normed_ref[...], dproj[:, cols]).astype(bf16)
        put_tiles(places, zones, 0, gqkv, tiles_out, sem_out, 0, D // BLOCK, part * (D // BLOCK), D // BLOCK)
        big[...] += nt(dproj[:, cols], wqkv[:, cols])

    loads[2].wait()
    step, gain = rms_back(big[...], x_ref[...], g_ref[...])
    gain_ref[...] = gain
    dx_ref[...] = back_ref[...] + step
    pltpu.make_async_copy(gqkv, gqkv, sem_out).wait()


def weight_shapes():
    return [(r * BLOCK, c * BLOCK) for r, c in GRIDS]


VMEM = pl.BlockSpec(memory_space=pltpu.VMEM)
SMEM = pl.BlockSpec(memory_space=pltpu.SMEM)
HBM = pl.BlockSpec(memory_space=pl.ANY)


def like(struct):
    return pltpu.VMEM(struct.shape, struct.dtype)


def cost(flops, bytes_accessed):
    return pl.CostEstimate(flops=flops, bytes_accessed=bytes_accessed, transcendentals=0)


def forward_layer(slots, length, x, gains, cos, sin, gathered):
    rows = x.shape[0]
    key_rows = round_up(rows, BLOCK)
    S = jax.ShapeDtypeStruct
    saved = [
        S((rows, D), bf16),
        S((key_rows, D), bf16),
        S((key_rows, D), bf16),
        S((key_rows, D), bf16),
        S((key_rows, BLOCK), f32),
        S((rows, D), bf16),
        S((rows, D), f32),
        S((rows, D), bf16),
        S((rows, 2 * FF), bf16),
    ] + [S(s, bf16) for s in weight_shapes()]
    return pl.pallas_call(
        forward_kernel,
        out_shape=[S((rows, D), f32)] + saved,
        in_specs=[SMEM, SMEM, VMEM, VMEM, VMEM, VMEM, HBM],
        out_specs=[VMEM] + [HBM] * 13,
        scratch_shapes=[like(s) for s in saved]
        + [
            pltpu.VMEM((rows, key_rows), f32),
            pltpu.SemaphoreType.DMA((4,)),
            pltpu.SemaphoreType.DMA((13,)),
        ],
        compiler_params=pltpu.CompilerParams(vmem_limit_bytes=VMEM_BYTES),
        cost_estimate=cost(2 * rows * PER_LAYER * BLOCK * BLOCK, 40 * 2**20),
        name="forward_block",
    )(slots, length, x, gains, cos, sin, gathered)


def tile_arrays(zones):
    return [jax.ShapeDtypeStruct((size, BLOCK, BLOCK), bf16) for _, _, size in zones]


def in_place(args, begun, zones, first):
    late = first + len(zones) - len(begun)
    return {len(args) + i: late + i for i in range(len(begun))}


def back_ffn(places, spare, back, gain, saved, zones, begun):
    rows = back.shape[0]
    S = jax.ShapeDtypeStruct
    args = (places, spare, back, gain) + tuple(saved)
    wgu, wd = saved[3], saved[4]
    return pl.pallas_call(
        functools.partial(back_ffn_kernel, len(begun), zones),
        out_shape=[S((rows, D), f32), S((1, D), f32)] + tile_arrays(zones),
        in_specs=[SMEM] * 2 + [VMEM] * 2 + [HBM] * (5 + len(begun)),
        out_specs=[VMEM, VMEM] + [HBM] * len(zones),
        input_output_aliases=in_place(args, begun, zones, 2),
        scratch_shapes=[like(s) for s in saved]
        + [like(wgu), like(wd)]
        + [
            pltpu.VMEM((rows, D), f32),
            pltpu.VMEM((BLOCK, BLOCK), bf16),
            pltpu.SemaphoreType.DMA((5,)),
            pltpu.SemaphoreType.DMA((2,)),
            pltpu.SemaphoreType.DMA,
        ],
        compiler_params=pltpu.CompilerParams(vmem_limit_bytes=VMEM_BYTES),
        cost_estimate=cost(4 * rows * (COUNTS[2] + COUNTS[3]) * BLOCK * BLOCK, 30 * 2**20),
        name="backward_feed_forward",
    )(*args, *begun)


def back_attention(places, length, back, cos, sin, saved, zones, begun):
    rows = back.shape[0]
    key_rows = round_up(rows, BLOCK)
    S = jax.ShapeDtypeStruct
    args = (places, length, back, cos, sin) + tuple(saved)
    return pl.pallas_call(
        functools.partial(back_attention_kernel, len(begun), zones),
        out_shape=[S((rows, 3 * D), bf16)] + tile_arrays(zones),
        in_specs=[SMEM] * 2 + [VMEM] * 3 + [HBM] * (6 + len(begun)),
        out_specs=[VMEM] + [HBM] * len(zones),
        input_output_aliases=in_place(args, begun, zones, 1),
        scratch_shapes=[like(s) for s in saved]
        + [
            like(saved[5]),
            pltpu.VMEM((key_rows, key_rows), f32),
            pltpu.VMEM((HEADS, 1, key_rows), f32),
            pltpu.VMEM((3, key_rows, PAIR), f32),
            pltpu.VMEM((key_rows, D), bf16),
            pltpu.SemaphoreType.DMA((6,)),
            pltpu.SemaphoreType.DMA,
        ],
        compiler_params=pltpu.CompilerParams(vmem_limit_bytes=VMEM_BYTES),
        cost_estimate=cost(4 * rows * COUNTS[1] * BLOCK * BLOCK + 20 * rows * rows * D, 30 * 2**20),
        name="backward_attention",
    )(*args, *begun)


def back_qkv(places, back, gain, d_projected, saved, zones, begun):
    rows = back.shape[0]
    S = jax.ShapeDtypeStruct
    args = (places, back, gain, d_projected) + tuple(saved)
    return pl.pallas_call(
        functools.partial(back_qkv_kernel, len(begun), zones),
        out_shape=[S((rows, D), f32), S((1, D), f32)] + tile_arrays(zones),
        in_specs=[SMEM] + [VMEM] * 3 + [HBM] * (3 + len(begun)),
        out_specs=[VMEM, VMEM] + [HBM] * len(zones),
        input_output_aliases=in_place(args, begun, zones, 2),
        scratch_shapes=[like(s) for s in saved]
        + [
            like(saved[2]),
            pltpu.VMEM((rows, D), f32),
            pltpu.SemaphoreType.DMA((3,)),
            pltpu.SemaphoreType.DMA,
        ],
        compiler_params=pltpu.CompilerParams(vmem_limit_bytes=VMEM_BYTES),
        cost_estimate=cost(4 * rows * COUNTS[0] * BLOCK * BLOCK, 20 * 2**20),
        name="backward_qkv",
    )(*args, *begun)


def optimizer_kernel(factor, rank, g_ref, m_ref, s_ref, r_ref, wg_ref, ns_ref, nm_ref, nc_ref):
    f = factor[0]
    count = m_ref.shape[0]
    for i in range(count):
        gb = g_ref[rank[pl.program_id(0) * count + i]]
        wg_ref[i] = gb.astype(f32) * f
        half = (1.0 - decay_rate) * f * f
        ns_ref[i, 0] = decay_rate * s_ref[i, 0] + half * nt(gb, gb)
        ns_ref[i, 1] = decay_rate * s_ref[i, 1] + half * tn(gb, gb)
        left = nn(r_ref[i, 0].astype(bf16), (gb.astype(f32) * f).astype(bf16)).astype(bf16)
        new = m_ref[i] - step_rate * nn(left, r_ref[i, 1].astype(bf16))
        nm_ref[i] = new
        nc_ref[i] = new.astype(bf16)


def optimizer(factor, rank, owned, master, statistics, inverse_roots):
    count = owned.shape[0]
    per = max(n for n in range(1, 13) if count % n == 0)
    S = jax.ShapeDtypeStruct
    one = pl.BlockSpec((per, BLOCK, BLOCK), lambda i: (i, 0, 0))
    two = pl.BlockSpec((per, 2, BLOCK, BLOCK), lambda i: (i, 0, 0, 0))
    return pl.pallas_call(
        optimizer_kernel,
        grid=(count // per,),
        out_shape=[
            S(master.shape, f32),
            S(statistics.shape, f32),
            S(master.shape, f32),
            S(master.shape, bf16),
        ],
        in_specs=[SMEM, SMEM, VMEM, one, two, two],
        out_specs=[one, two, one, one],
        compiler_params=pltpu.CompilerParams(vmem_limit_bytes=VMEM_BYTES),
        name="optimizer",
    )(factor, rank, owned, master, statistics, inverse_roots)


def to_images(local, bands, band):
    images, band_rows = local.shape[0], local.shape[-2]
    padded = jnp.concatenate([local, jnp.zeros((bands - images,) + local.shape[1:], local.dtype)], 0)
    whole = jnp.zeros((bands,) + local.shape[1:], local.dtype)
    for shift in range(bands):
        block = lax.dynamic_index_in_dim(padded, (band + shift) % bands, 0, keepdims=False)
        if shift > 0:
            pairs = [(b, (b + shift) % bands) for b in range(bands) if (b + shift) % bands < images]
            block = lax.ppermute(block, "band", pairs)
        whole = lax.dynamic_update_index_in_dim(whole, block, (band - shift) % bands, 0)
    return whole


def send_to_bands(whole, images, bands, band):
    blocks = []
    for shift in range(bands):
        block = lax.dynamic_index_in_dim(whole, (band + shift) % bands, 0, keepdims=False)
        if shift > 0:
            pairs = [(b, (b + shift) % bands) for b in range(images)]
            block = lax.ppermute(block, "band", pairs)
        blocks.append(block)
    return tuple(blocks)


def at_bands(blocks, images, bands, band):
    local = jnp.zeros((bands,) + blocks[0].shape, blocks[0].dtype)
    for shift, block in enumerate(blocks):
        local = lax.dynamic_update_index_in_dim(local, block, (band - shift) % bands, 0)
    return local[:images]


EARLY = (22, 18, 38)
LATE = (18, 12)
FFN_FIRST = OFFSETS[2]
LEAST = (PER_LAYER + FFN_FIRST, PER_LAYER, FFN_FIRST)


def chunk_places(slot_of_block, per_owner, me):
    blocks = slot_of_block.shape[0]
    block_of_slot = jnp.zeros((blocks,), jnp.int32).at[slot_of_block].set(
        jnp.arange(blocks, dtype=jnp.int32)
    )
    by_owner = block_of_slot.reshape(-1, per_owner)
    rank = jnp.sum(by_owner[:, None, :] > by_owner[:, :, None], -1, dtype=jnp.int32)
    owner = jnp.arange(by_owner.shape[0], dtype=jnp.int32)
    relative = (owner ^ me)[:, None]
    owner = owner[:, None]
    core, x, y = relative % 2, relative // 2 % 2, relative // 4
    place = jnp.zeros_like(rank)
    clean = jnp.bool_(True)
    start = 0
    for size, least in zip(EARLY, LEAST):
        at = rank - start
        here = (at >= 0) & (at < size)
        place = jnp.where(here, 8 * start + owner * size + at, place)
        clean = clean & jnp.all(jnp.where(here, by_owner >= least, True))
        start += size
    base = 8 * start + core * 4 * sum(LATE)
    for size in LATE:
        half = size // 2
        at = rank - start
        here = (at >= 0) & (at < size)
        spot = jnp.where(at < half, (x * 2 + y) * half + at, 4 * half + (y * 2 + x) * half + at - half)
        place = jnp.where(here, base + spot, place)
        start += size
        base += 4 * size
    return place.reshape(-1)[slot_of_block], rank, clean


CORE = [(i, i ^ 1) for i in range(8)]
ALONG_X = [(i, i ^ 2) for i in range(8)]
ALONG_Y = [(i, i ^ 4) for i in range(8)]


def wide(t, lo, hi):
    return t[lo:hi].astype(f32)


class Bands:
    def to_meet(self, plane):
        self.plane = plane
        return (plane,)

    def go_meet(self, plane):
        return lax.ppermute(plane, "band", [(0, 1)]), lax.ppermute(plane, "band", [(2, 1)])

    def to_part(self, up, down):
        self.total = (self.plane.astype(f32) + up.astype(f32) + down.astype(f32)).astype(bf16)
        return (self.total,)

    def go_part(self, total):
        return lax.ppermute(total, "band", [(1, 0)]), lax.ppermute(total, "band", [(1, 2)])

    def to_last(self, to_first, to_third):
        self.to_first, self.to_third = to_first, to_third
        return (to_third,)

    def go_last(self, to_third):
        return (lax.ppermute(to_third, "band", [(2, 3)]),)

    def to_end(self, to_last):
        band = lax.axis_index("band")
        total = jnp.where(band == 0, self.to_first, self.total)
        total = jnp.where(band == 2, self.to_third, total)
        self.total = jnp.where(band == 3, to_last, total)
        return ()

    def go_end(self):
        return ()


class Chunk(Bands):
    def __init__(self, index, kept, sent):
        size, at = LATE[index], 4 * sum(LATE[:index])
        self.half = size // 2
        self.kept, self.sent = kept[at : at + 4 * size], sent[at : at + 4 * size]

    def chip(self, lo, hi):
        lo, hi = lo * self.half, hi * self.half
        return wide(self.kept, lo, hi) + wide(self.received, lo, hi)

    def to_core(self):
        return (self.sent,)

    def go_core(self, send):
        return (lax.ppermute(send, "dp", CORE),)

    def to_plane(self, received):
        self.received = received
        return self.chip(2, 4).astype(bf16), self.chip(6, 8).astype(bf16)

    def go_plane(self, send_x, send_y):
        return lax.ppermute(send_x, "dp", ALONG_X), lax.ppermute(send_y, "dp", ALONG_Y)

    go_turn = go_plane

    def to_turn(self, from_x, from_y):
        self.from_x, self.from_y = from_x, from_y
        half = self.half
        send_y = (self.chip(1, 2) + wide(from_x, half, 2 * half)).astype(bf16)
        send_x = (self.chip(5, 6) + wide(from_y, half, 2 * half)).astype(bf16)
        return send_x, send_y

    def to_meet(self, from_x, from_y):
        half = self.half
        one = self.chip(0, 1) + wide(self.from_x, 0, half) + wide(from_y, 0, half)
        two = self.chip(4, 5) + wide(self.from_y, 0, half) + wide(from_x, 0, half)
        self.plane = jnp.concatenate([one, two], 0).astype(bf16)
        return (self.plane,)


class Sequence:
    def __init__(self):
        self.before = ()
        self.arrived = {}

    def round(self, *steps):
        arrived = [tuple(self.arrived.get(chunk, ())) for chunk, _ in steps]
        flat = sum(arrived, ())
        flat = lax.optimization_barrier(flat + self.before)
        at, self.before = 0, ()
        for (chunk, name), had in zip(steps, arrived):
            sends = getattr(chunk, "to_" + name)(*flat[at : at + len(had)])
            at += len(had)
            self.arrived[chunk] = getattr(chunk, "go_" + name)(*sends)
            self.before = self.before + tuple(sends)

    def wait_for(self, *arrays):
        arrays = lax.optimization_barrier(arrays + self.before)[: len(arrays)]
        self.before = self.before + arrays
        return arrays


def rope_tables(rows):
    half = HEAD_DIM // 2
    frequency = rope_base ** (-(jnp.arange(half, dtype=f32) * 2.0 / HEAD_DIM))
    angles = jnp.arange(rows, dtype=jnp.int32).astype(f32)[:, None] * frequency[None, :]
    cosine, sine = jnp.cos(angles), jnp.sin(angles)
    return jnp.tile(cosine, (1, 4)), jnp.tile(jnp.concatenate([-sine, sine], 1), (1, 2))


def shards(
    tokens,
    cotangent,
    lengths,
    slot_of_block,
    master,
    statistics,
    inverse_roots,
    gain_values,
    gain_moments,
):
    images, band_rows, _ = tokens.shape
    band = lax.axis_index("band")
    bands = lax.axis_size("band")
    seq = band_rows * bands
    rows = round_up(seq, 16)
    gathered = lax.all_gather(master.astype(bf16), "dp", axis=0, tiled=True)
    slot_count = gathered.shape[0]

    arrived = to_images(jnp.stack([tokens, cotangent], 1), bands, band)
    token_rows = jnp.pad(arrived[:, 0].reshape(seq, D), ((0, rows - seq), (0, 0)))
    back_rows = jnp.pad(arrived[:, 1].reshape(seq, D), ((0, rows - seq), (0, 0)))
    length = lengths[jnp.minimum(band, images - 1)]
    valid = (jnp.arange(rows, dtype=jnp.int32) < length).astype(f32)
    length = length.reshape(1)
    cos, sin = rope_tables(rows)

    spare_count = slot_count - slot_of_block.shape[0]
    spare = jnp.zeros((1,), jnp.int32)
    if spare_count > 0:
        used = jnp.zeros((slot_count,), jnp.int32).at[slot_of_block].set(1)
        spare = jnp.concatenate([jnp.argsort(used)[:spare_count].astype(jnp.int32), spare])

    hidden = token_rows.astype(f32)
    inputs, saves = [], []
    for layer in range(LAYERS):
        slots = slot_of_block[layer * PER_LAYER : (layer + 1) * PER_LAYER]
        gains = gain_values[2 * layer : 2 * layer + 2]
        inputs.append(hidden)
        hidden, *saved = forward_layer(slots, length, hidden, gains, cos, sin, gathered)
        saves.append(saved)

    def send_rows(t):
        return send_to_bands(t[:seq].astype(bf16).reshape(bands, band_rows, D), images, bands, band)

    output_blocks = send_rows(hidden)

    back = back_rows.astype(f32) * valid[:, None]
    per_owner = master.shape[0]
    me = lax.axis_index("dp")
    by_permutes = (
        lax.axis_size("dp") == 8
        and bands == 4
        and images == 3
        and slot_count == slot_of_block.shape[0]
        and per_owner == sum(EARLY) + sum(LATE)
    )
    if by_permutes:
        places, ranks, clean = chunk_places(slot_of_block, per_owner, me)
        rank = lax.dynamic_index_in_dim(ranks, me, 0, keepdims=False)
        ends = [8 * sum(EARLY[: i + 1]) for i in range(len(EARLY))]
        late = 4 * sum(LATE)
        bounds = [0] + ends + [ends[-1] + late, ends[-1] + 2 * late]
        zones = tuple((low, high, high - low) for low, high in zip(bounds, bounds[1:]))
    else:
        places, rank = slot_of_block, jnp.arange(per_owner, dtype=jnp.int32)
        zones = ((0, slot_count, slot_count),)

    def backward(layer, back, tiles, zones, freeze=lambda kernel, tiles, zones: (tiles, zones)):
        normed, q, k, v, st, mixed, mid, n2, gu, wqkv, wout, wgu, wd = saves[layer]
        slots = places[layer * PER_LAYER : (layer + 1) * PER_LAYER]
        fill = spare if layer == LAYERS - 1 else spare[-1:]
        first = 3 * (LAYERS - 1 - layer)
        back, gain_two, *tiles = back_ffn(
            slots, fill, back, gain_values[2 * layer + 1 : 2 * layer + 2], (mid, n2, gu, wgu, wd),
            zones, tiles,
        )
        tiles, zones = freeze(first, tiles, zones)
        d_projected, *tiles = back_attention(
            slots, length, back, cos, sin, (q, k, v, st, mixed, wout), zones, tiles
        )
        tiles, zones = freeze(first + 1, tiles, zones)
        back, gain_one, *tiles = back_qkv(
            slots, back, gain_values[2 * layer : 2 * layer + 1], d_projected,
            (inputs[layer], normed, wqkv), zones, tiles,
        )
        tiles, zones = freeze(first + 2, tiles, zones)
        return back, [gain_one, gain_two], tiles, zones

    if by_permutes:
        early, early_sums = [], []

        def freeze(kernel, tiles, zones):
            if kernel not in (0, 2, 3):
                return tiles, zones
            at = 0 if kernel == 0 else 1
            nonlocal output_blocks
            early.append(tiles[at])
            ready, *early_sums[:] = lax.optimization_barrier((tiles[at], *early_sums))
            if kernel == 0:
                ready, *output_blocks = lax.optimization_barrier((ready, *output_blocks))
            early_sums.append(lax.psum_scatter(ready, "dp", scatter_dimension=0, tiled=True))
            missed = (0, zones[at][1], ends[-1])
            return tiles[:at] + tiles[at + 1 :], (missed,) + zones[at + 1 :]

        back, gains_top, tiles, zones = backward(1, back, [], zones, freeze)
        back, gains_bottom, tiles, zones = backward(0, back, tiles, zones, freeze)
        missed, kept, sent = tiles
        gains = jnp.concatenate(gains_bottom + gains_top, 0).astype(bf16).reshape(-1, BLOCK)
        gains = jnp.pad(gains, ((0, BLOCK - gains.shape[0]), (0, 0)))[None]
        sequence = Sequence()
        one, two = [Chunk(i, kept, sent) for i in range(len(LATE))]
        top, bottom = Bands(), Bands()
        sequence.arrived[top] = (jnp.concatenate(early_sums[:2] + [gains], 0),)
        sequence.arrived[bottom] = (early_sums[2],)
        input_blocks = send_rows(back)
        sequence.round((one, "core"), (two, "core"), (top, "meet"))
        sequence.round((one, "plane"))
        sequence.round((one, "turn"))
        input_blocks = sequence.wait_for(*input_blocks)
        sequence.round((top, "part"))
        sequence.round((bottom, "meet"))
        sequence.round((one, "meet"), (two, "plane"))
        sequence.round((two, "turn"))
        sequence.round((top, "last"), (bottom, "part"))
        sequence.round((two, "meet"))
        sequence.round((one, "part"))
        sequence.round((bottom, "last"), (top, "end"))
        sequence.round((two, "part"), (one, "last"))
        sequence.round((two, "last"), (bottom, "end"))
        sequence.round((one, "end"), (two, "end"))
        early_total = jnp.concatenate([top.total[:-1], bottom.total], 0)

        def again(trip, total):
            _, spare_tiles, *parts = lax.optimization_barrier((trip, missed, *early))
            block_at = jnp.argsort(places)
            sums, start = [], 0
            for part, end, least in zip(parts, ends, LEAST):
                late_here = (block_at[start:end] < least)[:, None, None]
                whole = jnp.where(late_here, spare_tiles[start:end], part)
                sums.append(lax.psum_scatter(whole, "dp", scatter_dimension=0, tiled=True))
                start = end
            return lax.psum(jnp.concatenate(sums, 0), "band")

        early_total = lax.fori_loop(0, jnp.where(clean, 0, 1), again, early_total)
        owned = jnp.concatenate([early_total, one.total, two.total], 0)
        gain_total = top.total[-1].astype(f32)[: gain_values.size // BLOCK].reshape(-1, D)
        gain_total = lax.psum(gain_total, "dp")
    else:
        back, gains_top, tiles, _ = backward(1, back, [], zones)
        back, gains_bottom, tiles, _ = backward(0, back, tiles, zones)
        owned = lax.psum_scatter(tiles[0], "dp", scatter_dimension=0, tiled=True)
        owned = lax.psum(owned, "band")
        gain_total = lax.psum(jnp.concatenate(gains_bottom + gains_top, 0), ("dp", "band"))
        input_blocks = send_rows(back)

    layer_output = at_bands(output_blocks, images, bands, band)
    input_grad = at_bands(input_blocks[:bands], images, bands, band)
    owned_f = owned.astype(f32)
    owned_squares = lax.psum(jnp.sum(owned_f * owned_f), "dp")
    grad_norm = jnp.sqrt(owned_squares + jnp.sum(gain_total * gain_total))
    factor = jnp.minimum(1.0, clip_limit / grad_norm)
    weight_grads, new_statistics, new_master, master_copy = optimizer(
        factor.reshape(1), rank, owned, master, statistics, inverse_roots
    )
    gain_grads = gain_total * factor
    new_moments = decay_rate * gain_moments + (1.0 - decay_rate) * gain_grads * gain_grads
    new_gains = gain_values - gain_rate * gain_grads / (jnp.sqrt(new_moments) + epsilon)
    return (
        layer_output,
        input_grad,
        weight_grads,
        grad_norm,
        new_statistics,
        new_master,
        master_copy,
        gain_grads,
        new_moments,
        new_gains,
    )


def solution(mesh):
    return jax.shard_map(
        shards,
        mesh=mesh,
        in_specs=(
            P("dp", "band", None),
            P("dp", "band", None),
            P("dp"),
            P(),
            P("dp", None, None),
            P("dp", None, None, None),
            P("dp", None, None, None),
            P(),
            P(),
        ),
        out_specs=(
            P("dp", "band", None),
            P("dp", "band", None),
            P("dp", None, None),
            P(),
            P("dp", None, None, None),
            P("dp", None, None),
            P("dp", None, None),
            P(),
            P(),
            P(),
        ),
        check_vma=False,
    )
```

```python
import functools

import jax
import jax.numpy as jnp
from jax import lax
from jax.experimental import pallas as pl
from jax.experimental.pallas import tpu as pltpu
from jax.sharding import PartitionSpec as P

D = 768
HEADS = 12
HEAD_DIM = 64
FF = 2048
LAYERS = 2
BLOCK = 128
PAIR = 2 * HEAD_DIM

epsilon = 1e-05
rope_base = 10000.0
decay_rate = 0.5
step_rate = 0.4
gain_rate = 0.2
clip_limit = 1.0
masked_score = -1e30
VMEM_BYTES = 62 * 2**20

f32 = jnp.float32
bf16 = jnp.bfloat16

GRIDS = [
    (D // BLOCK, 3 * D // BLOCK),
    (D // BLOCK, D // BLOCK),
    (D // BLOCK, 2 * FF // BLOCK),
    (FF // BLOCK, D // BLOCK),
]
COUNTS = [r * c for r, c in GRIDS]
OFFSETS = [sum(COUNTS[:i]) for i in range(4)]
PER_LAYER = sum(COUNTS)
FF_STEP = 512
TOGETHER = 4


def round_up(n, m):
    return -(-n // m) * m


def nn(a, b):
    return lax.dot_general(a, b, (((1,), (0,)), ((), ())), preferred_element_type=f32)


def nt(a, b):
    return lax.dot_general(a, b, (((1,), (1,)), ((), ())), preferred_element_type=f32)


def tn(a, b):
    return lax.dot_general(a, b, (((0,), (0,)), ((), ())), preferred_element_type=f32)


def query_blocks(rows, step=256):
    return [(s, min(s + step, rows)) for s in range(0, rows, step)]


def swap_halves(t):
    lane = lax.broadcasted_iota(jnp.int32, t.shape, 1)
    half = HEAD_DIM // 2
    return jnp.where(lane % HEAD_DIM < half, pltpu.roll(t, PAIR - half, 1), pltpu.roll(t, half, 1))


def rms(m):
    return lax.rsqrt(jnp.mean(m * m, -1, keepdims=True) + epsilon)


def rms_back(u, m, g):
    r = rms(m)
    t = u * g
    dot = jnp.mean(t * m, -1, keepdims=True)
    return r * t - m * (r * r * r * dot), jnp.sum(u * m * r, 0, keepdims=True)


def copies(pairs, sem):
    return [pltpu.make_async_copy(src, dst, sem.at[i]) for i, (src, dst) in enumerate(pairs)]


def forward_kernel(
    slots, length, x_ref, g_ref, cos_ref, sin_ref, w_hbm,
    xn_ref, normed_o, q_o, k_o, v_o, st_o, mixed_o, mid_o, n2_o, gu_o, wqkv_o, wout_o, wgu_o, wd_o,
    normed_ref, q_ref, k_ref, v_ref, st_ref, mixed_ref, mid_ref, n2_ref, gu_ref,
    wqkv, wout, wgu, wd, bias, sem_in, sem_out,
):
    rows = x_ref.shape[0]
    key_rows = q_ref.shape[0]
    held = (wqkv, wout, wgu, wd)
    for m in range(4):
        tile_rows, tile_cols = GRIDS[m]

        @pl.loop(0, tile_rows)
        def _(i, m=m, tile_cols=tile_cols):
            for j in range(tile_cols):
                slot = slots[OFFSETS[m] + i * tile_cols + j]
                pltpu.make_async_copy(
                    w_hbm.at[slot],
                    held[m].at[pl.ds(pl.multiple_of(i * BLOCK, BLOCK), BLOCK), pl.ds(j * BLOCK, BLOCK)],
                    sem_in.at[m],
                ).start()

    def arrive(m):
        pltpu.make_async_copy(held[m], held[m], sem_in.at[m]).wait()

    saves = copies(
        [
            (normed_ref, normed_o), (q_ref, q_o), (k_ref, k_o), (v_ref, v_o), (st_ref, st_o),
            (mixed_ref, mixed_o), (mid_ref, mid_o), (n2_ref, n2_o), (gu_ref, gu_o),
            (wqkv, wqkv_o), (wout, wout_o), (wgu, wgu_o), (wd, wd_o),
        ],
        sem_out,
    )
    query = lax.broadcasted_iota(jnp.int32, bias.shape, 0)
    key = lax.broadcasted_iota(jnp.int32, bias.shape, 1)
    bias[...] = jnp.where((key <= query) & (key < length[0]), 0.0, masked_score)
    x = x_ref[...]
    normed_ref[...] = (x * rms(x) * g_ref[0:1, :]).astype(bf16)
    saves[0].start()
    tail = key_rows - rows
    for ref in (q_ref, k_ref, v_ref):
        ref[rows:, :] = jnp.zeros((tail, D), bf16)
    arrive(0)
    saves[9].start()

    @pl.loop(0, 2)
    def _(part):
        acc = nn(normed_ref[...], wqkv[:, pl.ds(pl.multiple_of(part * D, D), D)])
        scale = jnp.where(part == 0, HEAD_DIM ** (-0.5), 1.0)
        for p in range(HEADS // 2):
            t = acc[:, p * PAIR : (p + 1) * PAIR]
            rot = ((t * cos_ref[...] + swap_halves(t) * sin_ref[...]) * scale).astype(bf16)

            @pl.when(part == 0)
            def _(p=p, rot=rot):
                q_ref[0:rows, p * PAIR : (p + 1) * PAIR] = rot

            @pl.when(part == 1)
            def _(p=p, rot=rot):
                k_ref[0:rows, p * PAIR : (p + 1) * PAIR] = rot

    v_ref[0:rows, :] = nn(normed_ref[...], wqkv[:, 2 * D :]).astype(bf16)
    for i in (1, 2, 3):
        saves[i].start()
    st_ref[...] = jnp.zeros(st_ref.shape, f32)

    @pl.loop(0, HEADS // TOGETHER)
    def _(g):
        width = TOGETHER * HEAD_DIM
        cols = pl.ds(pl.multiple_of(g * width, width), width)
        for q0, q1 in query_blocks(rows):
            count = q1 - q0
            kend = min(round_up(q1, BLOCK), key_rows)
            qp = q_ref[q0:q1, cols]
            head = lax.broadcasted_iota(jnp.int32, qp.shape, 1) // HEAD_DIM
            stacked = jnp.concatenate([jnp.where(head == h, qp, 0) for h in range(TOGETHER)], 0)
            s = nt(stacked, k_ref[:kend, cols]).reshape(TOGETHER, count, kend) + bias[q0:q1, :kend][None]
            top = jnp.max(s, -1, keepdims=True)
            e = jnp.exp(s - top)
            total = jnp.sum(e, -1, keepdims=True)
            out = nn(e.astype(bf16).reshape(TOGETHER * count, kend), v_ref[:kend, cols])
            out = out.reshape(TOGETHER, count, width) / total
            level = top + jnp.log(total)
            mixed = out[0]
            lane = lax.broadcasted_iota(jnp.int32, (count, BLOCK), 1)
            levels = st_ref[q0:q1, :]
            for h in range(TOGETHER):
                mixed = jnp.where(head == h, out[h], mixed)
                levels = jnp.where(lane == g * TOGETHER + h, level[h], levels)
            mixed_ref[q0:q1, cols] = mixed.astype(bf16)
            st_ref[q0:q1, :] = levels

    saves[4].start()
    saves[5].start()
    arrive(1)
    saves[10].start()
    middle = x_ref[...] + nn(mixed_ref[...], wout[...])
    mid_ref[...] = middle
    saves[6].start()
    n2_ref[...] = (middle * rms(middle) * g_ref[1:2, :]).astype(bf16)
    saves[7].start()
    arrive(2)
    saves[11].start()
    arrive(3)
    saves[12].start()
    xn_ref[...] = mid_ref[...]

    @pl.loop(0, FF // FF_STEP)
    def _(t):
        at = pl.multiple_of(t * FF_STEP, FF_STEP)
        gate = nn(n2_ref[...], wgu[:, pl.ds(at, FF_STEP)])
        up = nn(n2_ref[...], wgu[:, pl.ds(FF + at, FF_STEP)])
        act = (gate / (1.0 + jnp.exp(-gate)) * up).astype(bf16)
        gu_ref[:, pl.ds(at, FF_STEP)] = gate.astype(bf16)
        gu_ref[:, pl.ds(FF + at, FF_STEP)] = up.astype(bf16)
        xn_ref[...] += nn(act, wd[pl.ds(at, FF_STEP), :])

    saves[8].start()
    for save in saves:
        save.wait()


def put_tiles(places, zones, m, grad, outs, sem, i0, i1, j0, count_j):
    @pl.loop(i0, i1)
    def _(i):
        for jj in range(count_j):
            j = j0 + jj
            place = places[OFFSETS[m] + i * GRIDS[m][1] + j]
            tile = grad.at[
                pl.ds(pl.multiple_of(i * BLOCK, BLOCK), BLOCK),
                pl.ds(pl.multiple_of(j * BLOCK, BLOCK), BLOCK),
            ]
            if len(outs) == 1:
                pltpu.make_async_copy(tile, outs[0].at[place], sem).start()
                continue
            for out, (low, high, _) in zip(outs, zones):

                @pl.when((place >= low) & (place < high))
                def _(tile=tile, out=out, place=place, low=low):
                    pltpu.make_async_copy(tile, out.at[place - low], sem).start()


def backward_kernel(
    begun, zones, places, spare, length, back_ref, g_ref, cos_ref, sin_ref,
    x_i, normed_i, q_i, k_i, v_i, st_i, mixed_i, mid_i, n2_i, gu_i, wqkv_i, wout_i, wgu_i, wd_i, *rest
):
    dx_ref, gain_ref, *rest = rest[begun:]
    tiles_out, rest = rest[: len(zones)], rest[len(zones) :]
    (
        x_ref, normed_ref, q_ref, k_ref, v_ref, st_ref, mixed_ref, mid_ref, n2_ref, gu_ref,
        wqkv, wout, wgu, wd, gqkv, gout, ggu, gd,
        turned, bias, levels, sums, big, mixed_back, dproj, zero, sem_in, sem_ffn, sem_out, sem_zero,
    ) = rest
    rows = back_ref.shape[0]
    key_rows = q_ref.shape[0]
    loads = dict(
        zip(
            ("n2", "mid", "wout", "mixed", "q", "k", "v", "st", "normed", "wqkv", "x"),
            copies(
                [
                    (n2_i, n2_ref), (mid_i, mid_ref), (wout_i, wout), (mixed_i, mixed_ref), (q_i, q_ref), (k_i, k_ref), (v_i, v_ref),
                    (st_i, st_ref), (normed_i, normed_ref), (wqkv_i, wqkv), (x_i, x_ref),
                ],
                sem_in,
            ),
        )
    )

    def ffn_loads(t):
        here = pl.ds(pl.multiple_of(t * FF_STEP, FF_STEP), FF_STEP)
        there = pl.ds(pl.multiple_of(FF + t * FF_STEP, FF_STEP), FF_STEP)
        parts = [(wd_i.at[here, :], wd.at[here, :])]
        for cols in (here, there):
            parts += [(gu_i.at[:, cols], gu_ref.at[:, cols]), (wgu_i.at[:, cols], wgu.at[:, cols])]
        return [pltpu.make_async_copy(src, dst, sem_ffn.at[t, i]) for i, (src, dst) in enumerate(parts)]

    loads["n2"].start()
    for t in range(FF // FF_STEP):
        for load in ffn_loads(t):
            load.start()
    for name, load in loads.items():
        if name != "n2":
            load.start()
    put = functools.partial(put_tiles, places, zones)
    spares = spare.shape[0] - 1
    if spares > 0:
        zero[...] = jnp.zeros(zero.shape, bf16)

        @pl.loop(0, spares)
        def _(i):
            pltpu.make_async_copy(zero, tiles_out[0].at[spare[i]], sem_zero).start()

    key = lax.broadcasted_iota(jnp.int32, bias.shape, 0)
    query = lax.broadcasted_iota(jnp.int32, bias.shape, 1)
    bias[...] = jnp.where((key <= query) & (key < length[0]), 0.0, masked_score)
    big[...] = jnp.zeros(big.shape, f32)
    loads["n2"].wait()
    turned[...] = n2_ref[...].T

    @pl.loop(0, FF // FF_STEP)
    def _(t):
        for load in ffn_loads(t):
            load.wait()
        at = pl.multiple_of(t * FF_STEP, FF_STEP)
        here = pl.ds(at, FF_STEP)
        there = pl.ds(FF + at, FF_STEP)
        back_ffn = back_ref[...].astype(bf16)
        d_act = nt(back_ffn, wd[here, :])
        gate = gu_ref[:, here].astype(f32)
        up = gu_ref[:, there].astype(f32)
        sig = 1.0 / (1.0 + jnp.exp(-gate))
        silu = gate * sig
        act = (silu * up).astype(bf16)
        d_gate = (d_act * up * (sig * (1.0 + gate * (1.0 - sig)))).astype(bf16)
        d_up = (d_act * silu).astype(bf16)
        gd[here, :] = tn(act, back_ffn).astype(bf16)
        ggu[:, here] = nn(turned[...], d_gate).astype(bf16)
        ggu[:, there] = nn(turned[...], d_up).astype(bf16)
        per = FF_STEP // BLOCK
        put(3, gd, tiles_out, sem_out.at[3], t * per, (t + 1) * per, 0, D // BLOCK)
        put(2, ggu, tiles_out, sem_out.at[2], 0, D // BLOCK, t * per, per)
        put(2, ggu, tiles_out, sem_out.at[2], 0, D // BLOCK, FF // BLOCK + t * per, per)
        big[...] += nt(d_gate, wgu[:, here]) + nt(d_up, wgu[:, there])

    loads["mid"].wait()
    step, gain = rms_back(big[...], mid_ref[...], g_ref[1:2, :])
    gain_ref[1:2, :] = gain
    dx_ref[...] = back_ref[...] + step
    back_attn = dx_ref[...].astype(bf16)
    loads["wout"].wait()
    mixed_back[0:rows, :] = nt(back_attn, wout[...]).astype(bf16)
    mixed_back[rows:, :] = jnp.zeros((key_rows - rows, D), bf16)
    loads["mixed"].wait()
    gout[...] = tn(mixed_ref[...], back_attn).astype(bf16)
    put(1, gout, tiles_out, sem_out.at[1], 0, D // BLOCK, 0, D // BLOCK)
    for name in ("q", "k", "v", "st"):
        loads[name].wait()
    by_head = st_ref[...].T
    for h in range(HEADS):
        levels[h] = by_head[h : h + 1, :]

    @pl.loop(0, HEADS // 2)
    def _(p):
        cols = pl.ds(pl.multiple_of(p * PAIR, PAIR), PAIR)
        low = lax.broadcasted_iota(jnp.int32, (key_rows, PAIR), 1) < HEAD_DIM

        def stacked(t, n):
            return jnp.concatenate([jnp.where(low[:n], t[:n], 0), jnp.where(low[:n], 0, t[:n])], 0)

        def chosen(t, n):
            return jnp.where(low[:n], t[:n], t[n:])

        for q0, q1 in query_blocks(key_rows):
            kend, count = q1, q1 - q0
            keys, values = k_ref[:kend, cols], v_ref[:kend, cols]
            queries, backs = q_ref[q0:q1, cols], mixed_back[q0:q1, cols]
            level = jnp.stack([levels[2 * p + h, :, q0:q1] for h in range(2)], 0)
            scores = nt(stacked(keys, kend), queries).reshape(2, kend, count)
            soft = jnp.exp(scores + bias[:kend, q0:q1][None] - level)
            d_prob = nt(stacked(values, kend), backs).reshape(2, kend, count)
            row_dot = jnp.sum(soft * d_prob, 1, keepdims=True)
            d_score = (soft * (d_prob - row_dot)).astype(bf16)
            d_value = chosen(nn(soft.astype(bf16).reshape(2 * kend, count), backs), kend)
            d_key = chosen(nn(d_score.reshape(2 * kend, count), queries), kend)
            d_query = jnp.where(low[:count], tn(d_score[0], keys), tn(d_score[1], keys))
            sums[0, q0:q1, :] = d_query * HEAD_DIM ** (-0.5)
            if q0 > 0:
                sums[1, :q0, :] += d_key[:q0]
                sums[2, :q0, :] += d_value[:q0]
            sums[1, q0:kend, :] = d_key[q0:]
            sums[2, q0:kend, :] = d_value[q0:]
        for part in range(2):
            t = sums[part, 0:rows, :]
            dproj[:, pl.ds(pl.multiple_of(part * D + p * PAIR, PAIR), PAIR)] = (
                t * cos_ref[...] - swap_halves(t) * sin_ref[...]
            ).astype(bf16)
        dproj[:, pl.ds(pl.multiple_of(2 * D + p * PAIR, PAIR), PAIR)] = sums[2, 0:rows, :].astype(bf16)

    loads["normed"].wait()
    turned[...] = normed_ref[...].T
    loads["wqkv"].wait()
    for part in range(3):
        cols = slice(part * D, (part + 1) * D)
        gqkv[:, cols] = nn(turned[...], dproj[:, cols]).astype(bf16)
        put(0, gqkv, tiles_out, sem_out.at[0], 0, D // BLOCK, part * (D // BLOCK), D // BLOCK)
        if part == 0:
            big[...] = nt(dproj[:, cols], wqkv[:, cols])
        else:
            big[...] += nt(dproj[:, cols], wqkv[:, cols])

    loads["x"].wait()
    step, gain = rms_back(big[...], x_ref[...], g_ref[0:1, :])
    gain_ref[0:1, :] = gain
    dx_ref[...] += step
    for m, grad in enumerate((gqkv, gout, ggu, gd)):
        pltpu.make_async_copy(grad, grad, sem_out.at[m]).wait()
    if spares > 0:

        @pl.loop(0, spares)
        def _(i):
            pltpu.make_async_copy(zero, tiles_out[0].at[spare[i]], sem_zero).wait()


def weight_shapes():
    return [(r * BLOCK, c * BLOCK) for r, c in GRIDS]


VMEM = pl.BlockSpec(memory_space=pltpu.VMEM)
SMEM = pl.BlockSpec(memory_space=pltpu.SMEM)
HBM = pl.BlockSpec(memory_space=pl.ANY)


def like(struct):
    return pltpu.VMEM(struct.shape, struct.dtype)


def cost(flops, bytes_accessed):
    return pl.CostEstimate(flops=flops, bytes_accessed=bytes_accessed, transcendentals=0)


def forward_layer(slots, length, x, gains, cos, sin, gathered):
    rows = x.shape[0]
    key_rows = round_up(rows, BLOCK)
    S = jax.ShapeDtypeStruct
    saved = [
        S((rows, D), bf16),
        S((key_rows, D), bf16),
        S((key_rows, D), bf16),
        S((key_rows, D), bf16),
        S((key_rows, BLOCK), f32),
        S((rows, D), bf16),
        S((rows, D), f32),
        S((rows, D), bf16),
        S((rows, 2 * FF), bf16),
    ] + [S(s, bf16) for s in weight_shapes()]
    return pl.pallas_call(
        forward_kernel,
        out_shape=[S((rows, D), f32)] + saved,
        in_specs=[SMEM, SMEM, VMEM, VMEM, VMEM, VMEM, HBM],
        out_specs=[VMEM] + [HBM] * 13,
        scratch_shapes=[like(s) for s in saved]
        + [
            pltpu.VMEM((rows, key_rows), f32),
            pltpu.SemaphoreType.DMA((4,)),
            pltpu.SemaphoreType.DMA((13,)),
        ],
        compiler_params=pltpu.CompilerParams(vmem_limit_bytes=VMEM_BYTES),
        cost_estimate=cost(2 * rows * PER_LAYER * BLOCK * BLOCK, 40 * 2**20),
        name="forward_block",
    )(slots, length, x, gains, cos, sin, gathered)


def tile_arrays(zones):
    return [jax.ShapeDtypeStruct((size, BLOCK, BLOCK), bf16) for _, _, size in zones]


def backward_layer(places, spare, length, back, gains, cos, sin, saved, zones, begun):
    rows = back.shape[0]
    key_rows = round_up(rows, BLOCK)
    S = jax.ShapeDtypeStruct
    args = (places, spare, length, back, gains, cos, sin) + tuple(saved)
    late = 2 + len(zones) - len(begun)
    return pl.pallas_call(
        functools.partial(backward_kernel, len(begun), zones),
        out_shape=[S((rows, D), f32), S((2, D), f32)] + tile_arrays(zones),
        in_specs=[SMEM] * 3 + [VMEM] * 4 + [HBM] * (14 + len(begun)),
        out_specs=[VMEM, VMEM] + [HBM] * len(zones),
        input_output_aliases={len(args) + i: late + i for i in range(len(begun))},
        scratch_shapes=[like(s) for s in saved]
        + [pltpu.VMEM(s, bf16) for s in weight_shapes()]
        + [
            pltpu.VMEM((D, rows), bf16),
            pltpu.VMEM((key_rows, key_rows), f32),
            pltpu.VMEM((HEADS, 1, key_rows), f32),
            pltpu.VMEM((3, key_rows, PAIR), f32),
            pltpu.VMEM((rows, D), f32),
            pltpu.VMEM((key_rows, D), bf16),
            pltpu.VMEM((rows, 3 * D), bf16),
            pltpu.VMEM((BLOCK, BLOCK), bf16),
            pltpu.SemaphoreType.DMA((11,)),
            pltpu.SemaphoreType.DMA((FF // FF_STEP, 5)),
            pltpu.SemaphoreType.DMA((4,)),
            pltpu.SemaphoreType.DMA,
        ],
        compiler_params=pltpu.CompilerParams(vmem_limit_bytes=VMEM_BYTES),
        cost_estimate=cost(4 * rows * PER_LAYER * BLOCK * BLOCK + 20 * rows * rows * D, 60 * 2**20),
        name="backward_block",
    )(*args, *begun)


def optimizer_kernel(factor, rank, g_ref, m_ref, s_ref, r_ref, wg_ref, ns_ref, nm_ref, nc_ref):
    f = factor[0]
    count = m_ref.shape[0]
    for i in range(count):
        gb = g_ref[rank[pl.program_id(0) * count + i]]
        wg_ref[i] = gb.astype(f32) * f
        half = (1.0 - decay_rate) * f * f
        ns_ref[i, 0] = decay_rate * s_ref[i, 0] + half * nt(gb, gb)
        ns_ref[i, 1] = decay_rate * s_ref[i, 1] + half * tn(gb, gb)
        left = nn(r_ref[i, 0].astype(bf16), (gb.astype(f32) * f).astype(bf16)).astype(bf16)
        new = m_ref[i] - step_rate * nn(left, r_ref[i, 1].astype(bf16))
        nm_ref[i] = new
        nc_ref[i] = new.astype(bf16)


def optimizer(factor, rank, owned, master, statistics, inverse_roots):
    count = owned.shape[0]
    per = max(n for n in range(1, 13) if count % n == 0)
    S = jax.ShapeDtypeStruct
    one = pl.BlockSpec((per, BLOCK, BLOCK), lambda i: (i, 0, 0))
    two = pl.BlockSpec((per, 2, BLOCK, BLOCK), lambda i: (i, 0, 0, 0))
    return pl.pallas_call(
        optimizer_kernel,
        grid=(count // per,),
        out_shape=[
            S(master.shape, f32),
            S(statistics.shape, f32),
            S(master.shape, f32),
            S(master.shape, bf16),
        ],
        in_specs=[SMEM, SMEM, VMEM, one, two, two],
        out_specs=[one, two, one, one],
        compiler_params=pltpu.CompilerParams(vmem_limit_bytes=VMEM_BYTES),
        name="optimizer",
    )(factor, rank, owned, master, statistics, inverse_roots)


def to_images(local, bands, band):
    images, band_rows = local.shape[0], local.shape[-2]
    padded = jnp.concatenate([local, jnp.zeros((bands - images,) + local.shape[1:], local.dtype)], 0)
    whole = jnp.zeros((bands,) + local.shape[1:], local.dtype)
    for shift in range(bands):
        block = lax.dynamic_index_in_dim(padded, (band + shift) % bands, 0, keepdims=False)
        if shift > 0:
            pairs = [(b, (b + shift) % bands) for b in range(bands) if (b + shift) % bands < images]
            block = lax.ppermute(block, "band", pairs)
        whole = lax.dynamic_update_index_in_dim(whole, block, (band - shift) % bands, 0)
    return whole


def send_to_bands(whole, images, bands, band):
    blocks = []
    for shift in range(bands):
        block = lax.dynamic_index_in_dim(whole, (band + shift) % bands, 0, keepdims=False)
        if shift > 0:
            pairs = [(b, (b + shift) % bands) for b in range(images)]
            block = lax.ppermute(block, "band", pairs)
        blocks.append(block)
    return tuple(blocks)


def at_bands(blocks, images, bands, band):
    local = jnp.zeros((bands,) + blocks[0].shape, blocks[0].dtype)
    for shift, block in enumerate(blocks):
        local = lax.dynamic_update_index_in_dim(local, block, (band - shift) % bands, 0)
    return local[:images]


EARLY = (36,)
LATE = (30, 26, 16)
LEAST = (PER_LAYER,)


def chunk_places(slot_of_block, per_owner, me):
    blocks = slot_of_block.shape[0]
    block_of_slot = jnp.zeros((blocks,), jnp.int32).at[slot_of_block].set(
        jnp.arange(blocks, dtype=jnp.int32)
    )
    by_owner = block_of_slot.reshape(-1, per_owner)
    rank = jnp.sum(by_owner[:, None, :] > by_owner[:, :, None], -1, dtype=jnp.int32)
    owner = jnp.arange(by_owner.shape[0], dtype=jnp.int32)
    relative = (owner ^ me)[:, None]
    owner = owner[:, None]
    core, x, y = relative % 2, relative // 2 % 2, relative // 4
    place = jnp.zeros_like(rank)
    clean = jnp.bool_(True)
    start = 0
    for size, least in zip(EARLY, LEAST):
        at = rank - start
        here = (at >= 0) & (at < size)
        place = jnp.where(here, 8 * start + owner * size + at, place)
        clean = clean & jnp.all(jnp.where(here, by_owner >= least, True))
        start += size
    for size in LATE:
        half = size // 2
        at = rank - start
        here = (at >= 0) & (at < size)
        spot = jnp.where(at < half, (x * 2 + y) * half + at, 4 * half + (y * 2 + x) * half + at - half)
        place = jnp.where(here, 8 * start + core * 4 * size + spot, place)
        start += size
    return place.reshape(-1)[slot_of_block], rank, clean


CORE = [(i, i ^ 1) for i in range(8)]
ALONG_X = [(i, i ^ 2) for i in range(8)]
ALONG_Y = [(i, i ^ 4) for i in range(8)]


def wide(t, lo, hi):
    return t[lo:hi].astype(f32)


class Bands:
    def to_meet(self, plane):
        self.plane = plane
        return (plane,)

    def go_meet(self, plane):
        return lax.ppermute(plane, "band", [(0, 1)]), lax.ppermute(plane, "band", [(2, 1)])

    def to_part(self, up, down):
        self.total = (self.plane.astype(f32) + up.astype(f32) + down.astype(f32)).astype(bf16)
        return (self.total,)

    def go_part(self, total):
        return lax.ppermute(total, "band", [(1, 0)]), lax.ppermute(total, "band", [(1, 2)])

    def to_last(self, to_first, to_third):
        self.to_first, self.to_third = to_first, to_third
        return (to_third,)

    def go_last(self, to_third):
        return (lax.ppermute(to_third, "band", [(2, 3)]),)

    def to_end(self, to_last):
        band = lax.axis_index("band")
        total = jnp.where(band == 0, self.to_first, self.total)
        total = jnp.where(band == 2, self.to_third, total)
        self.total = jnp.where(band == 3, to_last, total)
        return ()

    def go_end(self):
        return ()


class Chunk(Bands):
    def __init__(self, kept, sent):
        self.half = kept.shape[0] // 8
        self.kept, self.sent = kept, sent

    def chip(self, lo, hi):
        lo, hi = lo * self.half, hi * self.half
        return wide(self.kept, lo, hi) + wide(self.received, lo, hi)

    def to_core(self):
        return (self.sent,)

    def go_core(self, send):
        return (lax.ppermute(send, "dp", CORE),)

    def to_plane(self, received):
        self.received = received
        return self.chip(2, 4).astype(bf16), self.chip(6, 8).astype(bf16)

    def go_plane(self, send_x, send_y):
        return lax.ppermute(send_x, "dp", ALONG_X), lax.ppermute(send_y, "dp", ALONG_Y)

    go_turn = go_plane

    def to_turn(self, from_x, from_y):
        self.from_x, self.from_y = from_x, from_y
        half = self.half
        send_y = (self.chip(1, 2) + wide(from_x, half, 2 * half)).astype(bf16)
        send_x = (self.chip(5, 6) + wide(from_y, half, 2 * half)).astype(bf16)
        return send_x, send_y

    def to_meet(self, from_x, from_y):
        half = self.half
        one = self.chip(0, 1) + wide(self.from_x, 0, half) + wide(from_y, 0, half)
        two = self.chip(4, 5) + wide(self.from_y, 0, half) + wide(from_x, 0, half)
        self.plane = jnp.concatenate([one, two], 0).astype(bf16)
        return (self.plane,)


class Sequence:
    def __init__(self):
        self.before = ()
        self.arrived = {}

    def round(self, *steps):
        arrived = [tuple(self.arrived.get(chunk, ())) for chunk, _ in steps]
        flat = sum(arrived, ())
        flat = lax.optimization_barrier(flat + self.before)
        at, self.before = 0, ()
        for (chunk, name), had in zip(steps, arrived):
            sends = getattr(chunk, "to_" + name)(*flat[at : at + len(had)])
            at += len(had)
            self.arrived[chunk] = getattr(chunk, "go_" + name)(*sends)
            self.before = self.before + tuple(sends)

    def wait_for(self, *arrays):
        arrays = lax.optimization_barrier(arrays + self.before)[: len(arrays)]
        self.before = self.before + arrays
        return arrays


def rope_tables(rows):
    half = HEAD_DIM // 2
    frequency = rope_base ** (-(jnp.arange(half, dtype=f32) * 2.0 / HEAD_DIM))
    angles = jnp.arange(rows, dtype=jnp.int32).astype(f32)[:, None] * frequency[None, :]
    cosine, sine = jnp.cos(angles), jnp.sin(angles)
    return jnp.tile(cosine, (1, 4)), jnp.tile(jnp.concatenate([-sine, sine], 1), (1, 2))


def shards(
    tokens,
    cotangent,
    lengths,
    slot_of_block,
    master,
    statistics,
    inverse_roots,
    gain_values,
    gain_moments,
):
    images, band_rows, _ = tokens.shape
    band = lax.axis_index("band")
    bands = lax.axis_size("band")
    seq = band_rows * bands
    rows = round_up(seq, 16)
    gathered = lax.all_gather(master.astype(bf16), "dp", axis=0, tiled=True)
    slot_count = gathered.shape[0]

    arrived = to_images(jnp.stack([tokens, cotangent], 1), bands, band)
    token_rows = jnp.pad(arrived[:, 0].reshape(seq, D), ((0, rows - seq), (0, 0)))
    back_rows = jnp.pad(arrived[:, 1].reshape(seq, D), ((0, rows - seq), (0, 0)))
    length = lengths[jnp.minimum(band, images - 1)]
    valid = (jnp.arange(rows, dtype=jnp.int32) < length).astype(f32)
    length = length.reshape(1)
    cos, sin = rope_tables(rows)

    spare_count = slot_count - slot_of_block.shape[0]
    spare = jnp.zeros((1,), jnp.int32)
    if spare_count > 0:
        used = jnp.zeros((slot_count,), jnp.int32).at[slot_of_block].set(1)
        spare = jnp.concatenate([jnp.argsort(used)[:spare_count].astype(jnp.int32), spare])

    hidden = token_rows.astype(f32)
    inputs, saves = [], []
    for layer in range(LAYERS):
        slots = slot_of_block[layer * PER_LAYER : (layer + 1) * PER_LAYER]
        gains = gain_values[2 * layer : 2 * layer + 2]
        inputs.append(hidden)
        hidden, *saved = forward_layer(slots, length, hidden, gains, cos, sin, gathered)
        saves.append(saved)

    def send_rows(t):
        return send_to_bands(t[:seq].astype(bf16).reshape(bands, band_rows, D), images, bands, band)

    output_blocks = send_rows(hidden)

    back = back_rows.astype(f32) * valid[:, None]
    per_owner = master.shape[0]
    me = lax.axis_index("dp")
    by_permutes = (
        lax.axis_size("dp") == 8
        and bands == 4
        and images == 3
        and slot_count == slot_of_block.shape[0]
        and per_owner == sum(EARLY) + sum(LATE)
    )
    if by_permutes:
        places, ranks, clean = chunk_places(slot_of_block, per_owner, me)
        rank = lax.dynamic_index_in_dim(ranks, me, 0, keepdims=False)
        ends = [8 * sum(EARLY[: i + 1]) for i in range(len(EARLY))]
        bounds = [0] + ends
        for size in LATE:
            bounds += [bounds[-1] + 4 * size, bounds[-1] + 8 * size]
        zones = tuple((low, high, high - low) for low, high in zip(bounds, bounds[1:]))
    else:
        places, rank = slot_of_block, jnp.arange(per_owner, dtype=jnp.int32)
        zones = ((0, slot_count, slot_count),)

    def backward(layer, back, tiles, zones):
        fill = spare if layer == LAYERS - 1 else spare[-1:]
        back, gains, *tiles = backward_layer(
            places[layer * PER_LAYER : (layer + 1) * PER_LAYER], fill, length, back,
            gain_values[2 * layer : 2 * layer + 2], cos, sin, (inputs[layer], *saves[layer]), zones, tiles,
        )
        return back, gains, tiles

    if by_permutes:
        back, gains_top, tiles = backward(1, back, [], zones)
        early = tiles[:1]
        ready, *output_blocks = lax.optimization_barrier((tiles[0], *output_blocks))
        early_sums = [lax.psum_scatter(ready, "dp", scatter_dimension=0, tiled=True)]
        back, gains_bottom, tiles = backward(0, back, tiles[1:], zones)
        missed, *late = tiles
        gains = jnp.concatenate([gains_bottom, gains_top], 0).astype(bf16).reshape(-1, BLOCK)
        gains = jnp.pad(gains, ((0, BLOCK - gains.shape[0]), (0, 0)))[None]
        sequence = Sequence()
        chunks = [Chunk(*late[2 * i : 2 * i + 2]) for i in range(len(LATE))]
        one, two, three = chunks
        top = Bands()
        sequence.arrived[top] = (jnp.concatenate([early_sums[0], gains], 0),)
        sequence.round((one, "core"), (two, "core"), (three, "core"))
        sequence.round((one, "plane"))
        sequence.round((top, "meet"))
        sequence.round((one, "turn"))
        sequence.round((top, "part"))
        sequence.round((one, "meet"), (two, "plane"))
        sequence.round((two, "turn"))
        sequence.round((one, "part"), (top, "last"))
        sequence.round((two, "meet"), (three, "plane"))
        sequence.round((three, "turn"))
        sequence.round((two, "part"), (one, "last"))
        sequence.round((three, "meet"), (top, "end"))
        sequence.round((two, "last"), (three, "part"))
        (back,) = sequence.wait_for(back)
        input_blocks = send_rows(back)
        sequence.round((three, "last"), (one, "end"))
        sequence.round((two, "end"))
        sequence.round((three, "end"))
        early_total = top.total[:-1]

        def again(trip, total):
            _, spare_tiles, *parts = lax.optimization_barrier((trip, missed, *early))
            block_at = jnp.argsort(places)
            sums, start = [], 0
            for part, end, least in zip(parts, ends, LEAST):
                late_here = (block_at[start:end] < least)[:, None, None]
                whole = jnp.where(late_here, spare_tiles[start:end], part)
                sums.append(lax.psum_scatter(whole, "dp", scatter_dimension=0, tiled=True))
                start = end
            return lax.psum(jnp.concatenate(sums, 0), "band")

        early_total = lax.fori_loop(0, jnp.where(clean, 0, 1), again, early_total)
        owned = jnp.concatenate([early_total] + [chunk.total for chunk in chunks], 0)
        gain_total = top.total[-1].astype(f32)[: gain_values.size // BLOCK].reshape(-1, D)
    else:
        back, gains_top, tiles = backward(1, back, [], zones)
        back, gains_bottom, tiles = backward(0, back, tiles, zones)
        owned = lax.psum_scatter(tiles[0], "dp", scatter_dimension=0, tiled=True)
        owned = lax.psum(owned, "band")
        gain_total = lax.psum(jnp.concatenate([gains_bottom, gains_top], 0), ("dp", "band"))
        input_blocks = send_rows(back)

    layer_output = at_bands(output_blocks, images, bands, band)
    input_grad = at_bands(input_blocks[:bands], images, bands, band)
    owned_f = owned.astype(f32)
    owned_squares = jnp.sum(owned_f * owned_f)
    if by_permutes:
        last = jnp.concatenate([gain_total.reshape(-1, BLOCK), jnp.broadcast_to(owned_squares, (1, BLOCK))], 0)
        for pairs in (CORE, ALONG_X, ALONG_Y):
            last = last + lax.ppermute(last, "dp", pairs)
        gain_total, owned_squares = last[:-1].reshape(gain_values.shape), last[-1, 0]
    else:
        owned_squares = lax.psum(owned_squares, "dp")
    grad_norm = jnp.sqrt(owned_squares + jnp.sum(gain_total * gain_total))
    factor = jnp.minimum(1.0, clip_limit / grad_norm)
    weight_grads, new_statistics, new_master, master_copy = optimizer(
        factor.reshape(1), rank, owned, master, statistics, inverse_roots
    )
    gain_grads = gain_total * factor
    new_moments = decay_rate * gain_moments + (1.0 - decay_rate) * gain_grads * gain_grads
    new_gains = gain_values - gain_rate * gain_grads / (jnp.sqrt(new_moments) + epsilon)
    return (
        layer_output,
        input_grad,
        weight_grads,
        grad_norm,
        new_statistics,
        new_master,
        master_copy,
        gain_grads,
        new_moments,
        new_gains,
    )


def solution(mesh):
    return jax.shard_map(
        shards,
        mesh=mesh,
        in_specs=(
            P("dp", "band", None),
            P("dp", "band", None),
            P("dp"),
            P(),
            P("dp", None, None),
            P("dp", None, None, None),
            P("dp", None, None, None),
            P(),
            P(),
        ),
        out_specs=(
            P("dp", "band", None),
            P("dp", "band", None),
            P("dp", None, None),
            P(),
            P("dp", None, None, None),
            P("dp", None, None),
            P("dp", None, None),
            P(),
            P(),
            P(),
        ),
        check_vma=False,
    )
```

```python
import functools

import jax
import jax.numpy as jnp
from jax import lax
from jax.experimental import pallas as pl
from jax.experimental.pallas import tpu as pltpu
from jax.sharding import PartitionSpec as P

D = 768
HEADS = 12
HEAD_DIM = 64
FF = 2048
LAYERS = 2
BLOCK = 128
PAIR = 2 * HEAD_DIM

epsilon = 1e-05
rope_base = 10000.0
decay_rate = 0.5
step_rate = 0.4
gain_rate = 0.2
clip_limit = 1.0
masked_score = -1e30
VMEM_BYTES = 62 * 2**20

f32 = jnp.float32
bf16 = jnp.bfloat16

GRIDS = [
    (D // BLOCK, 3 * D // BLOCK),
    (D // BLOCK, D // BLOCK),
    (D // BLOCK, 2 * FF // BLOCK),
    (FF // BLOCK, D // BLOCK),
]
COUNTS = [r * c for r, c in GRIDS]
OFFSETS = [sum(COUNTS[:i]) for i in range(4)]
PER_LAYER = sum(COUNTS)
FF_STEP = 512
TOGETHER = 4


def round_up(n, m):
    return -(-n // m) * m


def nn(a, b):
    return lax.dot_general(a, b, (((1,), (0,)), ((), ())), preferred_element_type=f32)


def nt(a, b):
    return lax.dot_general(a, b, (((1,), (1,)), ((), ())), preferred_element_type=f32)


def tn(a, b):
    return lax.dot_general(a, b, (((0,), (0,)), ((), ())), preferred_element_type=f32)


def query_blocks(rows, step=256):
    return [(s, min(s + step, rows)) for s in range(0, rows, step)]


def swap_halves(t):
    lane = lax.broadcasted_iota(jnp.int32, t.shape, 1)
    half = HEAD_DIM // 2
    return jnp.where(lane % HEAD_DIM < half, pltpu.roll(t, PAIR - half, 1), pltpu.roll(t, half, 1))


def rms(m):
    return lax.rsqrt(jnp.mean(m * m, -1, keepdims=True) + epsilon)


def rms_back(u, m, g):
    r = rms(m)
    t = u * g
    dot = jnp.mean(t * m, -1, keepdims=True)
    return r * t - m * (r * r * r * dot), jnp.sum(u * m * r, 0, keepdims=True)


def copies(pairs, sem):
    return [pltpu.make_async_copy(src, dst, sem.at[i]) for i, (src, dst) in enumerate(pairs)]


def forward_kernel(
    slots, length, x_ref, g_ref, cos_ref, sin_ref, w_hbm,
    xn_ref, normed_o, q_o, k_o, v_o, st_o, mixed_o, mid_o, n2_o, gu_o, wqkv_o, wout_o, wgu_o, wd_o,
    normed_ref, q_ref, k_ref, v_ref, st_ref, mixed_ref, mid_ref, n2_ref, gu_ref,
    wqkv, wout, wgu, wd, bias, sem_in, sem_out,
):
    rows = x_ref.shape[0]
    key_rows = q_ref.shape[0]
    held = (wqkv, wout, wgu, wd)
    for m in range(4):
        tile_rows, tile_cols = GRIDS[m]

        @pl.loop(0, tile_rows)
        def _(i, m=m, tile_cols=tile_cols):
            for j in range(tile_cols):
                slot = slots[OFFSETS[m] + i * tile_cols + j]
                pltpu.make_async_copy(
                    w_hbm.at[slot],
                    held[m].at[pl.ds(pl.multiple_of(i * BLOCK, BLOCK), BLOCK), pl.ds(j * BLOCK, BLOCK)],
                    sem_in.at[m],
                ).start()

    def arrive(m):
        pltpu.make_async_copy(held[m], held[m], sem_in.at[m]).wait()

    saves = copies(
        [
            (normed_ref, normed_o), (q_ref, q_o), (k_ref, k_o), (v_ref, v_o), (st_ref, st_o),
            (mixed_ref, mixed_o), (mid_ref, mid_o), (n2_ref, n2_o), (gu_ref, gu_o),
            (wqkv, wqkv_o), (wout, wout_o), (wgu, wgu_o), (wd, wd_o),
        ],
        sem_out,
    )
    query = lax.broadcasted_iota(jnp.int32, bias.shape, 0)
    key = lax.broadcasted_iota(jnp.int32, bias.shape, 1)
    bias[...] = jnp.where((key <= query) & (key < length[0]), 0.0, masked_score)
    x = x_ref[...]
    normed_ref[...] = (x * rms(x) * g_ref[0:1, :]).astype(bf16)
    saves[0].start()
    tail = key_rows - rows
    for ref in (q_ref, k_ref, v_ref):
        ref[rows:, :] = jnp.zeros((tail, D), bf16)
    arrive(0)
    saves[9].start()

    @pl.loop(0, 2)
    def _(part):
        acc = nn(normed_ref[...], wqkv[:, pl.ds(pl.multiple_of(part * D, D), D)])
        scale = jnp.where(part == 0, HEAD_DIM ** (-0.5), 1.0)
        for p in range(HEADS // 2):
            t = acc[:, p * PAIR : (p + 1) * PAIR]
            rot = ((t * cos_ref[...] + swap_halves(t) * sin_ref[...]) * scale).astype(bf16)

            @pl.when(part == 0)
            def _(p=p, rot=rot):
                q_ref[0:rows, p * PAIR : (p + 1) * PAIR] = rot

            @pl.when(part == 1)
            def _(p=p, rot=rot):
                k_ref[0:rows, p * PAIR : (p + 1) * PAIR] = rot

    v_ref[0:rows, :] = nn(normed_ref[...], wqkv[:, 2 * D :]).astype(bf16)
    for i in (1, 2, 3):
        saves[i].start()
    st_ref[...] = jnp.zeros(st_ref.shape, f32)

    @pl.loop(0, HEADS // TOGETHER)
    def _(g):
        width = TOGETHER * HEAD_DIM
        cols = pl.ds(pl.multiple_of(g * width, width), width)
        for q0, q1 in query_blocks(rows):
            count = q1 - q0
            kend = min(round_up(q1, BLOCK), key_rows)
            qp = q_ref[q0:q1, cols]
            head = lax.broadcasted_iota(jnp.int32, qp.shape, 1) // HEAD_DIM
            stacked = jnp.concatenate([jnp.where(head == h, qp, 0) for h in range(TOGETHER)], 0)
            s = nt(stacked, k_ref[:kend, cols]).reshape(TOGETHER, count, kend) + bias[q0:q1, :kend][None]
            top = jnp.max(s, -1, keepdims=True)
            e = jnp.exp(s - top)
            total = jnp.sum(e, -1, keepdims=True)
            out = nn(e.astype(bf16).reshape(TOGETHER * count, kend), v_ref[:kend, cols])
            out = out.reshape(TOGETHER, count, width) / total
            level = top + jnp.log(total)
            mixed = out[0]
            lane = lax.broadcasted_iota(jnp.int32, (count, BLOCK), 1)
            levels = st_ref[q0:q1, :]
            for h in range(TOGETHER):
                mixed = jnp.where(head == h, out[h], mixed)
                levels = jnp.where(lane == g * TOGETHER + h, level[h], levels)
            mixed_ref[q0:q1, cols] = mixed.astype(bf16)
            st_ref[q0:q1, :] = levels

    saves[4].start()
    saves[5].start()
    arrive(1)
    saves[10].start()
    middle = x_ref[...] + nn(mixed_ref[...], wout[...])
    mid_ref[...] = middle
    saves[6].start()
    n2_ref[...] = (middle * rms(middle) * g_ref[1:2, :]).astype(bf16)
    saves[7].start()
    arrive(2)
    saves[11].start()
    arrive(3)
    saves[12].start()
    xn_ref[...] = mid_ref[...]

    @pl.loop(0, FF // FF_STEP)
    def _(t):
        at = pl.multiple_of(t * FF_STEP, FF_STEP)
        gate = nn(n2_ref[...], wgu[:, pl.ds(at, FF_STEP)])
        up = nn(n2_ref[...], wgu[:, pl.ds(FF + at, FF_STEP)])
        act = (gate / (1.0 + jnp.exp(-gate)) * up).astype(bf16)
        gu_ref[:, pl.ds(at, FF_STEP)] = gate.astype(bf16)
        gu_ref[:, pl.ds(FF + at, FF_STEP)] = up.astype(bf16)
        xn_ref[...] += nn(act, wd[pl.ds(at, FF_STEP), :])

    saves[8].start()
    for save in saves:
        save.wait()


def put_tiles(places, zones, m, grad, outs, sem, i0, i1, j0, count_j):
    @pl.loop(i0, i1)
    def _(i):
        for jj in range(count_j):
            j = j0 + jj
            place = places[OFFSETS[m] + i * GRIDS[m][1] + j]
            tile = grad.at[
                pl.ds(pl.multiple_of(i * BLOCK, BLOCK), BLOCK),
                pl.ds(pl.multiple_of(j * BLOCK, BLOCK), BLOCK),
            ]
            if len(outs) == 1:
                pltpu.make_async_copy(tile, outs[0].at[place], sem).start()
                continue
            for out, (low, high, _) in zip(outs, zones):

                @pl.when((place >= low) & (place < high))
                def _(tile=tile, out=out, place=place, low=low):
                    pltpu.make_async_copy(tile, out.at[place - low], sem).start()


def backward_kernel(
    begun, zones, places, spare, length, back_ref, g_ref, cos_ref, sin_ref,
    x_i, normed_i, q_i, k_i, v_i, st_i, mixed_i, mid_i, n2_i, gu_i, wqkv_i, wout_i, wgu_i, wd_i, *rest
):
    dx_ref, gain_ref, *rest = rest[begun:]
    tiles_out, rest = rest[: len(zones)], rest[len(zones) :]
    (
        x_ref, normed_ref, q_ref, k_ref, v_ref, st_ref, mixed_ref, mid_ref, n2_ref, gu_ref,
        wqkv, wout, wgu, wd, gqkv, gout, ggu, gd,
        turned, bias, levels, sums, big, mixed_back, dproj, zero, sem_in, sem_ffn, sem_out, sem_zero,
    ) = rest
    rows = back_ref.shape[0]
    key_rows = q_ref.shape[0]
    loads = dict(
        zip(
            ("n2", "mid", "wout", "mixed", "q", "k", "v", "st", "normed", "wqkv", "x"),
            copies(
                [
                    (n2_i, n2_ref), (mid_i, mid_ref), (wout_i, wout), (mixed_i, mixed_ref), (q_i, q_ref), (k_i, k_ref), (v_i, v_ref),
                    (st_i, st_ref), (normed_i, normed_ref), (wqkv_i, wqkv), (x_i, x_ref),
                ],
                sem_in,
            ),
        )
    )

    def ffn_loads(t):
        here = pl.ds(pl.multiple_of(t * FF_STEP, FF_STEP), FF_STEP)
        there = pl.ds(pl.multiple_of(FF + t * FF_STEP, FF_STEP), FF_STEP)
        parts = [(wd_i.at[here, :], wd.at[here, :])]
        for cols in (here, there):
            parts += [(gu_i.at[:, cols], gu_ref.at[:, cols]), (wgu_i.at[:, cols], wgu.at[:, cols])]
        return [pltpu.make_async_copy(src, dst, sem_ffn.at[t, i]) for i, (src, dst) in enumerate(parts)]

    loads["n2"].start()
    for t in range(FF // FF_STEP):
        for load in ffn_loads(t):
            load.start()
    for name, load in loads.items():
        if name != "n2":
            load.start()
    put = functools.partial(put_tiles, places, zones)
    spares = spare.shape[0] - 1
    if spares > 0:
        zero[...] = jnp.zeros(zero.shape, bf16)

        @pl.loop(0, spares)
        def _(i):
            pltpu.make_async_copy(zero, tiles_out[0].at[spare[i]], sem_zero).start()

    key = lax.broadcasted_iota(jnp.int32, bias.shape, 0)
    query = lax.broadcasted_iota(jnp.int32, bias.shape, 1)
    bias[...] = jnp.where((key <= query) & (key < length[0]), 0.0, masked_score)
    big[...] = jnp.zeros(big.shape, f32)
    loads["n2"].wait()
    turned[...] = n2_ref[...].T

    @pl.loop(0, FF // FF_STEP)
    def _(t):
        for load in ffn_loads(t):
            load.wait()
        at = pl.multiple_of(t * FF_STEP, FF_STEP)
        here = pl.ds(at, FF_STEP)
        there = pl.ds(FF + at, FF_STEP)
        back_ffn = back_ref[...].astype(bf16)
        d_act = nt(back_ffn, wd[here, :])
        gate = gu_ref[:, here].astype(f32)
        up = gu_ref[:, there].astype(f32)
        sig = 1.0 / (1.0 + jnp.exp(-gate))
        silu = gate * sig
        act = (silu * up).astype(bf16)
        d_gate = (d_act * up * (sig * (1.0 + gate * (1.0 - sig)))).astype(bf16)
        d_up = (d_act * silu).astype(bf16)
        gd[here, :] = tn(act, back_ffn).astype(bf16)
        ggu[:, here] = nn(turned[...], d_gate).astype(bf16)
        ggu[:, there] = nn(turned[...], d_up).astype(bf16)
        per = FF_STEP // BLOCK
        put(3, gd, tiles_out, sem_out.at[3], t * per, (t + 1) * per, 0, D // BLOCK)
        put(2, ggu, tiles_out, sem_out.at[2], 0, D // BLOCK, t * per, per)
        put(2, ggu, tiles_out, sem_out.at[2], 0, D // BLOCK, FF // BLOCK + t * per, per)
        big[...] += nt(d_gate, wgu[:, here]) + nt(d_up, wgu[:, there])

    loads["mid"].wait()
    step, gain = rms_back(big[...], mid_ref[...], g_ref[1:2, :])
    gain_ref[1:2, :] = gain
    dx_ref[...] = back_ref[...] + step
    back_attn = dx_ref[...].astype(bf16)
    loads["wout"].wait()
    mixed_back[0:rows, :] = nt(back_attn, wout[...]).astype(bf16)
    mixed_back[rows:, :] = jnp.zeros((key_rows - rows, D), bf16)
    loads["mixed"].wait()
    gout[...] = tn(mixed_ref[...], back_attn).astype(bf16)
    put(1, gout, tiles_out, sem_out.at[1], 0, D // BLOCK, 0, D // BLOCK)
    for name in ("q", "k", "v", "st"):
        loads[name].wait()
    by_head = st_ref[...].T
    for h in range(HEADS):
        levels[h] = by_head[h : h + 1, :]

    @pl.loop(0, HEADS // 2)
    def _(p):
        cols = pl.ds(pl.multiple_of(p * PAIR, PAIR), PAIR)
        low = lax.broadcasted_iota(jnp.int32, (key_rows, PAIR), 1) < HEAD_DIM

        def stacked(t, n):
            return jnp.concatenate([jnp.where(low[:n], t[:n], 0), jnp.where(low[:n], 0, t[:n])], 0)

        def chosen(t, n):
            return jnp.where(low[:n], t[:n], t[n:])

        for q0, q1 in query_blocks(key_rows):
            kend, count = q1, q1 - q0
            keys, values = k_ref[:kend, cols], v_ref[:kend, cols]
            queries, backs = q_ref[q0:q1, cols], mixed_back[q0:q1, cols]
            level = jnp.stack([levels[2 * p + h, :, q0:q1] for h in range(2)], 0)
            scores = nt(stacked(keys, kend), queries).reshape(2, kend, count)
            soft = jnp.exp(scores + bias[:kend, q0:q1][None] - level)
            d_prob = nt(stacked(values, kend), backs).reshape(2, kend, count)
            row_dot = jnp.sum(soft * d_prob, 1, keepdims=True)
            d_score = (soft * (d_prob - row_dot)).astype(bf16)
            d_value = chosen(nn(soft.astype(bf16).reshape(2 * kend, count), backs), kend)
            d_key = chosen(nn(d_score.reshape(2 * kend, count), queries), kend)
            d_query = jnp.where(low[:count], tn(d_score[0], keys), tn(d_score[1], keys))
            sums[0, q0:q1, :] = d_query * HEAD_DIM ** (-0.5)
            if q0 > 0:
                sums[1, :q0, :] += d_key[:q0]
                sums[2, :q0, :] += d_value[:q0]
            sums[1, q0:kend, :] = d_key[q0:]
            sums[2, q0:kend, :] = d_value[q0:]
        for part in range(2):
            t = sums[part, 0:rows, :]
            dproj[:, pl.ds(pl.multiple_of(part * D + p * PAIR, PAIR), PAIR)] = (
                t * cos_ref[...] - swap_halves(t) * sin_ref[...]
            ).astype(bf16)
        dproj[:, pl.ds(pl.multiple_of(2 * D + p * PAIR, PAIR), PAIR)] = sums[2, 0:rows, :].astype(bf16)

    loads["normed"].wait()
    turned[...] = normed_ref[...].T
    loads["wqkv"].wait()
    for part in range(3):
        cols = slice(part * D, (part + 1) * D)
        gqkv[:, cols] = nn(turned[...], dproj[:, cols]).astype(bf16)
        put(0, gqkv, tiles_out, sem_out.at[0], 0, D // BLOCK, part * (D // BLOCK), D // BLOCK)
        if part == 0:
            big[...] = nt(dproj[:, cols], wqkv[:, cols])
        else:
            big[...] += nt(dproj[:, cols], wqkv[:, cols])

    loads["x"].wait()
    step, gain = rms_back(big[...], x_ref[...], g_ref[0:1, :])
    gain_ref[0:1, :] = gain
    dx_ref[...] += step
    for m, grad in enumerate((gqkv, gout, ggu, gd)):
        pltpu.make_async_copy(grad, grad, sem_out.at[m]).wait()
    if spares > 0:

        @pl.loop(0, spares)
        def _(i):
            pltpu.make_async_copy(zero, tiles_out[0].at[spare[i]], sem_zero).wait()


def weight_shapes():
    return [(r * BLOCK, c * BLOCK) for r, c in GRIDS]


VMEM = pl.BlockSpec(memory_space=pltpu.VMEM)
SMEM = pl.BlockSpec(memory_space=pltpu.SMEM)
HBM = pl.BlockSpec(memory_space=pl.ANY)


def like(struct):
    return pltpu.VMEM(struct.shape, struct.dtype)


def cost(flops, bytes_accessed):
    return pl.CostEstimate(flops=flops, bytes_accessed=bytes_accessed, transcendentals=0)


def forward_layer(slots, length, x, gains, cos, sin, gathered):
    rows = x.shape[0]
    key_rows = round_up(rows, BLOCK)
    S = jax.ShapeDtypeStruct
    saved = [
        S((rows, D), bf16),
        S((key_rows, D), bf16),
        S((key_rows, D), bf16),
        S((key_rows, D), bf16),
        S((key_rows, BLOCK), f32),
        S((rows, D), bf16),
        S((rows, D), f32),
        S((rows, D), bf16),
        S((rows, 2 * FF), bf16),
    ] + [S(s, bf16) for s in weight_shapes()]
    return pl.pallas_call(
        forward_kernel,
        out_shape=[S((rows, D), f32)] + saved,
        in_specs=[SMEM, SMEM, VMEM, VMEM, VMEM, VMEM, HBM],
        out_specs=[VMEM] + [HBM] * 13,
        scratch_shapes=[like(s) for s in saved]
        + [
            pltpu.VMEM((rows, key_rows), f32),
            pltpu.SemaphoreType.DMA((4,)),
            pltpu.SemaphoreType.DMA((13,)),
        ],
        compiler_params=pltpu.CompilerParams(vmem_limit_bytes=VMEM_BYTES),
        cost_estimate=cost(2 * rows * PER_LAYER * BLOCK * BLOCK, 40 * 2**20),
        name="forward_block",
    )(slots, length, x, gains, cos, sin, gathered)


def tile_arrays(zones):
    return [jax.ShapeDtypeStruct((size, BLOCK, BLOCK), bf16) for _, _, size in zones]


def backward_layer(places, spare, length, back, gains, cos, sin, saved, zones, begun):
    rows = back.shape[0]
    key_rows = round_up(rows, BLOCK)
    S = jax.ShapeDtypeStruct
    args = (places, spare, length, back, gains, cos, sin) + tuple(saved)
    late = 2 + len(zones) - len(begun)
    return pl.pallas_call(
        functools.partial(backward_kernel, len(begun), zones),
        out_shape=[S((rows, D), f32), S((2, D), f32)] + tile_arrays(zones),
        in_specs=[SMEM] * 3 + [VMEM] * 4 + [HBM] * (14 + len(begun)),
        out_specs=[VMEM, VMEM] + [HBM] * len(zones),
        input_output_aliases={len(args) + i: late + i for i in range(len(begun))},
        scratch_shapes=[like(s) for s in saved]
        + [pltpu.VMEM(s, bf16) for s in weight_shapes()]
        + [
            pltpu.VMEM((D, rows), bf16),
            pltpu.VMEM((key_rows, key_rows), f32),
            pltpu.VMEM((HEADS, 1, key_rows), f32),
            pltpu.VMEM((3, key_rows, PAIR), f32),
            pltpu.VMEM((rows, D), f32),
            pltpu.VMEM((key_rows, D), bf16),
            pltpu.VMEM((rows, 3 * D), bf16),
            pltpu.VMEM((BLOCK, BLOCK), bf16),
            pltpu.SemaphoreType.DMA((11,)),
            pltpu.SemaphoreType.DMA((FF // FF_STEP, 5)),
            pltpu.SemaphoreType.DMA((4,)),
            pltpu.SemaphoreType.DMA,
        ],
        compiler_params=pltpu.CompilerParams(vmem_limit_bytes=VMEM_BYTES),
        cost_estimate=cost(4 * rows * PER_LAYER * BLOCK * BLOCK + 20 * rows * rows * D, 60 * 2**20),
        name="backward_block",
    )(*args, *begun)


def optimizer_kernel(factor, rank, g_ref, m_ref, s_ref, r_ref, wg_ref, ns_ref, nm_ref, nc_ref):
    f = factor[0]
    count = m_ref.shape[0]
    for i in range(count):
        gb = g_ref[rank[pl.program_id(0) * count + i]]
        wg_ref[i] = gb.astype(f32) * f
        half = (1.0 - decay_rate) * f * f
        ns_ref[i, 0] = decay_rate * s_ref[i, 0] + half * nt(gb, gb)
        ns_ref[i, 1] = decay_rate * s_ref[i, 1] + half * tn(gb, gb)
        left = nn(r_ref[i, 0].astype(bf16), (gb.astype(f32) * f).astype(bf16)).astype(bf16)
        new = m_ref[i] - step_rate * nn(left, r_ref[i, 1].astype(bf16))
        nm_ref[i] = new
        nc_ref[i] = new.astype(bf16)


def optimizer(factor, rank, owned, master, statistics, inverse_roots):
    count = owned.shape[0]
    per = max(n for n in range(1, 13) if count % n == 0)
    S = jax.ShapeDtypeStruct
    one = pl.BlockSpec((per, BLOCK, BLOCK), lambda i: (i, 0, 0))
    two = pl.BlockSpec((per, 2, BLOCK, BLOCK), lambda i: (i, 0, 0, 0))
    return pl.pallas_call(
        optimizer_kernel,
        grid=(count // per,),
        out_shape=[
            S(master.shape, f32),
            S(statistics.shape, f32),
            S(master.shape, f32),
            S(master.shape, bf16),
        ],
        in_specs=[SMEM, SMEM, VMEM, one, two, two],
        out_specs=[one, two, one, one],
        compiler_params=pltpu.CompilerParams(vmem_limit_bytes=VMEM_BYTES),
        name="optimizer",
    )(factor, rank, owned, master, statistics, inverse_roots)


def to_images(local, bands, band):
    images, band_rows = local.shape[0], local.shape[-2]
    padded = jnp.concatenate([local, jnp.zeros((bands - images,) + local.shape[1:], local.dtype)], 0)
    whole = jnp.zeros((bands,) + local.shape[1:], local.dtype)
    for shift in range(bands):
        block = lax.dynamic_index_in_dim(padded, (band + shift) % bands, 0, keepdims=False)
        if shift > 0:
            pairs = [(b, (b + shift) % bands) for b in range(bands) if (b + shift) % bands < images]
            block = lax.ppermute(block, "band", pairs)
        whole = lax.dynamic_update_index_in_dim(whole, block, (band - shift) % bands, 0)
    return whole


def send_to_bands(whole, images, bands, band):
    blocks = []
    for shift in range(bands):
        block = lax.dynamic_index_in_dim(whole, (band + shift) % bands, 0, keepdims=False)
        if shift > 0:
            pairs = [(b, (b + shift) % bands) for b in range(images)]
            block = lax.ppermute(block, "band", pairs)
        blocks.append(block)
    return tuple(blocks)


def at_bands(blocks, images, bands, band):
    local = jnp.zeros((bands,) + blocks[0].shape, blocks[0].dtype)
    for shift, block in enumerate(blocks):
        local = lax.dynamic_update_index_in_dim(local, block, (band - shift) % bands, 0)
    return local[:images]


EARLY = (36,)
LATE = (24, 28, 20)
LEAST = (PER_LAYER,)


def chunk_places(slot_of_block, per_owner, me):
    blocks = slot_of_block.shape[0]
    block_of_slot = jnp.zeros((blocks,), jnp.int32).at[slot_of_block].set(
        jnp.arange(blocks, dtype=jnp.int32)
    )
    by_owner = block_of_slot.reshape(-1, per_owner)
    rank = jnp.sum(by_owner[:, None, :] > by_owner[:, :, None], -1, dtype=jnp.int32)
    owner = jnp.arange(by_owner.shape[0], dtype=jnp.int32)
    relative = (owner ^ me)[:, None]
    owner = owner[:, None]
    core, x, y = relative % 2, relative // 2 % 2, relative // 4
    place = jnp.zeros_like(rank)
    clean = jnp.bool_(True)
    start = 0
    for size, least in zip(EARLY, LEAST):
        at = rank - start
        here = (at >= 0) & (at < size)
        place = jnp.where(here, 8 * start + owner * size + at, place)
        clean = clean & jnp.all(jnp.where(here, by_owner >= least, True))
        start += size
    for size in LATE:
        half = size // 2
        at = rank - start
        here = (at >= 0) & (at < size)
        spot = jnp.where(at < half, (x * 2 + y) * half + at, 4 * half + (y * 2 + x) * half + at - half)
        place = jnp.where(here, 8 * start + core * 4 * size + spot, place)
        start += size
    return place.reshape(-1)[slot_of_block], rank, clean


CORE = [(i, i ^ 1) for i in range(8)]
ALONG_X = [(i, i ^ 2) for i in range(8)]
ALONG_Y = [(i, i ^ 4) for i in range(8)]


def wide(t, lo, hi):
    return t[lo:hi].astype(f32)


class Bands:
    def to_meet(self, plane):
        self.plane = plane
        return (plane,)

    def go_meet(self, plane):
        return lax.ppermute(plane, "band", [(0, 1)]), lax.ppermute(plane, "band", [(2, 1)])

    def to_part(self, up, down):
        self.total = (self.plane.astype(f32) + up.astype(f32) + down.astype(f32)).astype(bf16)
        return (self.total,)

    def go_part(self, total):
        return lax.ppermute(total, "band", [(1, 0)]), lax.ppermute(total, "band", [(1, 2)])

    def to_last(self, to_first, to_third):
        self.to_first, self.to_third = to_first, to_third
        return (to_third,)

    def go_last(self, to_third):
        return (lax.ppermute(to_third, "band", [(2, 3)]),)

    def to_end(self, to_last):
        band = lax.axis_index("band")
        total = jnp.where(band == 0, self.to_first, self.total)
        total = jnp.where(band == 2, self.to_third, total)
        self.total = jnp.where(band == 3, to_last, total)
        return (self.total,)

    def go_end(self, total):
        return ()


class Chunk(Bands):
    def __init__(self, kept, sent):
        self.half = kept.shape[0] // 8
        self.kept, self.sent = kept, sent

    def chip(self, lo, hi):
        lo, hi = lo * self.half, hi * self.half
        return wide(self.kept, lo, hi) + wide(self.received, lo, hi)

    def to_core(self):
        return (self.sent,)

    def go_core(self, send):
        return (lax.ppermute(send, "dp", CORE),)

    def to_plane(self, received):
        self.received = received
        return self.chip(2, 4).astype(bf16), self.chip(6, 8).astype(bf16)

    def go_plane(self, send_x, send_y):
        return lax.ppermute(send_x, "dp", ALONG_X), lax.ppermute(send_y, "dp", ALONG_Y)

    go_turn = go_plane

    def to_turn(self, from_x, from_y):
        self.from_x, self.from_y = from_x, from_y
        half = self.half
        send_y = (self.chip(1, 2) + wide(from_x, half, 2 * half)).astype(bf16)
        send_x = (self.chip(5, 6) + wide(from_y, half, 2 * half)).astype(bf16)
        return send_x, send_y

    def to_meet(self, from_x, from_y):
        half = self.half
        one = self.chip(0, 1) + wide(self.from_x, 0, half) + wide(from_y, 0, half)
        two = self.chip(4, 5) + wide(self.from_y, 0, half) + wide(from_x, 0, half)
        self.plane = jnp.concatenate([one, two], 0).astype(bf16)
        return (self.plane,)


class Sequence:
    def __init__(self):
        self.before = ()
        self.arrived = {}

    def round(self, *steps):
        arrived = [tuple(self.arrived.get(chunk, ())) for chunk, _ in steps]
        flat = sum(arrived, ())
        flat = lax.optimization_barrier(flat + self.before)
        at, self.before = 0, ()
        for (chunk, name), had in zip(steps, arrived):
            sends = getattr(chunk, "to_" + name)(*flat[at : at + len(had)])
            at += len(had)
            self.arrived[chunk] = getattr(chunk, "go_" + name)(*sends)
            self.before = self.before + tuple(sends)

    def wait_for(self, *arrays):
        arrays = lax.optimization_barrier(arrays + self.before)[: len(arrays)]
        self.before = self.before + arrays
        return arrays


def rope_tables(rows):
    half = HEAD_DIM // 2
    frequency = rope_base ** (-(jnp.arange(half, dtype=f32) * 2.0 / HEAD_DIM))
    angles = jnp.arange(rows, dtype=jnp.int32).astype(f32)[:, None] * frequency[None, :]
    cosine, sine = jnp.cos(angles), jnp.sin(angles)
    return jnp.tile(cosine, (1, 4)), jnp.tile(jnp.concatenate([-sine, sine], 1), (1, 2))


def shards(
    tokens,
    cotangent,
    lengths,
    slot_of_block,
    master,
    statistics,
    inverse_roots,
    gain_values,
    gain_moments,
):
    images, band_rows, _ = tokens.shape
    band = lax.axis_index("band")
    bands = lax.axis_size("band")
    seq = band_rows * bands
    rows = round_up(seq, 16)
    gathered = lax.all_gather(master.astype(bf16), "dp", axis=0, tiled=True)
    slot_count = gathered.shape[0]

    arrived = to_images(jnp.stack([tokens, cotangent], 1), bands, band)
    token_rows = jnp.pad(arrived[:, 0].reshape(seq, D), ((0, rows - seq), (0, 0)))
    back_rows = jnp.pad(arrived[:, 1].reshape(seq, D), ((0, rows - seq), (0, 0)))
    length = lengths[jnp.minimum(band, images - 1)]
    valid = (jnp.arange(rows, dtype=jnp.int32) < length).astype(f32)
    length = length.reshape(1)
    cos, sin = rope_tables(rows)

    spare_count = slot_count - slot_of_block.shape[0]
    spare = jnp.zeros((1,), jnp.int32)
    if spare_count > 0:
        used = jnp.zeros((slot_count,), jnp.int32).at[slot_of_block].set(1)
        spare = jnp.concatenate([jnp.argsort(used)[:spare_count].astype(jnp.int32), spare])

    hidden = token_rows.astype(f32)
    inputs, saves = [], []
    for layer in range(LAYERS):
        slots = slot_of_block[layer * PER_LAYER : (layer + 1) * PER_LAYER]
        gains = gain_values[2 * layer : 2 * layer + 2]
        inputs.append(hidden)
        hidden, *saved = forward_layer(slots, length, hidden, gains, cos, sin, gathered)
        saves.append(saved)

    def send_rows(t):
        return send_to_bands(t[:seq].astype(bf16).reshape(bands, band_rows, D), images, bands, band)

    output_blocks = send_rows(hidden)

    back = back_rows.astype(f32) * valid[:, None]
    per_owner = master.shape[0]
    me = lax.axis_index("dp")
    by_permutes = (
        lax.axis_size("dp") == 8
        and bands == 4
        and images == 3
        and slot_count == slot_of_block.shape[0]
        and per_owner == sum(EARLY) + sum(LATE)
    )
    if by_permutes:
        places, ranks, clean = chunk_places(slot_of_block, per_owner, me)
        rank = lax.dynamic_index_in_dim(ranks, me, 0, keepdims=False)
        ends = [8 * sum(EARLY[: i + 1]) for i in range(len(EARLY))]
        bounds = [0] + ends
        for size in LATE:
            bounds += [bounds[-1] + 4 * size, bounds[-1] + 8 * size]
        zones = tuple((low, high, high - low) for low, high in zip(bounds, bounds[1:]))
    else:
        places, rank = slot_of_block, jnp.arange(per_owner, dtype=jnp.int32)
        zones = ((0, slot_count, slot_count),)

    def backward(layer, back, tiles, zones):
        fill = spare if layer == LAYERS - 1 else spare[-1:]
        back, gains, *tiles = backward_layer(
            places[layer * PER_LAYER : (layer + 1) * PER_LAYER], fill, length, back,
            gain_values[2 * layer : 2 * layer + 2], cos, sin, (inputs[layer], *saves[layer]), zones, tiles,
        )
        return back, gains, tiles

    if by_permutes:
        back, gains_top, tiles = backward(1, back, [], zones)
        early = tiles[:1]
        ready, *output_blocks = lax.optimization_barrier((tiles[0], *output_blocks))
        early_sums = [lax.psum_scatter(ready, "dp", scatter_dimension=0, tiled=True)]
        back, gains_bottom, tiles = backward(0, back, tiles[1:], zones)
        missed, *late = tiles
        gains = jnp.concatenate([gains_bottom, gains_top], 0).astype(bf16).reshape(-1, BLOCK)
        gains = jnp.pad(gains, ((0, BLOCK - gains.shape[0]), (0, 0)))[None]
        sequence = Sequence()
        chunks = [Chunk(*late[2 * i : 2 * i + 2]) for i in range(len(LATE))]
        one, two, three = chunks
        top = Bands()
        sequence.arrived[top] = (jnp.concatenate([early_sums[0], gains], 0),)
        sequence.round((one, "core"), (two, "core"), (three, "core"))
        sequence.round((one, "plane"))
        sequence.round((top, "meet"))
        sequence.round((one, "turn"))
        sequence.round((two, "plane"))
        sequence.round((one, "meet"))
        sequence.round((top, "part"))
        sequence.round((two, "turn"))
        sequence.round((three, "plane"))
        sequence.round((one, "part"))
        sequence.round((two, "meet"))
        sequence.round((top, "last"))
        sequence.round((three, "turn"))
        sequence.round((three, "meet"))
        sequence.round((two, "part"))
        sequence.round((one, "last"))
        sequence.round((three, "part"), (top, "end"))
        sequence.round((two, "last"))
        sequence.round((three, "last"))
        sequence.round((one, "end"))
        sequence.round((two, "end"))
        sequence.round((three, "end"))
        early_total = top.total[:-1]

        def again(trip, total):
            _, spare_tiles, *parts = lax.optimization_barrier((trip, missed, *early))
            block_at = jnp.argsort(places)
            sums, start = [], 0
            for part, end, least in zip(parts, ends, LEAST):
                late_here = (block_at[start:end] < least)[:, None, None]
                whole = jnp.where(late_here, spare_tiles[start:end], part)
                sums.append(lax.psum_scatter(whole, "dp", scatter_dimension=0, tiled=True))
                start = end
            return lax.psum(jnp.concatenate(sums, 0), "band")

        early_total = lax.fori_loop(0, jnp.where(clean, 0, 1), again, early_total)
        owned = jnp.concatenate([early_total] + [chunk.total for chunk in chunks], 0)
        gain_total = top.total[-1].astype(f32)[: gain_values.size // BLOCK].reshape(-1, D)
    else:
        back, gains_top, tiles = backward(1, back, [], zones)
        back, gains_bottom, tiles = backward(0, back, tiles, zones)
        owned = lax.psum_scatter(tiles[0], "dp", scatter_dimension=0, tiled=True)
        owned = lax.psum(owned, "band")
        gain_total = lax.psum(jnp.concatenate([gains_bottom, gains_top], 0), ("dp", "band"))

    layer_output = at_bands(output_blocks, images, bands, band)
    owned_f = owned.astype(f32)
    owned_squares = jnp.sum(owned_f * owned_f)
    if by_permutes:
        last = jnp.concatenate([gain_total.reshape(-1, BLOCK), jnp.broadcast_to(owned_squares, (1, BLOCK))], 0)
        for pairs in (CORE, ALONG_X, ALONG_Y):
            last = last + lax.ppermute(last, "dp", pairs)
        gain_total, owned_squares = last[:-1].reshape(gain_values.shape), last[-1, 0]
    else:
        owned_squares = lax.psum(owned_squares, "dp")
    grad_norm = jnp.sqrt(owned_squares + jnp.sum(gain_total * gain_total))
    factor = jnp.minimum(1.0, clip_limit / grad_norm)
    back, factor = lax.optimization_barrier((back, factor))
    input_grad = at_bands(send_rows(back), images, bands, band)
    weight_grads, new_statistics, new_master, master_copy = optimizer(
        factor.reshape(1), rank, owned, master, statistics, inverse_roots
    )
    gain_grads = gain_total * factor
    new_moments = decay_rate * gain_moments + (1.0 - decay_rate) * gain_grads * gain_grads
    new_gains = gain_values - gain_rate * gain_grads / (jnp.sqrt(new_moments) + epsilon)
    return (
        layer_output,
        input_grad,
        weight_grads,
        grad_norm,
        new_statistics,
        new_master,
        master_copy,
        gain_grads,
        new_moments,
        new_gains,
    )


def solution(mesh):
    return jax.shard_map(
        shards,
        mesh=mesh,
        in_specs=(
            P("dp", "band", None),
            P("dp", "band", None),
            P("dp"),
            P(),
            P("dp", None, None),
            P("dp", None, None, None),
            P("dp", None, None, None),
            P(),
            P(),
        ),
        out_specs=(
            P("dp", "band", None),
            P("dp", "band", None),
            P("dp", None, None),
            P(),
            P("dp", None, None, None),
            P("dp", None, None),
            P("dp", None, None),
            P(),
            P(),
            P(),
        ),
        check_vma=False,
    )
```

```python
import functools

import jax
import jax.numpy as jnp
from jax import lax
from jax.experimental import pallas as pl
from jax.experimental.pallas import tpu as pltpu
from jax.sharding import PartitionSpec as P

D = 768
HEADS = 12
HEAD_DIM = 64
FF = 2048
LAYERS = 2
BLOCK = 128
PAIR = 2 * HEAD_DIM

epsilon = 1e-05
rope_base = 10000.0
decay_rate = 0.5
step_rate = 0.4
gain_rate = 0.2
clip_limit = 1.0
masked_score = -1e30
VMEM_BYTES = 62 * 2**20

f32 = jnp.float32
bf16 = jnp.bfloat16

GRIDS = [
    (D // BLOCK, 3 * D // BLOCK),
    (D // BLOCK, D // BLOCK),
    (D // BLOCK, 2 * FF // BLOCK),
    (FF // BLOCK, D // BLOCK),
]
COUNTS = [r * c for r, c in GRIDS]
OFFSETS = [sum(COUNTS[:i]) for i in range(4)]
PER_LAYER = sum(COUNTS)
FF_STEP = 512
TOGETHER = 4


def round_up(n, m):
    return -(-n // m) * m


def nn(a, b):
    return lax.dot_general(a, b, (((1,), (0,)), ((), ())), preferred_element_type=f32)


def nt(a, b):
    return lax.dot_general(a, b, (((1,), (1,)), ((), ())), preferred_element_type=f32)


def tn(a, b):
    return lax.dot_general(a, b, (((0,), (0,)), ((), ())), preferred_element_type=f32)


def query_blocks(rows, step=256):
    return [(s, min(s + step, rows)) for s in range(0, rows, step)]


def swap_halves(t):
    lane = lax.broadcasted_iota(jnp.int32, t.shape, 1)
    half = HEAD_DIM // 2
    return jnp.where(lane % HEAD_DIM < half, pltpu.roll(t, PAIR - half, 1), pltpu.roll(t, half, 1))


def rms(m):
    return lax.rsqrt(jnp.mean(m * m, -1, keepdims=True) + epsilon)


def rms_back(u, m, g):
    r = rms(m)
    t = u * g
    dot = jnp.mean(t * m, -1, keepdims=True)
    return r * t - m * (r * r * r * dot), jnp.sum(u * m * r, 0, keepdims=True)


def copies(pairs, sem):
    return [pltpu.make_async_copy(src, dst, sem.at[i]) for i, (src, dst) in enumerate(pairs)]


def forward_kernel(
    slots, length, x_ref, g_ref, cos_ref, sin_ref, w_hbm,
    xn_ref, normed_o, q_o, k_o, v_o, st_o, mixed_o, mid_o, n2_o, gu_o, wqkv_o, wout_o, wgu_o, wd_o,
    normed_ref, q_ref, k_ref, v_ref, st_ref, mixed_ref, mid_ref, n2_ref, gu_ref,
    wqkv, wout, wgu, wd, bias, sem_in, sem_out,
):
    rows = x_ref.shape[0]
    key_rows = q_ref.shape[0]
    held = (wqkv, wout, wgu, wd)
    for m in range(4):
        tile_rows, tile_cols = GRIDS[m]

        @pl.loop(0, tile_rows)
        def _(i, m=m, tile_cols=tile_cols):
            for j in range(tile_cols):
                slot = slots[OFFSETS[m] + i * tile_cols + j]
                pltpu.make_async_copy(
                    w_hbm.at[slot],
                    held[m].at[pl.ds(pl.multiple_of(i * BLOCK, BLOCK), BLOCK), pl.ds(j * BLOCK, BLOCK)],
                    sem_in.at[m],
                ).start()

    def arrive(m):
        pltpu.make_async_copy(held[m], held[m], sem_in.at[m]).wait()

    saves = copies(
        [
            (normed_ref, normed_o), (q_ref, q_o), (k_ref, k_o), (v_ref, v_o), (st_ref, st_o),
            (mixed_ref, mixed_o), (mid_ref, mid_o), (n2_ref, n2_o), (gu_ref, gu_o),
            (wqkv, wqkv_o), (wout, wout_o), (wgu, wgu_o), (wd, wd_o),
        ],
        sem_out,
    )
    query = lax.broadcasted_iota(jnp.int32, bias.shape, 0)
    key = lax.broadcasted_iota(jnp.int32, bias.shape, 1)
    bias[...] = jnp.where((key <= query) & (key < length[0]), 0.0, masked_score)
    x = x_ref[...]
    normed_ref[...] = (x * rms(x) * g_ref[0:1, :]).astype(bf16)
    saves[0].start()
    tail = key_rows - rows
    for ref in (q_ref, k_ref, v_ref):
        ref[rows:, :] = jnp.zeros((tail, D), bf16)
    arrive(0)
    saves[9].start()

    @pl.loop(0, 2)
    def _(part):
        acc = nn(normed_ref[...], wqkv[:, pl.ds(pl.multiple_of(part * D, D), D)])
        scale = jnp.where(part == 0, HEAD_DIM ** (-0.5), 1.0)
        for p in range(HEADS // 2):
            t = acc[:, p * PAIR : (p + 1) * PAIR]
            rot = ((t * cos_ref[...] + swap_halves(t) * sin_ref[...]) * scale).astype(bf16)

            @pl.when(part == 0)
            def _(p=p, rot=rot):
                q_ref[0:rows, p * PAIR : (p + 1) * PAIR] = rot

            @pl.when(part == 1)
            def _(p=p, rot=rot):
                k_ref[0:rows, p * PAIR : (p + 1) * PAIR] = rot

    v_ref[0:rows, :] = nn(normed_ref[...], wqkv[:, 2 * D :]).astype(bf16)
    for i in (1, 2, 3):
        saves[i].start()
    st_ref[...] = jnp.zeros(st_ref.shape, f32)

    @pl.loop(0, HEADS // TOGETHER)
    def _(g):
        width = TOGETHER * HEAD_DIM
        cols = pl.ds(pl.multiple_of(g * width, width), width)
        for q0, q1 in query_blocks(rows):
            count = q1 - q0
            kend = min(round_up(q1, BLOCK), key_rows)
            qp = q_ref[q0:q1, cols]
            head = lax.broadcasted_iota(jnp.int32, qp.shape, 1) // HEAD_DIM
            stacked = jnp.concatenate([jnp.where(head == h, qp, 0) for h in range(TOGETHER)], 0)
            s = nt(stacked, k_ref[:kend, cols]).reshape(TOGETHER, count, kend) + bias[q0:q1, :kend][None]
            top = jnp.max(s, -1, keepdims=True)
            e = jnp.exp(s - top)
            total = jnp.sum(e, -1, keepdims=True)
            out = nn(e.astype(bf16).reshape(TOGETHER * count, kend), v_ref[:kend, cols])
            out = out.reshape(TOGETHER, count, width) / total
            level = top + jnp.log(total)
            mixed = out[0]
            lane = lax.broadcasted_iota(jnp.int32, (count, BLOCK), 1)
            levels = st_ref[q0:q1, :]
            for h in range(TOGETHER):
                mixed = jnp.where(head == h, out[h], mixed)
                levels = jnp.where(lane == g * TOGETHER + h, level[h], levels)
            mixed_ref[q0:q1, cols] = mixed.astype(bf16)
            st_ref[q0:q1, :] = levels

    saves[4].start()
    saves[5].start()
    arrive(1)
    saves[10].start()
    middle = x_ref[...] + nn(mixed_ref[...], wout[...])
    mid_ref[...] = middle
    saves[6].start()
    n2_ref[...] = (middle * rms(middle) * g_ref[1:2, :]).astype(bf16)
    saves[7].start()
    arrive(2)
    saves[11].start()
    arrive(3)
    saves[12].start()
    xn_ref[...] = mid_ref[...]

    @pl.loop(0, FF // FF_STEP)
    def _(t):
        at = pl.multiple_of(t * FF_STEP, FF_STEP)
        gate = nn(n2_ref[...], wgu[:, pl.ds(at, FF_STEP)])
        up = nn(n2_ref[...], wgu[:, pl.ds(FF + at, FF_STEP)])
        act = (gate / (1.0 + jnp.exp(-gate)) * up).astype(bf16)
        gu_ref[:, pl.ds(at, FF_STEP)] = gate.astype(bf16)
        gu_ref[:, pl.ds(FF + at, FF_STEP)] = up.astype(bf16)
        xn_ref[...] += nn(act, wd[pl.ds(at, FF_STEP), :])

    saves[8].start()
    for save in saves:
        save.wait()


def put_tiles(places, zones, m, grad, outs, sem, i0, i1, j0, count_j):
    @pl.loop(i0, i1)
    def _(i):
        for jj in range(count_j):
            j = j0 + jj
            place = places[OFFSETS[m] + i * GRIDS[m][1] + j]
            tile = grad.at[
                pl.ds(pl.multiple_of(i * BLOCK, BLOCK), BLOCK),
                pl.ds(pl.multiple_of(j * BLOCK, BLOCK), BLOCK),
            ]
            if len(outs) == 1:
                pltpu.make_async_copy(tile, outs[0].at[place], sem).start()
                continue
            for out, (low, high, _) in zip(outs, zones):

                @pl.when((place >= low) & (place < high))
                def _(tile=tile, out=out, place=place, low=low):
                    pltpu.make_async_copy(tile, out.at[place - low], sem).start()


def backward_kernel(
    begun, zones, places, spare, length, back_ref, g_ref, cos_ref, sin_ref,
    x_i, normed_i, q_i, k_i, v_i, st_i, mixed_i, mid_i, n2_i, gu_i, wqkv_i, wout_i, wgu_i, wd_i, *rest
):
    dx_ref, gain_ref, *rest = rest[begun:]
    tiles_out, rest = rest[: len(zones)], rest[len(zones) :]
    (
        x_ref, normed_ref, q_ref, k_ref, v_ref, st_ref, mixed_ref, mid_ref, n2_ref, gu_ref,
        wqkv, wout, wgu, wd, gqkv, gout, ggu, gd,
        turned, bias, levels, sums, big, mixed_back, dproj, zero, sem_in, sem_ffn, sem_out, sem_zero,
    ) = rest
    rows = back_ref.shape[0]
    key_rows = q_ref.shape[0]
    loads = dict(
        zip(
            ("n2", "mid", "wout", "mixed", "q", "k", "v", "st", "normed", "wqkv", "x"),
            copies(
                [
                    (n2_i, n2_ref), (mid_i, mid_ref), (wout_i, wout), (mixed_i, mixed_ref), (q_i, q_ref), (k_i, k_ref), (v_i, v_ref),
                    (st_i, st_ref), (normed_i, normed_ref), (wqkv_i, wqkv), (x_i, x_ref),
                ],
                sem_in,
            ),
        )
    )

    def ffn_loads(t):
        here = pl.ds(pl.multiple_of(t * FF_STEP, FF_STEP), FF_STEP)
        there = pl.ds(pl.multiple_of(FF + t * FF_STEP, FF_STEP), FF_STEP)
        parts = [(wd_i.at[here, :], wd.at[here, :])]
        for cols in (here, there):
            parts += [(gu_i.at[:, cols], gu_ref.at[:, cols]), (wgu_i.at[:, cols], wgu.at[:, cols])]
        return [pltpu.make_async_copy(src, dst, sem_ffn.at[t, i]) for i, (src, dst) in enumerate(parts)]

    loads["n2"].start()
    for t in range(FF // FF_STEP):
        for load in ffn_loads(t):
            load.start()
    for name, load in loads.items():
        if name != "n2":
            load.start()
    put = functools.partial(put_tiles, places, zones)
    spares = spare.shape[0] - 1
    if spares > 0:
        zero[...] = jnp.zeros(zero.shape, bf16)

        @pl.loop(0, spares)
        def _(i):
            pltpu.make_async_copy(zero, tiles_out[0].at[spare[i]], sem_zero).start()

    key = lax.broadcasted_iota(jnp.int32, bias.shape, 0)
    query = lax.broadcasted_iota(jnp.int32, bias.shape, 1)
    bias[...] = jnp.where((key <= query) & (key < length[0]), 0.0, masked_score)
    big[...] = jnp.zeros(big.shape, f32)
    loads["n2"].wait()
    turned[...] = n2_ref[...].T

    @pl.loop(0, FF // FF_STEP)
    def _(t):
        for load in ffn_loads(t):
            load.wait()
        at = pl.multiple_of(t * FF_STEP, FF_STEP)
        here = pl.ds(at, FF_STEP)
        there = pl.ds(FF + at, FF_STEP)
        back_ffn = back_ref[...].astype(bf16)
        d_act = nt(back_ffn, wd[here, :])
        gate = gu_ref[:, here].astype(f32)
        up = gu_ref[:, there].astype(f32)
        sig = 1.0 / (1.0 + jnp.exp(-gate))
        silu = gate * sig
        act = (silu * up).astype(bf16)
        d_gate = (d_act * up * (sig * (1.0 + gate * (1.0 - sig)))).astype(bf16)
        d_up = (d_act * silu).astype(bf16)
        gd[here, :] = tn(act, back_ffn).astype(bf16)
        ggu[:, here] = nn(turned[...], d_gate).astype(bf16)
        ggu[:, there] = nn(turned[...], d_up).astype(bf16)
        per = FF_STEP // BLOCK
        put(3, gd, tiles_out, sem_out.at[3], t * per, (t + 1) * per, 0, D // BLOCK)
        put(2, ggu, tiles_out, sem_out.at[2], 0, D // BLOCK, t * per, per)
        put(2, ggu, tiles_out, sem_out.at[2], 0, D // BLOCK, FF // BLOCK + t * per, per)
        big[...] += nt(d_gate, wgu[:, here]) + nt(d_up, wgu[:, there])

    loads["mid"].wait()
    step, gain = rms_back(big[...], mid_ref[...], g_ref[1:2, :])
    gain_ref[1:2, :] = gain
    dx_ref[...] = back_ref[...] + step
    back_attn = dx_ref[...].astype(bf16)
    loads["wout"].wait()
    mixed_back[0:rows, :] = nt(back_attn, wout[...]).astype(bf16)
    mixed_back[rows:, :] = jnp.zeros((key_rows - rows, D), bf16)
    loads["mixed"].wait()
    gout[...] = tn(mixed_ref[...], back_attn).astype(bf16)
    put(1, gout, tiles_out, sem_out.at[1], 0, D // BLOCK, 0, D // BLOCK)
    for name in ("q", "k", "v", "st"):
        loads[name].wait()
    by_head = st_ref[...].T
    for h in range(HEADS):
        levels[h] = by_head[h : h + 1, :]

    @pl.loop(0, HEADS // 2)
    def _(p):
        cols = pl.ds(pl.multiple_of(p * PAIR, PAIR), PAIR)
        low = lax.broadcasted_iota(jnp.int32, (key_rows, PAIR), 1) < HEAD_DIM

        def stacked(t, n):
            return jnp.concatenate([jnp.where(low[:n], t[:n], 0), jnp.where(low[:n], 0, t[:n])], 0)

        def chosen(t, n):
            return jnp.where(low[:n], t[:n], t[n:])

        for q0, q1 in query_blocks(key_rows):
            kend, count = q1, q1 - q0
            keys, values = k_ref[:kend, cols], v_ref[:kend, cols]
            queries, backs = q_ref[q0:q1, cols], mixed_back[q0:q1, cols]
            level = jnp.stack([levels[2 * p + h, :, q0:q1] for h in range(2)], 0)
            scores = nt(stacked(keys, kend), queries).reshape(2, kend, count)
            soft = jnp.exp(scores + bias[:kend, q0:q1][None] - level)
            d_prob = nt(stacked(values, kend), backs).reshape(2, kend, count)
            row_dot = jnp.sum(soft * d_prob, 1, keepdims=True)
            d_score = (soft * (d_prob - row_dot)).astype(bf16)
            d_value = chosen(nn(soft.astype(bf16).reshape(2 * kend, count), backs), kend)
            d_key = chosen(nn(d_score.reshape(2 * kend, count), queries), kend)
            d_query = jnp.where(low[:count], tn(d_score[0], keys), tn(d_score[1], keys))
            sums[0, q0:q1, :] = d_query * HEAD_DIM ** (-0.5)
            if q0 > 0:
                sums[1, :q0, :] += d_key[:q0]
                sums[2, :q0, :] += d_value[:q0]
            sums[1, q0:kend, :] = d_key[q0:]
            sums[2, q0:kend, :] = d_value[q0:]
        for part in range(2):
            t = sums[part, 0:rows, :]
            dproj[:, pl.ds(pl.multiple_of(part * D + p * PAIR, PAIR), PAIR)] = (
                t * cos_ref[...] - swap_halves(t) * sin_ref[...]
            ).astype(bf16)
        dproj[:, pl.ds(pl.multiple_of(2 * D + p * PAIR, PAIR), PAIR)] = sums[2, 0:rows, :].astype(bf16)

    loads["normed"].wait()
    turned[...] = normed_ref[...].T
    loads["wqkv"].wait()
    for part in range(3):
        cols = slice(part * D, (part + 1) * D)
        gqkv[:, cols] = nn(turned[...], dproj[:, cols]).astype(bf16)
        put(0, gqkv, tiles_out, sem_out.at[0], 0, D // BLOCK, part * (D // BLOCK), D // BLOCK)
        if part == 0:
            big[...] = nt(dproj[:, cols], wqkv[:, cols])
        else:
            big[...] += nt(dproj[:, cols], wqkv[:, cols])

    loads["x"].wait()
    step, gain = rms_back(big[...], x_ref[...], g_ref[0:1, :])
    gain_ref[0:1, :] = gain
    dx_ref[...] += step
    for m, grad in enumerate((gqkv, gout, ggu, gd)):
        pltpu.make_async_copy(grad, grad, sem_out.at[m]).wait()
    if spares > 0:

        @pl.loop(0, spares)
        def _(i):
            pltpu.make_async_copy(zero, tiles_out[0].at[spare[i]], sem_zero).wait()


def weight_shapes():
    return [(r * BLOCK, c * BLOCK) for r, c in GRIDS]


VMEM = pl.BlockSpec(memory_space=pltpu.VMEM)
SMEM = pl.BlockSpec(memory_space=pltpu.SMEM)
HBM = pl.BlockSpec(memory_space=pl.ANY)


def like(struct):
    return pltpu.VMEM(struct.shape, struct.dtype)


def cost(flops, bytes_accessed):
    return pl.CostEstimate(flops=flops, bytes_accessed=bytes_accessed, transcendentals=0)


def forward_layer(slots, length, x, gains, cos, sin, gathered):
    rows = x.shape[0]
    key_rows = round_up(rows, BLOCK)
    S = jax.ShapeDtypeStruct
    saved = [
        S((rows, D), bf16),
        S((key_rows, D), bf16),
        S((key_rows, D), bf16),
        S((key_rows, D), bf16),
        S((key_rows, BLOCK), f32),
        S((rows, D), bf16),
        S((rows, D), f32),
        S((rows, D), bf16),
        S((rows, 2 * FF), bf16),
    ] + [S(s, bf16) for s in weight_shapes()]
    return pl.pallas_call(
        forward_kernel,
        out_shape=[S((rows, D), f32)] + saved,
        in_specs=[SMEM, SMEM, VMEM, VMEM, VMEM, VMEM, HBM],
        out_specs=[VMEM] + [HBM] * 13,
        scratch_shapes=[like(s) for s in saved]
        + [
            pltpu.VMEM((rows, key_rows), f32),
            pltpu.SemaphoreType.DMA((4,)),
            pltpu.SemaphoreType.DMA((13,)),
        ],
        compiler_params=pltpu.CompilerParams(vmem_limit_bytes=VMEM_BYTES),
        cost_estimate=cost(2 * rows * PER_LAYER * BLOCK * BLOCK, 40 * 2**20),
        name="forward_block",
    )(slots, length, x, gains, cos, sin, gathered)


def tile_arrays(zones):
    return [jax.ShapeDtypeStruct((size, BLOCK, BLOCK), bf16) for _, _, size in zones]


def backward_layer(places, spare, length, back, gains, cos, sin, saved, zones, begun):
    rows = back.shape[0]
    key_rows = round_up(rows, BLOCK)
    S = jax.ShapeDtypeStruct
    args = (places, spare, length, back, gains, cos, sin) + tuple(saved)
    late = 2 + len(zones) - len(begun)
    return pl.pallas_call(
        functools.partial(backward_kernel, len(begun), zones),
        out_shape=[S((rows, D), f32), S((2, D), f32)] + tile_arrays(zones),
        in_specs=[SMEM] * 3 + [VMEM] * 4 + [HBM] * (14 + len(begun)),
        out_specs=[VMEM, VMEM] + [HBM] * len(zones),
        input_output_aliases={len(args) + i: late + i for i in range(len(begun))},
        scratch_shapes=[like(s) for s in saved]
        + [pltpu.VMEM(s, bf16) for s in weight_shapes()]
        + [
            pltpu.VMEM((D, rows), bf16),
            pltpu.VMEM((key_rows, key_rows), f32),
            pltpu.VMEM((HEADS, 1, key_rows), f32),
            pltpu.VMEM((3, key_rows, PAIR), f32),
            pltpu.VMEM((rows, D), f32),
            pltpu.VMEM((key_rows, D), bf16),
            pltpu.VMEM((rows, 3 * D), bf16),
            pltpu.VMEM((BLOCK, BLOCK), bf16),
            pltpu.SemaphoreType.DMA((11,)),
            pltpu.SemaphoreType.DMA((FF // FF_STEP, 5)),
            pltpu.SemaphoreType.DMA((4,)),
            pltpu.SemaphoreType.DMA,
        ],
        compiler_params=pltpu.CompilerParams(vmem_limit_bytes=VMEM_BYTES),
        cost_estimate=cost(4 * rows * PER_LAYER * BLOCK * BLOCK + 20 * rows * rows * D, 60 * 2**20),
        name="backward_block",
    )(*args, *begun)


def optimizer_kernel(factor, rank, g_ref, m_ref, s_ref, r_ref, wg_ref, ns_ref, nm_ref, nc_ref):
    f = factor[0]
    count = m_ref.shape[0]
    for i in range(count):
        gb = g_ref[rank[pl.program_id(0) * count + i]]
        wg_ref[i] = gb.astype(f32) * f
        half = (1.0 - decay_rate) * f * f
        ns_ref[i, 0] = decay_rate * s_ref[i, 0] + half * nt(gb, gb)
        ns_ref[i, 1] = decay_rate * s_ref[i, 1] + half * tn(gb, gb)
        left = nn(r_ref[i, 0].astype(bf16), (gb.astype(f32) * f).astype(bf16)).astype(bf16)
        new = m_ref[i] - step_rate * nn(left, r_ref[i, 1].astype(bf16))
        nm_ref[i] = new
        nc_ref[i] = new.astype(bf16)


def optimizer(factor, rank, owned, master, statistics, inverse_roots):
    count = owned.shape[0]
    per = max(n for n in range(1, 19) if count % n == 0)
    S = jax.ShapeDtypeStruct
    one = pl.BlockSpec((per, BLOCK, BLOCK), lambda i: (i, 0, 0))
    two = pl.BlockSpec((per, 2, BLOCK, BLOCK), lambda i: (i, 0, 0, 0))
    return pl.pallas_call(
        optimizer_kernel,
        grid=(count // per,),
        out_shape=[
            S(master.shape, f32),
            S(statistics.shape, f32),
            S(master.shape, f32),
            S(master.shape, bf16),
        ],
        in_specs=[SMEM, SMEM, VMEM, one, two, two],
        out_specs=[one, two, one, one],
        compiler_params=pltpu.CompilerParams(vmem_limit_bytes=VMEM_BYTES),
        name="optimizer",
    )(factor, rank, owned, master, statistics, inverse_roots)


def to_images(local, bands, band):
    images, band_rows = local.shape[0], local.shape[-2]
    padded = jnp.concatenate([local, jnp.zeros((bands - images,) + local.shape[1:], local.dtype)], 0)
    whole = jnp.zeros((bands,) + local.shape[1:], local.dtype)
    for shift in range(bands):
        block = lax.dynamic_index_in_dim(padded, (band + shift) % bands, 0, keepdims=False)
        if shift > 0:
            pairs = [(b, (b + shift) % bands) for b in range(bands) if (b + shift) % bands < images]
            block = lax.ppermute(block, "band", pairs)
        whole = lax.dynamic_update_index_in_dim(whole, block, (band - shift) % bands, 0)
    return whole


def send_to_bands(whole, images, bands, band):
    blocks = []
    for shift in range(bands):
        block = lax.dynamic_index_in_dim(whole, (band + shift) % bands, 0, keepdims=False)
        if shift > 0:
            pairs = [(b, (b + shift) % bands) for b in range(images)]
            block = lax.ppermute(block, "band", pairs)
        blocks.append(block)
    return tuple(blocks)


def at_bands(blocks, images, bands, band):
    local = jnp.zeros((bands,) + blocks[0].shape, blocks[0].dtype)
    for shift, block in enumerate(blocks):
        local = lax.dynamic_update_index_in_dim(local, block, (band - shift) % bands, 0)
    return local[:images]


EARLY = (36,)
LATE = (24, 28, 20)
LEAST = (PER_LAYER,)


def chunk_places(slot_of_block, per_owner, me):
    blocks = slot_of_block.shape[0]
    block_of_slot = jnp.zeros((blocks,), jnp.int32).at[slot_of_block].set(
        jnp.arange(blocks, dtype=jnp.int32)
    )
    by_owner = block_of_slot.reshape(-1, per_owner)
    rank = jnp.sum(by_owner[:, None, :] > by_owner[:, :, None], -1, dtype=jnp.int32)
    owner = jnp.arange(by_owner.shape[0], dtype=jnp.int32)
    relative = (owner ^ me)[:, None]
    owner = owner[:, None]
    core, x, y = relative % 2, relative // 2 % 2, relative // 4
    place = jnp.zeros_like(rank)
    clean = jnp.bool_(True)
    start = 0
    for size, least in zip(EARLY, LEAST):
        at = rank - start
        here = (at >= 0) & (at < size)
        place = jnp.where(here, 8 * start + owner * size + at, place)
        clean = clean & jnp.all(jnp.where(here, by_owner >= least, True))
        start += size
    for size in LATE:
        half = size // 2
        at = rank - start
        here = (at >= 0) & (at < size)
        spot = jnp.where(at < half, (x * 2 + y) * half + at, 4 * half + (y * 2 + x) * half + at - half)
        place = jnp.where(here, 8 * start + core * 4 * size + spot, place)
        start += size
    return place.reshape(-1)[slot_of_block], rank, clean


CORE = [(i, i ^ 1) for i in range(8)]
ALONG_X = [(i, i ^ 2) for i in range(8)]
ALONG_Y = [(i, i ^ 4) for i in range(8)]


def wide(t, lo, hi):
    return t[lo:hi].astype(f32)


class Bands:
    def to_meet(self, plane):
        self.plane = plane
        return (plane,)

    def go_meet(self, plane):
        return lax.ppermute(plane, "band", [(0, 1)]), lax.ppermute(plane, "band", [(2, 1)])

    def to_part(self, up, down):
        self.total = (self.plane.astype(f32) + up.astype(f32) + down.astype(f32)).astype(bf16)
        return (self.total,)

    def go_part(self, total):
        return lax.ppermute(total, "band", [(1, 0)]), lax.ppermute(total, "band", [(1, 2)])

    def to_last(self, to_first, to_third):
        self.to_first, self.to_third = to_first, to_third
        return (to_third,)

    def go_last(self, to_third):
        return (lax.ppermute(to_third, "band", [(2, 3)]),)

    def to_end(self, to_last):
        band = lax.axis_index("band")
        total = jnp.where(band == 0, self.to_first, self.total)
        total = jnp.where(band == 2, self.to_third, total)
        self.total = jnp.where(band == 3, to_last, total)
        return (self.total,)

    def go_end(self, total):
        return ()


class Chunk(Bands):
    def __init__(self, kept, sent):
        self.half = kept.shape[0] // 8
        self.kept, self.sent = kept, sent

    def chip(self, lo, hi):
        lo, hi = lo * self.half, hi * self.half
        return wide(self.kept, lo, hi) + wide(self.received, lo, hi)

    def to_core(self):
        return (self.sent,)

    def go_core(self, send):
        return (lax.ppermute(send, "dp", CORE),)

    def to_plane(self, received):
        self.received = received
        return self.chip(2, 4).astype(bf16), self.chip(6, 8).astype(bf16)

    def go_plane(self, send_x, send_y):
        return lax.ppermute(send_x, "dp", ALONG_X), lax.ppermute(send_y, "dp", ALONG_Y)

    go_turn = go_plane

    def to_turn(self, from_x, from_y):
        self.from_x, self.from_y = from_x, from_y
        half = self.half
        send_y = (self.chip(1, 2) + wide(from_x, half, 2 * half)).astype(bf16)
        send_x = (self.chip(5, 6) + wide(from_y, half, 2 * half)).astype(bf16)
        return send_x, send_y

    def to_meet(self, from_x, from_y):
        half = self.half
        one = self.chip(0, 1) + wide(self.from_x, 0, half) + wide(from_y, 0, half)
        two = self.chip(4, 5) + wide(self.from_y, 0, half) + wide(from_x, 0, half)
        self.plane = jnp.concatenate([one, two], 0).astype(bf16)
        return (self.plane,)


class Sequence:
    def __init__(self):
        self.before = ()
        self.arrived = {}

    def round(self, *steps):
        arrived = [tuple(self.arrived.get(chunk, ())) for chunk, _ in steps]
        flat = sum(arrived, ())
        flat = lax.optimization_barrier(flat + self.before)
        at, self.before = 0, ()
        for (chunk, name), had in zip(steps, arrived):
            sends = getattr(chunk, "to_" + name)(*flat[at : at + len(had)])
            at += len(had)
            self.arrived[chunk] = getattr(chunk, "go_" + name)(*sends)
            self.before = self.before + tuple(sends)

    def wait_for(self, *arrays):
        arrays = lax.optimization_barrier(arrays + self.before)[: len(arrays)]
        self.before = self.before + arrays
        return arrays


def rope_tables(rows):
    half = HEAD_DIM // 2
    frequency = rope_base ** (-(jnp.arange(half, dtype=f32) * 2.0 / HEAD_DIM))
    angles = jnp.arange(rows, dtype=jnp.int32).astype(f32)[:, None] * frequency[None, :]
    cosine, sine = jnp.cos(angles), jnp.sin(angles)
    return jnp.tile(cosine, (1, 4)), jnp.tile(jnp.concatenate([-sine, sine], 1), (1, 2))


def shards(
    tokens,
    cotangent,
    lengths,
    slot_of_block,
    master,
    statistics,
    inverse_roots,
    gain_values,
    gain_moments,
):
    images, band_rows, _ = tokens.shape
    band = lax.axis_index("band")
    bands = lax.axis_size("band")
    seq = band_rows * bands
    rows = round_up(seq, 16)
    gathered = lax.all_gather(master.astype(bf16), "dp", axis=0, tiled=True)
    slot_count = gathered.shape[0]

    arrived = to_images(jnp.stack([tokens, cotangent], 1), bands, band)
    token_rows = jnp.pad(arrived[:, 0].reshape(seq, D), ((0, rows - seq), (0, 0)))
    back_rows = jnp.pad(arrived[:, 1].reshape(seq, D), ((0, rows - seq), (0, 0)))
    length = lengths[jnp.minimum(band, images - 1)]
    valid = (jnp.arange(rows, dtype=jnp.int32) < length).astype(f32)
    length = length.reshape(1)
    cos, sin = rope_tables(rows)

    spare_count = slot_count - slot_of_block.shape[0]
    spare = jnp.zeros((1,), jnp.int32)
    if spare_count > 0:
        used = jnp.zeros((slot_count,), jnp.int32).at[slot_of_block].set(1)
        spare = jnp.concatenate([jnp.argsort(used)[:spare_count].astype(jnp.int32), spare])

    hidden = token_rows.astype(f32)
    inputs, saves = [], []
    for layer in range(LAYERS):
        slots = slot_of_block[layer * PER_LAYER : (layer + 1) * PER_LAYER]
        gains = gain_values[2 * layer : 2 * layer + 2]
        inputs.append(hidden)
        hidden, *saved = forward_layer(slots, length, hidden, gains, cos, sin, gathered)
        saves.append(saved)

    def send_rows(t):
        return send_to_bands(t[:seq].astype(bf16).reshape(bands, band_rows, D), images, bands, band)

    output_blocks = send_rows(hidden)

    back = back_rows.astype(f32) * valid[:, None]
    per_owner = master.shape[0]
    me = lax.axis_index("dp")
    by_permutes = (
        lax.axis_size("dp") == 8
        and bands == 4
        and images == 3
        and slot_count == slot_of_block.shape[0]
        and per_owner == sum(EARLY) + sum(LATE)
    )
    if by_permutes:
        places, ranks, clean = chunk_places(slot_of_block, per_owner, me)
        rank = lax.dynamic_index_in_dim(ranks, me, 0, keepdims=False)
        ends = [8 * sum(EARLY[: i + 1]) for i in range(len(EARLY))]
        bounds = [0] + ends
        for size in LATE:
            bounds += [bounds[-1] + 4 * size, bounds[-1] + 8 * size]
        zones = tuple((low, high, high - low) for low, high in zip(bounds, bounds[1:]))
    else:
        places, rank = slot_of_block, jnp.arange(per_owner, dtype=jnp.int32)
        zones = ((0, slot_count, slot_count),)

    def backward(layer, back, tiles, zones):
        fill = spare if layer == LAYERS - 1 else spare[-1:]
        back, gains, *tiles = backward_layer(
            places[layer * PER_LAYER : (layer + 1) * PER_LAYER], fill, length, back,
            gain_values[2 * layer : 2 * layer + 2], cos, sin, (inputs[layer], *saves[layer]), zones, tiles,
        )
        return back, gains, tiles

    if by_permutes:
        back, gains_top, tiles = backward(1, back, [], zones)
        early = tiles[:1]
        ready, *output_blocks = lax.optimization_barrier((tiles[0], *output_blocks))
        early_sums = [lax.psum_scatter(ready, "dp", scatter_dimension=0, tiled=True)]
        back, gains_bottom, tiles = backward(0, back, tiles[1:], zones)
        missed, *late = tiles
        gains = jnp.concatenate([gains_bottom, gains_top], 0).astype(bf16).reshape(-1, BLOCK)
        gains = jnp.pad(gains, ((0, BLOCK - gains.shape[0]), (0, 0)))[None]
        sequence = Sequence()
        chunks = [Chunk(*late[2 * i : 2 * i + 2]) for i in range(len(LATE))]
        one, two, three = chunks
        top = Bands()
        sequence.arrived[top] = (jnp.concatenate([early_sums[0], gains], 0),)
        sequence.round((one, "core"), (two, "core"), (three, "core"))
        sequence.round((one, "plane"))
        sequence.round((top, "meet"))
        sequence.round((one, "turn"))
        sequence.round((two, "plane"))
        sequence.round((one, "meet"))
        sequence.round((top, "part"))
        sequence.round((two, "turn"))
        sequence.round((three, "plane"))
        sequence.round((one, "part"))
        sequence.round((two, "meet"))
        sequence.round((top, "last"))
        sequence.round((three, "turn"))
        sequence.round((three, "meet"))
        sequence.round((two, "part"), (top, "end"))
        sequence.round((one, "last"))
        sequence.round((three, "part"))
        sequence.round((two, "last"))
        sequence.round((three, "last"))
        sequence.round((one, "end"))
        sequence.round((two, "end"))
        sequence.round((three, "end"))
        early_total = top.total[:-1]

        def again(trip, total):
            _, spare_tiles, *parts = lax.optimization_barrier((trip, missed, *early))
            block_at = jnp.argsort(places)
            sums, start = [], 0
            for part, end, least in zip(parts, ends, LEAST):
                late_here = (block_at[start:end] < least)[:, None, None]
                whole = jnp.where(late_here, spare_tiles[start:end], part)
                sums.append(lax.psum_scatter(whole, "dp", scatter_dimension=0, tiled=True))
                start = end
            return lax.psum(jnp.concatenate(sums, 0), "band")

        early_total = lax.fori_loop(0, jnp.where(clean, 0, 1), again, early_total)
        owned = jnp.concatenate([early_total] + [chunk.total for chunk in chunks], 0)
        gain_total = top.total[-1].astype(f32)[: gain_values.size // BLOCK].reshape(-1, D)
    else:
        back, gains_top, tiles = backward(1, back, [], zones)
        back, gains_bottom, tiles = backward(0, back, tiles, zones)
        owned = lax.psum_scatter(tiles[0], "dp", scatter_dimension=0, tiled=True)
        owned = lax.psum(owned, "band")
        gain_total = lax.psum(jnp.concatenate([gains_bottom, gains_top], 0), ("dp", "band"))

    layer_output = at_bands(output_blocks, images, bands, band)
    owned_f = owned.astype(f32)
    owned_squares = jnp.sum(owned_f * owned_f)
    if by_permutes:
        last = jnp.concatenate([gain_total.reshape(-1, BLOCK), jnp.broadcast_to(owned_squares, (1, BLOCK))], 0)
        for pairs in (CORE, ALONG_X, ALONG_Y):
            last = last + lax.ppermute(last, "dp", pairs)
        gain_total, owned_squares = last[:-1].reshape(gain_values.shape), last[-1, 0]
    else:
        owned_squares = lax.psum(owned_squares, "dp")
    grad_norm = jnp.sqrt(owned_squares + jnp.sum(gain_total * gain_total))
    factor = jnp.minimum(1.0, clip_limit / grad_norm)
    back, factor = lax.optimization_barrier((back, factor))
    input_grad = at_bands(send_rows(back), images, bands, band)
    weight_grads, new_statistics, new_master, master_copy = optimizer(
        factor.reshape(1), rank, owned, master, statistics, inverse_roots
    )
    gain_grads = gain_total * factor
    new_moments = decay_rate * gain_moments + (1.0 - decay_rate) * gain_grads * gain_grads
    new_gains = gain_values - gain_rate * gain_grads / (jnp.sqrt(new_moments) + epsilon)
    return (
        layer_output,
        input_grad,
        weight_grads,
        grad_norm,
        new_statistics,
        new_master,
        master_copy,
        gain_grads,
        new_moments,
        new_gains,
    )


def solution(mesh):
    return jax.shard_map(
        shards,
        mesh=mesh,
        in_specs=(
            P("dp", "band", None),
            P("dp", "band", None),
            P("dp"),
            P(),
            P("dp", None, None),
            P("dp", None, None, None),
            P("dp", None, None, None),
            P(),
            P(),
        ),
        out_specs=(
            P("dp", "band", None),
            P("dp", "band", None),
            P("dp", None, None),
            P(),
            P("dp", None, None, None),
            P("dp", None, None),
            P("dp", None, None),
            P(),
            P(),
            P(),
        ),
        check_vma=False,
    )
```

```python
import functools

import jax
import jax.numpy as jnp
from jax import lax
from jax.experimental import pallas as pl
from jax.experimental.pallas import tpu as pltpu
from jax.sharding import PartitionSpec as P

D = 768
HEADS = 12
HEAD_DIM = 64
FF = 2048
LAYERS = 2
BLOCK = 128
PAIR = 2 * HEAD_DIM

epsilon = 1e-05
rope_base = 10000.0
decay_rate = 0.5
step_rate = 0.4
gain_rate = 0.2
clip_limit = 1.0
masked_score = -1e30
VMEM_BYTES = 62 * 2**20

f32 = jnp.float32
bf16 = jnp.bfloat16

GRIDS = [
    (D // BLOCK, 3 * D // BLOCK),
    (D // BLOCK, D // BLOCK),
    (D // BLOCK, 2 * FF // BLOCK),
    (FF // BLOCK, D // BLOCK),
]
COUNTS = [r * c for r, c in GRIDS]
OFFSETS = [sum(COUNTS[:i]) for i in range(4)]
PER_LAYER = sum(COUNTS)
FF_STEP = 512
TOGETHER = 4


def round_up(n, m):
    return -(-n // m) * m


def nn(a, b):
    return lax.dot_general(a, b, (((1,), (0,)), ((), ())), preferred_element_type=f32)


def nt(a, b):
    return lax.dot_general(a, b, (((1,), (1,)), ((), ())), preferred_element_type=f32)


def tn(a, b):
    return lax.dot_general(a, b, (((0,), (0,)), ((), ())), preferred_element_type=f32)


def query_blocks(rows, step=256):
    return [(s, min(s + step, rows)) for s in range(0, rows, step)]


def swap_halves(t):
    lane = lax.broadcasted_iota(jnp.int32, t.shape, 1)
    half = HEAD_DIM // 2
    return jnp.where(lane % HEAD_DIM < half, pltpu.roll(t, PAIR - half, 1), pltpu.roll(t, half, 1))


def rms(m):
    return lax.rsqrt(jnp.mean(m * m, -1, keepdims=True) + epsilon)


def rms_back(u, m, g):
    r = rms(m)
    t = u * g
    dot = jnp.mean(t * m, -1, keepdims=True)
    return r * t - m * (r * r * r * dot), jnp.sum(u * m * r, 0, keepdims=True)


def copies(pairs, sem):
    return [pltpu.make_async_copy(src, dst, sem.at[i]) for i, (src, dst) in enumerate(pairs)]


def forward_kernel(
    slots, length, x_ref, g_ref, cos_ref, sin_ref, w_hbm,
    xn_ref, normed_o, q_o, k_o, v_o, st_o, mixed_o, mid_o, n2_o, gu_o, wqkv_o, wout_o, wgu_o, wd_o,
    normed_ref, q_ref, k_ref, v_ref, st_ref, mixed_ref, mid_ref, n2_ref, gu_ref,
    wqkv, wout, wgu, wd, bias, sem_in, sem_out,
):
    rows = x_ref.shape[0]
    key_rows = q_ref.shape[0]
    held = (wqkv, wout, wgu, wd)
    for m in range(4):
        tile_rows, tile_cols = GRIDS[m]

        @pl.loop(0, tile_rows)
        def _(i, m=m, tile_cols=tile_cols):
            for j in range(tile_cols):
                slot = slots[OFFSETS[m] + i * tile_cols + j]
                pltpu.make_async_copy(
                    w_hbm.at[slot],
                    held[m].at[pl.ds(pl.multiple_of(i * BLOCK, BLOCK), BLOCK), pl.ds(j * BLOCK, BLOCK)],
                    sem_in.at[m],
                ).start()

    def arrive(m):
        pltpu.make_async_copy(held[m], held[m], sem_in.at[m]).wait()

    saves = copies(
        [
            (normed_ref, normed_o), (q_ref, q_o), (k_ref, k_o), (v_ref, v_o), (st_ref, st_o),
            (mixed_ref, mixed_o), (mid_ref, mid_o), (n2_ref, n2_o), (gu_ref, gu_o),
            (wqkv, wqkv_o), (wout, wout_o), (wgu, wgu_o), (wd, wd_o),
        ],
        sem_out,
    )
    query = lax.broadcasted_iota(jnp.int32, bias.shape, 0)
    key = lax.broadcasted_iota(jnp.int32, bias.shape, 1)
    bias[...] = jnp.where((key <= query) & (key < length[0]), 0.0, masked_score)
    x = x_ref[...]
    normed_ref[...] = (x * rms(x) * g_ref[0:1, :]).astype(bf16)
    saves[0].start()
    tail = key_rows - rows
    for ref in (q_ref, k_ref, v_ref):
        ref[rows:, :] = jnp.zeros((tail, D), bf16)
    arrive(0)
    saves[9].start()

    @pl.loop(0, 2)
    def _(part):
        acc = nn(normed_ref[...], wqkv[:, pl.ds(pl.multiple_of(part * D, D), D)])
        scale = jnp.where(part == 0, HEAD_DIM ** (-0.5), 1.0)
        for p in range(HEADS // 2):
            t = acc[:, p * PAIR : (p + 1) * PAIR]
            rot = ((t * cos_ref[...] + swap_halves(t) * sin_ref[...]) * scale).astype(bf16)

            @pl.when(part == 0)
            def _(p=p, rot=rot):
                q_ref[0:rows, p * PAIR : (p + 1) * PAIR] = rot

            @pl.when(part == 1)
            def _(p=p, rot=rot):
                k_ref[0:rows, p * PAIR : (p + 1) * PAIR] = rot

    v_ref[0:rows, :] = nn(normed_ref[...], wqkv[:, 2 * D :]).astype(bf16)
    for i in (1, 2, 3):
        saves[i].start()
    st_ref[...] = jnp.zeros(st_ref.shape, f32)

    @pl.loop(0, HEADS // TOGETHER)
    def _(g):
        width = TOGETHER * HEAD_DIM
        cols = pl.ds(pl.multiple_of(g * width, width), width)
        for q0, q1 in query_blocks(rows):
            count = q1 - q0
            kend = min(round_up(q1, BLOCK), key_rows)
            qp = q_ref[q0:q1, cols]
            head = lax.broadcasted_iota(jnp.int32, qp.shape, 1) // HEAD_DIM
            stacked = jnp.concatenate([jnp.where(head == h, qp, 0) for h in range(TOGETHER)], 0)
            s = nt(stacked, k_ref[:kend, cols]).reshape(TOGETHER, count, kend) + bias[q0:q1, :kend][None]
            top = jnp.max(s, -1, keepdims=True)
            e = jnp.exp(s - top)
            total = jnp.sum(e, -1, keepdims=True)
            out = nn(e.astype(bf16).reshape(TOGETHER * count, kend), v_ref[:kend, cols])
            out = out.reshape(TOGETHER, count, width) / total
            level = top + jnp.log(total)
            mixed = out[0]
            lane = lax.broadcasted_iota(jnp.int32, (count, BLOCK), 1)
            levels = st_ref[q0:q1, :]
            for h in range(TOGETHER):
                mixed = jnp.where(head == h, out[h], mixed)
                levels = jnp.where(lane == g * TOGETHER + h, level[h], levels)
            mixed_ref[q0:q1, cols] = mixed.astype(bf16)
            st_ref[q0:q1, :] = levels

    saves[4].start()
    saves[5].start()
    arrive(1)
    saves[10].start()
    middle = x_ref[...] + nn(mixed_ref[...], wout[...])
    mid_ref[...] = middle
    saves[6].start()
    n2_ref[...] = (middle * rms(middle) * g_ref[1:2, :]).astype(bf16)
    saves[7].start()
    arrive(2)
    saves[11].start()
    arrive(3)
    saves[12].start()
    xn_ref[...] = mid_ref[...]

    @pl.loop(0, FF // FF_STEP)
    def _(t):
        at = pl.multiple_of(t * FF_STEP, FF_STEP)
        gate = nn(n2_ref[...], wgu[:, pl.ds(at, FF_STEP)])
        up = nn(n2_ref[...], wgu[:, pl.ds(FF + at, FF_STEP)])
        act = (gate / (1.0 + jnp.exp(-gate)) * up).astype(bf16)
        gu_ref[:, pl.ds(at, FF_STEP)] = gate.astype(bf16)
        gu_ref[:, pl.ds(FF + at, FF_STEP)] = up.astype(bf16)
        xn_ref[...] += nn(act, wd[pl.ds(at, FF_STEP), :])

    saves[8].start()
    for save in saves:
        save.wait()


def put_tiles(places, zones, m, grad, outs, sem, i0, i1, j0, count_j):
    @pl.loop(i0, i1)
    def _(i):
        for jj in range(count_j):
            j = j0 + jj
            place = places[OFFSETS[m] + i * GRIDS[m][1] + j]
            tile = grad.at[
                pl.ds(pl.multiple_of(i * BLOCK, BLOCK), BLOCK),
                pl.ds(pl.multiple_of(j * BLOCK, BLOCK), BLOCK),
            ]
            if len(outs) == 1:
                pltpu.make_async_copy(tile, outs[0].at[place], sem).start()
                continue
            for out, (low, high, _) in zip(outs, zones):

                @pl.when((place >= low) & (place < high))
                def _(tile=tile, out=out, place=place, low=low):
                    pltpu.make_async_copy(tile, out.at[place - low], sem).start()


def backward_kernel(
    begun, zones, places, spare, length, back_ref, g_ref, cos_ref, sin_ref,
    x_i, normed_i, q_i, k_i, v_i, st_i, mixed_i, mid_i, n2_i, gu_i, wqkv_i, wout_i, wgu_i, wd_i, *rest
):
    dx_ref, gain_ref, *rest = rest[begun:]
    tiles_out, rest = rest[: len(zones)], rest[len(zones) :]
    (
        x_ref, normed_ref, q_ref, k_ref, v_ref, st_ref, mixed_ref, mid_ref, n2_ref, gu_ref,
        wqkv, wout, wgu, wd, gqkv, gout, ggu, gd,
        turned, bias, levels, sums, big, mixed_back, dproj, zero, sem_in, sem_ffn, sem_out, sem_zero,
    ) = rest
    rows = back_ref.shape[0]
    key_rows = q_ref.shape[0]
    loads = dict(
        zip(
            ("n2", "mid", "wout", "mixed", "q", "k", "v", "st", "normed", "wqkv", "x"),
            copies(
                [
                    (n2_i, n2_ref), (mid_i, mid_ref), (wout_i, wout), (mixed_i, mixed_ref), (q_i, q_ref), (k_i, k_ref), (v_i, v_ref),
                    (st_i, st_ref), (normed_i, normed_ref), (wqkv_i, wqkv), (x_i, x_ref),
                ],
                sem_in,
            ),
        )
    )

    def ffn_loads(t):
        here = pl.ds(pl.multiple_of(t * FF_STEP, FF_STEP), FF_STEP)
        there = pl.ds(pl.multiple_of(FF + t * FF_STEP, FF_STEP), FF_STEP)
        parts = [(wd_i.at[here, :], wd.at[here, :])]
        for cols in (here, there):
            parts += [(gu_i.at[:, cols], gu_ref.at[:, cols]), (wgu_i.at[:, cols], wgu.at[:, cols])]
        return [pltpu.make_async_copy(src, dst, sem_ffn.at[t, i]) for i, (src, dst) in enumerate(parts)]

    loads["n2"].start()
    for t in range(FF // FF_STEP):
        for load in ffn_loads(t):
            load.start()
    for name, load in loads.items():
        if name != "n2":
            load.start()
    put = functools.partial(put_tiles, places, zones)
    spares = spare.shape[0] - 1
    if spares > 0:
        zero[...] = jnp.zeros(zero.shape, bf16)

        @pl.loop(0, spares)
        def _(i):
            pltpu.make_async_copy(zero, tiles_out[0].at[spare[i]], sem_zero).start()

    key = lax.broadcasted_iota(jnp.int32, bias.shape, 0)
    query = lax.broadcasted_iota(jnp.int32, bias.shape, 1)
    bias[...] = jnp.where((key <= query) & (key < length[0]), 0.0, masked_score)
    big[...] = jnp.zeros(big.shape, f32)
    loads["n2"].wait()
    turned[...] = n2_ref[...].T

    @pl.loop(0, FF // FF_STEP)
    def _(t):
        for load in ffn_loads(t):
            load.wait()
        at = pl.multiple_of(t * FF_STEP, FF_STEP)
        here = pl.ds(at, FF_STEP)
        there = pl.ds(FF + at, FF_STEP)
        back_ffn = back_ref[...].astype(bf16)
        d_act = nt(back_ffn, wd[here, :])
        gate = gu_ref[:, here].astype(f32)
        up = gu_ref[:, there].astype(f32)
        sig = 1.0 / (1.0 + jnp.exp(-gate))
        silu = gate * sig
        act = (silu * up).astype(bf16)
        d_gate = (d_act * up * (sig * (1.0 + gate * (1.0 - sig)))).astype(bf16)
        d_up = (d_act * silu).astype(bf16)
        gd[here, :] = tn(act, back_ffn).astype(bf16)
        ggu[:, here] = nn(turned[...], d_gate).astype(bf16)
        ggu[:, there] = nn(turned[...], d_up).astype(bf16)
        per = FF_STEP // BLOCK
        put(3, gd, tiles_out, sem_out.at[3], t * per, (t + 1) * per, 0, D // BLOCK)
        put(2, ggu, tiles_out, sem_out.at[2], 0, D // BLOCK, t * per, per)
        put(2, ggu, tiles_out, sem_out.at[2], 0, D // BLOCK, FF // BLOCK + t * per, per)
        big[...] += nt(d_gate, wgu[:, here]) + nt(d_up, wgu[:, there])

    loads["mid"].wait()
    step, gain = rms_back(big[...], mid_ref[...], g_ref[1:2, :])
    gain_ref[1:2, :] = gain
    dx_ref[...] = back_ref[...] + step
    back_attn = dx_ref[...].astype(bf16)
    loads["wout"].wait()
    mixed_back[0:rows, :] = nt(back_attn, wout[...]).astype(bf16)
    mixed_back[rows:, :] = jnp.zeros((key_rows - rows, D), bf16)
    loads["mixed"].wait()
    gout[...] = tn(mixed_ref[...], back_attn).astype(bf16)
    put(1, gout, tiles_out, sem_out.at[1], 0, D // BLOCK, 0, D // BLOCK)
    for name in ("q", "k", "v", "st"):
        loads[name].wait()
    by_head = st_ref[...].T
    for h in range(HEADS):
        levels[h] = by_head[h : h + 1, :]

    @pl.loop(0, HEADS // 2)
    def _(p):
        cols = pl.ds(pl.multiple_of(p * PAIR, PAIR), PAIR)
        low = lax.broadcasted_iota(jnp.int32, (key_rows, PAIR), 1) < HEAD_DIM

        def stacked(t, n):
            return jnp.concatenate([jnp.where(low[:n], t[:n], 0), jnp.where(low[:n], 0, t[:n])], 0)

        def chosen(t, n):
            return jnp.where(low[:n], t[:n], t[n:])

        for q0, q1 in query_blocks(key_rows):
            kend, count = q1, q1 - q0
            keys, values = k_ref[:kend, cols], v_ref[:kend, cols]
            queries, backs = q_ref[q0:q1, cols], mixed_back[q0:q1, cols]
            level = jnp.stack([levels[2 * p + h, :, q0:q1] for h in range(2)], 0)
            scores = nt(stacked(keys, kend), queries).reshape(2, kend, count)
            soft = jnp.exp(scores + bias[:kend, q0:q1][None] - level)
            d_prob = nt(stacked(values, kend), backs).reshape(2, kend, count)
            row_dot = jnp.sum(soft * d_prob, 1, keepdims=True)
            d_score = (soft * (d_prob - row_dot)).astype(bf16)
            d_value = chosen(nn(soft.astype(bf16).reshape(2 * kend, count), backs), kend)
            d_key = chosen(nn(d_score.reshape(2 * kend, count), queries), kend)
            d_query = jnp.where(low[:count], tn(d_score[0], keys), tn(d_score[1], keys))
            sums[0, q0:q1, :] = d_query * HEAD_DIM ** (-0.5)
            if q0 > 0:
                sums[1, :q0, :] += d_key[:q0]
                sums[2, :q0, :] += d_value[:q0]
            sums[1, q0:kend, :] = d_key[q0:]
            sums[2, q0:kend, :] = d_value[q0:]
        for part in range(2):
            t = sums[part, 0:rows, :]
            dproj[:, pl.ds(pl.multiple_of(part * D + p * PAIR, PAIR), PAIR)] = (
                t * cos_ref[...] - swap_halves(t) * sin_ref[...]
            ).astype(bf16)
        dproj[:, pl.ds(pl.multiple_of(2 * D + p * PAIR, PAIR), PAIR)] = sums[2, 0:rows, :].astype(bf16)

    loads["normed"].wait()
    turned[...] = normed_ref[...].T
    loads["wqkv"].wait()
    for part in range(3):
        cols = slice(part * D, (part + 1) * D)
        gqkv[:, cols] = nn(turned[...], dproj[:, cols]).astype(bf16)
        put(0, gqkv, tiles_out, sem_out.at[0], 0, D // BLOCK, part * (D // BLOCK), D // BLOCK)
        if part == 0:
            big[...] = nt(dproj[:, cols], wqkv[:, cols])
        else:
            big[...] += nt(dproj[:, cols], wqkv[:, cols])

    loads["x"].wait()
    step, gain = rms_back(big[...], x_ref[...], g_ref[0:1, :])
    gain_ref[0:1, :] = gain
    dx_ref[...] += step
    for m, grad in enumerate((gqkv, gout, ggu, gd)):
        pltpu.make_async_copy(grad, grad, sem_out.at[m]).wait()
    if spares > 0:

        @pl.loop(0, spares)
        def _(i):
            pltpu.make_async_copy(zero, tiles_out[0].at[spare[i]], sem_zero).wait()


def weight_shapes():
    return [(r * BLOCK, c * BLOCK) for r, c in GRIDS]


VMEM = pl.BlockSpec(memory_space=pltpu.VMEM)
SMEM = pl.BlockSpec(memory_space=pltpu.SMEM)
HBM = pl.BlockSpec(memory_space=pl.ANY)


def like(struct):
    return pltpu.VMEM(struct.shape, struct.dtype)


def cost(flops, bytes_accessed):
    return pl.CostEstimate(flops=flops, bytes_accessed=bytes_accessed, transcendentals=0)


def forward_layer(slots, length, x, gains, cos, sin, gathered):
    rows = x.shape[0]
    key_rows = round_up(rows, BLOCK)
    S = jax.ShapeDtypeStruct
    saved = [
        S((rows, D), bf16),
        S((key_rows, D), bf16),
        S((key_rows, D), bf16),
        S((key_rows, D), bf16),
        S((key_rows, BLOCK), f32),
        S((rows, D), bf16),
        S((rows, D), f32),
        S((rows, D), bf16),
        S((rows, 2 * FF), bf16),
    ] + [S(s, bf16) for s in weight_shapes()]
    return pl.pallas_call(
        forward_kernel,
        out_shape=[S((rows, D), f32)] + saved,
        in_specs=[SMEM, SMEM, VMEM, VMEM, VMEM, VMEM, HBM],
        out_specs=[VMEM] + [HBM] * 13,
        scratch_shapes=[like(s) for s in saved]
        + [
            pltpu.VMEM((rows, key_rows), f32),
            pltpu.SemaphoreType.DMA((4,)),
            pltpu.SemaphoreType.DMA((13,)),
        ],
        compiler_params=pltpu.CompilerParams(vmem_limit_bytes=VMEM_BYTES),
        cost_estimate=cost(2 * rows * PER_LAYER * BLOCK * BLOCK, 40 * 2**20),
        name="forward_block",
    )(slots, length, x, gains, cos, sin, gathered)


def tile_arrays(zones):
    return [jax.ShapeDtypeStruct((size, BLOCK, BLOCK), bf16) for _, _, size in zones]


def backward_layer(places, spare, length, back, gains, cos, sin, saved, zones, begun):
    rows = back.shape[0]
    key_rows = round_up(rows, BLOCK)
    S = jax.ShapeDtypeStruct
    args = (places, spare, length, back, gains, cos, sin) + tuple(saved)
    late = 2 + len(zones) - len(begun)
    return pl.pallas_call(
        functools.partial(backward_kernel, len(begun), zones),
        out_shape=[S((rows, D), f32), S((2, D), f32)] + tile_arrays(zones),
        in_specs=[SMEM] * 3 + [VMEM] * 4 + [HBM] * (14 + len(begun)),
        out_specs=[VMEM, VMEM] + [HBM] * len(zones),
        input_output_aliases={len(args) + i: late + i for i in range(len(begun))},
        scratch_shapes=[like(s) for s in saved]
        + [pltpu.VMEM(s, bf16) for s in weight_shapes()]
        + [
            pltpu.VMEM((D, rows), bf16),
            pltpu.VMEM((key_rows, key_rows), f32),
            pltpu.VMEM((HEADS, 1, key_rows), f32),
            pltpu.VMEM((3, key_rows, PAIR), f32),
            pltpu.VMEM((rows, D), f32),
            pltpu.VMEM((key_rows, D), bf16),
            pltpu.VMEM((rows, 3 * D), bf16),
            pltpu.VMEM((BLOCK, BLOCK), bf16),
            pltpu.SemaphoreType.DMA((11,)),
            pltpu.SemaphoreType.DMA((FF // FF_STEP, 5)),
            pltpu.SemaphoreType.DMA((4,)),
            pltpu.SemaphoreType.DMA,
        ],
        compiler_params=pltpu.CompilerParams(vmem_limit_bytes=VMEM_BYTES),
        cost_estimate=cost(4 * rows * PER_LAYER * BLOCK * BLOCK + 20 * rows * rows * D, 60 * 2**20),
        name="backward_block",
    )(*args, *begun)


def optimizer_kernel(factor, rank, g_ref, m_ref, s_ref, r_ref, wg_ref, ns_ref, nm_ref, nc_ref):
    f = factor[0]
    count = m_ref.shape[0]
    for i in range(count):
        gb = g_ref[rank[pl.program_id(0) * count + i]]
        wg_ref[i] = gb.astype(f32) * f
        half = (1.0 - decay_rate) * f * f
        ns_ref[i, 0] = decay_rate * s_ref[i, 0] + half * nt(gb, gb)
        ns_ref[i, 1] = decay_rate * s_ref[i, 1] + half * tn(gb, gb)
        left = nn(r_ref[i, 0].astype(bf16), (gb.astype(f32) * f).astype(bf16)).astype(bf16)
        new = m_ref[i] - step_rate * nn(left, r_ref[i, 1].astype(bf16))
        nm_ref[i] = new
        nc_ref[i] = new.astype(bf16)


def optimizer(factor, rank, owned, master, statistics, inverse_roots):
    count = owned.shape[0]
    per = max(n for n in range(1, 19) if count % n == 0)
    S = jax.ShapeDtypeStruct
    one = pl.BlockSpec((per, BLOCK, BLOCK), lambda i: (i, 0, 0))
    two = pl.BlockSpec((per, 2, BLOCK, BLOCK), lambda i: (i, 0, 0, 0))
    return pl.pallas_call(
        optimizer_kernel,
        grid=(count // per,),
        out_shape=[
            S(master.shape, f32),
            S(statistics.shape, f32),
            S(master.shape, f32),
            S(master.shape, bf16),
        ],
        in_specs=[SMEM, SMEM, VMEM, one, two, two],
        out_specs=[one, two, one, one],
        compiler_params=pltpu.CompilerParams(vmem_limit_bytes=VMEM_BYTES),
        name="optimizer",
    )(factor, rank, owned, master, statistics, inverse_roots)


def to_images(local, bands, band):
    images, band_rows = local.shape[0], local.shape[-2]
    padded = jnp.concatenate([local, jnp.zeros((bands - images,) + local.shape[1:], local.dtype)], 0)
    whole = jnp.zeros((bands,) + local.shape[1:], local.dtype)
    for shift in range(bands):
        block = lax.dynamic_index_in_dim(padded, (band + shift) % bands, 0, keepdims=False)
        if shift > 0:
            pairs = [(b, (b + shift) % bands) for b in range(bands) if (b + shift) % bands < images]
            block = lax.ppermute(block, "band", pairs)
        whole = lax.dynamic_update_index_in_dim(whole, block, (band - shift) % bands, 0)
    return whole


def send_to_bands(whole, images, bands, band):
    blocks = []
    for shift in range(bands):
        block = lax.dynamic_index_in_dim(whole, (band + shift) % bands, 0, keepdims=False)
        if shift > 0:
            pairs = [(b, (b + shift) % bands) for b in range(images)]
            block = lax.ppermute(block, "band", pairs)
        blocks.append(block)
    return tuple(blocks)


def at_bands(blocks, images, bands, band):
    local = jnp.zeros((bands,) + blocks[0].shape, blocks[0].dtype)
    for shift, block in enumerate(blocks):
        local = lax.dynamic_update_index_in_dim(local, block, (band - shift) % bands, 0)
    return local[:images]


EARLY = (36,)
LATE = (24, 28, 20)
LEAST = (PER_LAYER,)


def chunk_places(slot_of_block, per_owner, me):
    blocks = slot_of_block.shape[0]
    block_of_slot = jnp.zeros((blocks,), jnp.int32).at[slot_of_block].set(
        jnp.arange(blocks, dtype=jnp.int32)
    )
    by_owner = block_of_slot.reshape(-1, per_owner)
    rank = jnp.sum(by_owner[:, None, :] > by_owner[:, :, None], -1, dtype=jnp.int32)
    owner = jnp.arange(by_owner.shape[0], dtype=jnp.int32)
    relative = (owner ^ me)[:, None]
    owner = owner[:, None]
    core, x, y = relative % 2, relative // 2 % 2, relative // 4
    place = jnp.zeros_like(rank)
    clean = jnp.bool_(True)
    start = 0
    for size, least in zip(EARLY, LEAST):
        at = rank - start
        here = (at >= 0) & (at < size)
        place = jnp.where(here, 8 * start + owner * size + at, place)
        clean = clean & jnp.all(jnp.where(here, by_owner >= least, True))
        start += size
    for size in LATE:
        half = size // 2
        at = rank - start
        here = (at >= 0) & (at < size)
        spot = jnp.where(at < half, (x * 2 + y) * half + at, 4 * half + (y * 2 + x) * half + at - half)
        place = jnp.where(here, 8 * start + core * 4 * size + spot, place)
        start += size
    return place.reshape(-1)[slot_of_block], rank, clean


CORE = [(i, i ^ 1) for i in range(8)]
ALONG_X = [(i, i ^ 2) for i in range(8)]
ALONG_Y = [(i, i ^ 4) for i in range(8)]


def wide(t, lo, hi):
    return t[lo:hi].astype(f32)


class Bands:
    def to_meet(self, plane):
        self.plane = plane
        return (plane,)

    def go_meet(self, plane):
        return lax.ppermute(plane, "band", [(0, 1)]), lax.ppermute(plane, "band", [(2, 1)])

    def to_part(self, up, down):
        self.total = (self.plane.astype(f32) + up.astype(f32) + down.astype(f32)).astype(bf16)
        return (self.total,)

    def go_part(self, total):
        return lax.ppermute(total, "band", [(1, 0)]), lax.ppermute(total, "band", [(1, 2)])

    def to_last(self, to_first, to_third):
        self.to_first, self.to_third = to_first, to_third
        return (to_third,)

    def go_last(self, to_third):
        return (lax.ppermute(to_third, "band", [(2, 3)]),)

    def to_end(self, to_last):
        band = lax.axis_index("band")
        total = jnp.where(band == 0, self.to_first, self.total)
        total = jnp.where(band == 2, self.to_third, total)
        self.total = jnp.where(band == 3, to_last, total)
        return (self.total,)

    def go_end(self, total):
        return ()


class Chunk(Bands):
    def __init__(self, kept, sent):
        self.half = kept.shape[0] // 8
        self.kept, self.sent = kept, sent

    def chip(self, lo, hi):
        lo, hi = lo * self.half, hi * self.half
        return wide(self.kept, lo, hi) + wide(self.received, lo, hi)

    def to_core(self):
        return (self.sent,)

    def go_core(self, send):
        return (lax.ppermute(send, "dp", CORE),)

    def to_plane(self, received):
        self.received = received
        return self.chip(2, 4).astype(bf16), self.chip(6, 8).astype(bf16)

    def go_plane(self, send_x, send_y):
        return lax.ppermute(send_x, "dp", ALONG_X), lax.ppermute(send_y, "dp", ALONG_Y)

    go_turn = go_plane

    def to_turn(self, from_x, from_y):
        self.from_x, self.from_y = from_x, from_y
        half = self.half
        send_y = (self.chip(1, 2) + wide(from_x, half, 2 * half)).astype(bf16)
        send_x = (self.chip(5, 6) + wide(from_y, half, 2 * half)).astype(bf16)
        return send_x, send_y

    def to_meet(self, from_x, from_y):
        half = self.half
        one = self.chip(0, 1) + wide(self.from_x, 0, half) + wide(from_y, 0, half)
        two = self.chip(4, 5) + wide(self.from_y, 0, half) + wide(from_x, 0, half)
        self.plane = jnp.concatenate([one, two], 0).astype(bf16)
        return (self.plane,)


class Sequence:
    def __init__(self):
        self.before = ()
        self.arrived = {}

    def round(self, *steps):
        arrived = [tuple(self.arrived.get(chunk, ())) for chunk, _ in steps]
        flat = sum(arrived, ())
        flat = lax.optimization_barrier(flat + self.before)
        at, self.before = 0, ()
        for (chunk, name), had in zip(steps, arrived):
            sends = getattr(chunk, "to_" + name)(*flat[at : at + len(had)])
            at += len(had)
            self.arrived[chunk] = getattr(chunk, "go_" + name)(*sends)
            self.before = self.before + tuple(sends)

    def wait_for(self, *arrays):
        arrays = lax.optimization_barrier(arrays + self.before)[: len(arrays)]
        self.before = self.before + arrays
        return arrays


def rope_tables(rows):
    half = HEAD_DIM // 2
    frequency = rope_base ** (-(jnp.arange(half, dtype=f32) * 2.0 / HEAD_DIM))
    angles = jnp.arange(rows, dtype=jnp.int32).astype(f32)[:, None] * frequency[None, :]
    cosine, sine = jnp.cos(angles), jnp.sin(angles)
    return jnp.tile(cosine, (1, 4)), jnp.tile(jnp.concatenate([-sine, sine], 1), (1, 2))


def shards(
    tokens,
    cotangent,
    lengths,
    slot_of_block,
    master,
    statistics,
    inverse_roots,
    gain_values,
    gain_moments,
):
    images, band_rows, _ = tokens.shape
    band = lax.axis_index("band")
    bands = lax.axis_size("band")
    seq = band_rows * bands
    rows = round_up(seq, 16)
    gathered = lax.all_gather(master.astype(bf16), "dp", axis=0, tiled=True)
    slot_count = gathered.shape[0]

    arrived = to_images(jnp.stack([tokens, cotangent], 1), bands, band)
    token_rows = jnp.pad(arrived[:, 0].reshape(seq, D), ((0, rows - seq), (0, 0)))
    back_rows = jnp.pad(arrived[:, 1].reshape(seq, D), ((0, rows - seq), (0, 0)))
    length = lengths[jnp.minimum(band, images - 1)]
    valid = (jnp.arange(rows, dtype=jnp.int32) < length).astype(f32)
    length = length.reshape(1)
    cos, sin = rope_tables(rows)

    spare_count = slot_count - slot_of_block.shape[0]
    spare = jnp.zeros((1,), jnp.int32)
    if spare_count > 0:
        used = jnp.zeros((slot_count,), jnp.int32).at[slot_of_block].set(1)
        spare = jnp.concatenate([jnp.argsort(used)[:spare_count].astype(jnp.int32), spare])

    hidden = token_rows.astype(f32)
    inputs, saves = [], []
    for layer in range(LAYERS):
        slots = slot_of_block[layer * PER_LAYER : (layer + 1) * PER_LAYER]
        gains = gain_values[2 * layer : 2 * layer + 2]
        inputs.append(hidden)
        hidden, *saved = forward_layer(slots, length, hidden, gains, cos, sin, gathered)
        saves.append(saved)

    def send_rows(t):
        return send_to_bands(t[:seq].astype(bf16).reshape(bands, band_rows, D), images, bands, band)

    output_blocks = send_rows(hidden)

    back = back_rows.astype(f32) * valid[:, None]
    per_owner = master.shape[0]
    me = lax.axis_index("dp")
    by_permutes = (
        lax.axis_size("dp") == 8
        and bands == 4
        and images == 3
        and slot_count == slot_of_block.shape[0]
        and per_owner == sum(EARLY) + sum(LATE)
    )
    if by_permutes:
        places, ranks, clean = chunk_places(slot_of_block, per_owner, me)
        rank = lax.dynamic_index_in_dim(ranks, me, 0, keepdims=False)
        ends = [8 * sum(EARLY[: i + 1]) for i in range(len(EARLY))]
        bounds = [0] + ends
        for size in LATE:
            bounds += [bounds[-1] + 4 * size, bounds[-1] + 8 * size]
        zones = tuple((low, high, high - low) for low, high in zip(bounds, bounds[1:]))
    else:
        places, rank = slot_of_block, jnp.arange(per_owner, dtype=jnp.int32)
        zones = ((0, slot_count, slot_count),)

    def backward(layer, back, tiles, zones):
        fill = spare if layer == LAYERS - 1 else spare[-1:]
        back, gains, *tiles = backward_layer(
            places[layer * PER_LAYER : (layer + 1) * PER_LAYER], fill, length, back,
            gain_values[2 * layer : 2 * layer + 2], cos, sin, (inputs[layer], *saves[layer]), zones, tiles,
        )
        return back, gains, tiles

    if by_permutes:
        back, gains_top, tiles = backward(1, back, [], zones)
        early = tiles[:1]
        ready, *output_blocks = lax.optimization_barrier((tiles[0], *output_blocks))
        early_sums = [lax.psum_scatter(ready, "dp", scatter_dimension=0, tiled=True)]
        back, gains_bottom, tiles = backward(0, back, tiles[1:], zones)
        missed, *late = tiles
        gains = jnp.concatenate([gains_bottom, gains_top], 0).astype(bf16).reshape(-1, BLOCK)
        gains = jnp.pad(gains, ((0, BLOCK - gains.shape[0]), (0, 0)))[None]
        sequence = Sequence()
        chunks = [Chunk(*late[2 * i : 2 * i + 2]) for i in range(len(LATE))]
        one, two, three = chunks
        top = Bands()
        sequence.arrived[top] = (jnp.concatenate([early_sums[0], gains], 0),)
        sequence.round((one, "core"), (two, "core"), (three, "core"))
        sequence.round((one, "plane"))
        sequence.round((top, "meet"))
        sequence.round((one, "turn"))
        sequence.round((two, "plane"))
        sequence.round((one, "meet"))
        sequence.round((top, "part"))
        sequence.round((two, "turn"))
        sequence.round((three, "plane"))
        sequence.round((one, "part"))
        sequence.round((top, "last"))
        sequence.round((two, "meet"))
        sequence.round((three, "turn"))
        sequence.round((three, "meet"))
        sequence.round((two, "part"), (top, "end"))
        sequence.round((one, "last"))
        sequence.round((three, "part"))
        sequence.round((two, "last"))
        sequence.round((three, "last"))
        sequence.round((one, "end"))
        sequence.round((two, "end"))
        sequence.round((three, "end"))
        early_total = top.total[:-1]

        def again(trip, total):
            _, spare_tiles, *parts = lax.optimization_barrier((trip, missed, *early))
            block_at = jnp.argsort(places)
            sums, start = [], 0
            for part, end, least in zip(parts, ends, LEAST):
                late_here = (block_at[start:end] < least)[:, None, None]
                whole = jnp.where(late_here, spare_tiles[start:end], part)
                sums.append(lax.psum_scatter(whole, "dp", scatter_dimension=0, tiled=True))
                start = end
            return lax.psum(jnp.concatenate(sums, 0), "band")

        early_total = lax.fori_loop(0, jnp.where(clean, 0, 1), again, early_total)
        owned = jnp.concatenate([early_total] + [chunk.total for chunk in chunks], 0)
        gain_total = top.total[-1].astype(f32)[: gain_values.size // BLOCK].reshape(-1, D)
    else:
        back, gains_top, tiles = backward(1, back, [], zones)
        back, gains_bottom, tiles = backward(0, back, tiles, zones)
        owned = lax.psum_scatter(tiles[0], "dp", scatter_dimension=0, tiled=True)
        owned = lax.psum(owned, "band")
        gain_total = lax.psum(jnp.concatenate([gains_bottom, gains_top], 0), ("dp", "band"))

    layer_output = at_bands(output_blocks, images, bands, band)
    owned_f = owned.astype(f32)
    owned_squares = jnp.sum(owned_f * owned_f)
    if by_permutes:
        last = jnp.concatenate([gain_total.reshape(-1, BLOCK), jnp.broadcast_to(owned_squares, (1, BLOCK))], 0)
        for pairs in (CORE, ALONG_X, ALONG_Y):
            last = last + lax.ppermute(last, "dp", pairs)
        gain_total, owned_squares = last[:-1].reshape(gain_values.shape), last[-1, 0]
    else:
        owned_squares = lax.psum(owned_squares, "dp")
    grad_norm = jnp.sqrt(owned_squares + jnp.sum(gain_total * gain_total))
    factor = jnp.minimum(1.0, clip_limit / grad_norm)
    back, factor = lax.optimization_barrier((back, factor))
    input_grad = at_bands(send_rows(back), images, bands, band)
    weight_grads, new_statistics, new_master, master_copy = optimizer(
        factor.reshape(1), rank, owned, master, statistics, inverse_roots
    )
    gain_grads = gain_total * factor
    new_moments = decay_rate * gain_moments + (1.0 - decay_rate) * gain_grads * gain_grads
    new_gains = gain_values - gain_rate * gain_grads / (jnp.sqrt(new_moments) + epsilon)
    return (
        layer_output,
        input_grad,
        weight_grads,
        grad_norm,
        new_statistics,
        new_master,
        master_copy,
        gain_grads,
        new_moments,
        new_gains,
    )


def solution(mesh):
    return jax.shard_map(
        shards,
        mesh=mesh,
        in_specs=(
            P("dp", "band", None),
            P("dp", "band", None),
            P("dp"),
            P(),
            P("dp", None, None),
            P("dp", None, None, None),
            P("dp", None, None, None),
            P(),
            P(),
        ),
        out_specs=(
            P("dp", "band", None),
            P("dp", "band", None),
            P("dp", None, None),
            P(),
            P("dp", None, None, None),
            P("dp", None, None),
            P("dp", None, None),
            P(),
            P(),
            P(),
        ),
        check_vma=False,
    )
```
